32 devices in a mesh: dp: 8 (over y, x, core), chan: 4 (over z).
Axes of the slice: x: 2, y: 2, z: 4, core: 2. Of those that a mesh axis runs over, the one named last changes fastest.
Arguments:
- latents_in: bfloat16 [16, 16, 16, 512], P('dp', None, None, 'chan'), may hold values from -6 to 6
- norm_gains: float32 [3, 512], P(None, 'chan'), may hold values from 0.1 to 1.9
- norm_shifts: float32 [3, 512], P(None, 'chan'), may hold values from -3 to 3
- conv_weights: bfloat16 [2, 3, 3, 512, 512], P(None, None, None, None, 'chan'), may hold values from -0.09375 to 0.09375
- conv_biases: float32 [2, 512], P(None, 'chan'), may hold values from -3 to 3
- qkv_weights: bfloat16 [3, 512, 512], P(None, None, 'chan'), may hold values from -0.375 to 0.375
- attn_biases: float32 [3, 512], P(None, 'chan'), may hold values from -3 to 3
- out_weight: bfloat16 [512, 512], P(None, 'chan'), may hold values from -0.75 to 0.75
- proj_weight: bfloat16 [512, 256], P(None, 'chan'), may hold values from -0.25 to 0.25
- proj_bias: float32 [256], P('chan'), may hold values from -3 to 3
- codebook: float32 [1024, 256], P(None, 'chan'), may hold values from -6 to 6
- codes: int32 [16, 16, 16], P('dp'), may hold values from 0 to 1023, as said below
- reset_src: int32 [1024], replicated, may hold values from 0 to 4095
- cotangent: bfloat16 [16, 16, 16, 256], P('dp', None, None, 'chan'), may hold values from -6 to 6
Outputs:
- latents_out: float32 [16, 16, 16, 256], P('dp', None, None, 'chan')
- commitment: float32 [256], P('chan')
- perplexity: float32 [], replicated
- new_codebook: float32 [1024, 256], P(None, 'chan')
- grad_latents: float32 [16, 16, 16, 512], P('dp', None, None, 'chan')
- grad_norm_gains: float32 [3, 512], P(None, 'chan')
- grad_norm_shifts: float32 [3, 512], P(None, 'chan')
- grad_conv_weights: float32 [2, 3, 3, 512, 512], P(None, None, None, None, 'chan')
- grad_conv_biases: float32 [2, 512], P(None, 'chan')
- grad_qkv_weights: float32 [3, 512, 512], P(None, None, 'chan')
- grad_attn_biases: float32 [3, 512], P(None, 'chan')
- grad_out_weight: float32 [512, 512], P(None, 'chan')
- grad_proj_weight: float32 [512, 256], P(None, 'chan')
- grad_proj_bias: float32 [256], P('chan')
- grad_codebook: float32 [1024, 256], P(None, 'chan')
The draws below stay inside these ranges and needn't reach their ends.
Inputs may be any that keep to these rules, and one draw needn't show every extreme that they name: All code indices lie in one set of 768 codes chosen by the seed. `reset_src`: a position number (image × 16 + row) × 16 + column.
All inputs are finite; a program needn't handle non-finite values.
Results may differ from the reference program's by a relative error of at most 0.02.
Values may be sent and summed in bfloat16 or wider, within the bound.
No kernel may reach another device: no remote copies, remote signals or barrier semaphores. Data moves between devices by JAX's collectives and lax.ppermute only.
A program may use at most 128 MiB of HBM per device.

```python
import jax
import jax.numpy as jnp
from jax import lax

C = 512
E = 256
CODES = 1024
GROUPS = 32
LAT = 16
IMAGES = 16
TOKENS = 4096
USED = 768


def draw_codes(key, part):
    key = jax.random.fold_in(key, 3)
    order_key, slot_key = jax.random.split(key)
    chosen = jax.random.permutation(order_key, CODES)
    drawn_slots = jax.random.randint(slot_key, (IMAGES, LAT, LAT), 0, USED)
    return chosen[drawn_slots].astype(jnp.int32)


def touch_ends(result, own_key, smallest, top_value):
    spot = [jax.random.randint(jax.random.fold_in(own_key, axis), (), 0, length) for axis, length in enumerate(result.shape)]
    longest = result.shape.index(max(result.shape))
    next_to = spot[:longest] + [(spot[longest] + 1) % result.shape[longest]] + spot[longest + 1:]
    return result.at[tuple(spot)].set(smallest).at[tuple(next_to)].set(top_value)


def block_scale(rng, shape, pieces, low, high):
    factor_of = 1.0
    for axis_at, shards_of in pieces:
        heights = jax.random.uniform(jax.random.fold_in(jax.random.fold_in(rng, 6), axis_at), (shards_of,), jnp.float32, low / len(pieces), high / len(pieces))
        factor_of = factor_of * jnp.repeat(jnp.exp(heights), shape[axis_at] // shards_of).reshape((-1,) + (1,) * (len(shape) - 1 - axis_at))
    return factor_of


def noise(stream_key, shape, scale, bound, shards=(), dtype=jnp.bfloat16):
    gain = block_scale(stream_key, shape, shards, -0.22, 0.18) if shards else 1.0
    array = jax.random.normal(stream_key, shape, jnp.float32) * scale * gain
    return jnp.minimum(jnp.maximum(array, -bound), bound).astype(dtype)


def setup_inputs(seed: int = 0) -> dict:
    splits = jax.random.split(jax.random.key(seed), 15)
    latents_in = noise(splits[0], (IMAGES, LAT, LAT, C), 1.0, 6.0, ((0, 8), (3, 4)))
    norm_gains = jnp.clip(1.0 + 0.18 * jax.random.normal(splits[1], (3, C), jnp.float32), 0.1, 1.9)
    norm_shifts = noise(splits[2], (3, C), 0.5, 3.0, ((1, 4),), jnp.float32)
    conv_weights = noise(splits[3], (2, 3, 3, C, C), (9 * C) ** -0.5, 0.09375, ((4, 4),))
    conv_biases = noise(splits[4], (2, C), 0.5, 3.0, ((1, 4),), jnp.float32)
    qkv_weights = noise(splits[5], (3, C, C), (C // 2) ** -0.5, 0.375, ((2, 4),))
    attn_biases = noise(splits[6], (3, C), 0.5, 3.0, ((1, 4),), jnp.float32)
    out_weight = noise(splits[7], (C, C), (C // 8) ** -0.5, 0.75, ((1, 4),))
    proj_weight = noise(splits[8], (C, E), C ** -0.5, 0.25, ((1, 4),))
    proj_bias = noise(splits[9], (E,), 0.5, 3.0, ((0, 4),), jnp.float32)
    codebook = noise(splits[10], (CODES, E), 1.0, 6.0, ((1, 4),), jnp.float32)
    codes = draw_codes(jax.random.fold_in(splits[14], 71), 0)
    reset_src = touch_ends(jax.random.randint(splits[12], (CODES,), 0, TOKENS), jax.random.fold_in(splits[12], 1), 0, TOKENS - 1).astype(jnp.int32)
    cotangent = noise(splits[13], (IMAGES, LAT, LAT, E), 1.0, 6.0, ((0, 8), (3, 4)))
    return dict(latents_in=latents_in, norm_gains=norm_gains, norm_shifts=norm_shifts, conv_weights=conv_weights, conv_biases=conv_biases, qkv_weights=qkv_weights, attn_biases=attn_biases, out_weight=out_weight, proj_weight=proj_weight, proj_bias=proj_bias, codebook=codebook, codes=codes, reset_src=reset_src, cotangent=cotangent)


EPSILON = 1e-06
BETA = 0.25
FULL_PRECISION = lax.Precision.HIGHEST

@jax.custom_vjp
def reduced_cast(v):
    return lax.optimization_barrier(v.astype(jnp.bfloat16)).astype(jnp.float32)

@jax.custom_vjp
def reduced_cast_back(v):
    return v

def low_keep(v):
    return (reduced_cast(v), None)

def low_pass(kept, grad):
    return (grad,)

def back_keep(v):
    return (v, None)

def back_low(kept, grad):
    return (reduced_cast(grad),)
reduced_cast.defvjp(low_keep, low_pass)
reduced_cast_back.defvjp(back_keep, back_low)

def swish(values):
    return values * jax.nn.sigmoid(values)

def group_norm(values, gain_vec, shift_vec):
    dims_in = values.shape
    grouped = values.reshape(dims_in[0], dims_in[1] * dims_in[2], GROUPS, dims_in[3] // GROUPS)
    mean_value = lax.optimization_barrier(jnp.mean(grouped, axis=(1, 3), keepdims=True))
    centred = grouped - mean_value
    variance = lax.optimization_barrier(jnp.mean(centred * centred, axis=(1, 3), keepdims=True))
    return (centred * lax.rsqrt(variance + EPSILON)).reshape(dims_in) * gain_vec + shift_vec

def convolve(images, kernel):
    return lax.conv_general_dilated(images, kernel, (1, 1), 'SAME', dimension_numbers=('NHWC', 'HWIO', 'NHWC'), precision=FULL_PRECISION)

def network(images, params):
    gains, shifts, conv_weight, conv_bias, qkv_weight, attn_bias, out_weight, proj_weight, proj_bias = params
    image_count = images.shape[0]
    scores_scale_factor = float(C) ** (-0.5)
    first = reduced_cast(swish(group_norm(images, gains[0], shifts[0])))
    hidden = reduced_cast_back(convolve(first, conv_weight[0]) + conv_bias[0])
    second = reduced_cast(swish(group_norm(hidden, gains[1], shifts[1])))
    branch = reduced_cast_back(convolve(second, conv_weight[1]) + conv_bias[1])
    residual = images + branch
    normed = reduced_cast(group_norm(residual, gains[2], shifts[2])).reshape(image_count, LAT * LAT, C)
    query_input = reduced_cast(reduced_cast_back(jnp.einsum('bpc,cd->bpd', normed, qkv_weight[0], precision=FULL_PRECISION) + attn_bias[0]))
    gathered_keys = reduced_cast(reduced_cast_back(jnp.einsum('bpc,cd->bpd', normed, qkv_weight[1], precision=FULL_PRECISION)))
    gathered_values = reduced_cast(reduced_cast_back(jnp.einsum('bpc,cd->bpd', normed, qkv_weight[2], precision=FULL_PRECISION) + attn_bias[1]))
    attention_scores = reduced_cast_back(jnp.einsum('ulp,ugp->ulg', query_input, gathered_keys, precision=FULL_PRECISION) * scores_scale_factor)
    attention_weights = reduced_cast(jax.nn.softmax(attention_scores, axis=-1))
    mixed_output = reduced_cast(reduced_cast_back(jnp.einsum('pth,phz->ptz', attention_weights, gathered_values, precision=FULL_PRECISION)))
    attended = reduced_cast_back(jnp.einsum('bpc,cd->bpd', mixed_output, out_weight, precision=FULL_PRECISION) + attn_bias[2])
    output = reduced_cast(residual.reshape(image_count, LAT * LAT, C) + attended)
    latents = reduced_cast_back(jnp.einsum('bpc,ce->bpe', output, proj_weight, precision=FULL_PRECISION) + proj_bias)
    return latents.reshape(image_count, LAT, LAT, E)

def reference(latents_in, norm_gains, norm_shifts, conv_weights, conv_biases, qkv_weights, attn_biases, out_weight, proj_weight, proj_bias, codebook, codes, reset_src, cotangent):
    params = tuple((member.astype(jnp.float32) for member in (norm_gains, norm_shifts, conv_weights, conv_biases, qkv_weights, attn_biases, out_weight, proj_weight, proj_bias)))
    image_count = latents_in.shape[0]
    per_step = 16
    inputs = latents_in.astype(jnp.float32).reshape(image_count // per_step, per_step, LAT, LAT, C)

    def forward(inputs_in, params_in):

        def advance(state_in, images_in):
            return (state_in, jax.checkpoint(network)(images_in, params_in))
        final_state, stacked = lax.scan(advance, jnp.zeros((), jnp.float32), inputs_in)
        return stacked
    latents, pullback = jax.vjp(forward, inputs, params)
    flat_latents = latents.reshape(TOKENS, E)
    code_index = codes.reshape(TOKENS)
    quantized = codebook[code_index]
    difference = flat_latents - quantized
    commitment = lax.optimization_barrier(jnp.mean(difference * difference, axis=0))
    unit_value = jnp.ones((), jnp.float32)

    def commit_term(latent_rows):
        offset = latent_rows - quantized
        return BETA * jnp.sum(offset * offset)

    def book_term(book_rows):
        offset = book_rows[code_index] - flat_latents
        return CODES / TOKENS * jnp.sum(offset * offset)
    commit_value, commit_pull = jax.vjp(commit_term, flat_latents)
    latent_grad = cotangent.astype(jnp.float32).reshape(TOKENS, E) + commit_pull(unit_value)[0]
    book_value, book_pull = jax.vjp(book_term, codebook)
    grad_codebook = book_pull(unit_value)[0]
    grad_inputs, grad_params = pullback(latent_grad.reshape(latents.shape))
    usage = jnp.zeros((CODES,), jnp.float32).at[code_index].add(1.0)
    share = usage / TOKENS
    perplexity = jnp.exp(-jnp.sum(share * jnp.log(jnp.maximum(share, 1.0 / TOKENS))))
    new_codebook = jnp.where(usage[:, None] > 0.5, codebook, flat_latents[reset_src])
    return (latents.reshape(IMAGES, LAT, LAT, E), commitment, perplexity, new_codebook, grad_inputs.reshape(IMAGES, LAT, LAT, C), grad_params[0], grad_params[1], grad_params[2], grad_params[3], grad_params[4], grad_params[5], grad_params[6], grad_params[7], grad_params[8], grad_codebook)
```

```python
import jax
import jax.numpy as jnp
from jax import lax
from jax.experimental import pallas as pl
from jax.experimental.pallas import tpu as pltpu
from jax.sharding import PartitionSpec as P

F32 = jnp.float32
BF = jnp.bfloat16
C = 512
CODES = 1024
LAT = 16
POS = LAT * LAT
EPSILON = 1e-06
BETA = 0.25
SCORE_SCALE = float(C) ** (-0.5)
GROUP_COUNT = float(POS * 16)
WIDE = 1152
VMEM = 20
HEAVY = 10**11
PARTS = 8


def call(body, outs, *args, scratch=(), flops=0, name=None, space=pltpu.VMEM):
    result = pl.pallas_call(
        body,
        out_shape=list(outs),
        in_specs=[pl.BlockSpec(memory_space=pltpu.SMEM)]
        + [pl.BlockSpec(memory_space=space)] * (len(args) - 1),
        out_specs=[pl.BlockSpec(memory_space=pltpu.VMEM)] * len(outs),
        scratch_shapes=list(scratch),
        compiler_params=pltpu.CompilerParams(vmem_limit_bytes=VMEM * 2**20),
        cost_estimate=pl.CostEstimate(flops=flops, bytes_accessed=1, transcendentals=0),
        name=name,
    )(*args)
    return result


def sds(shape, dtype):
    return jax.ShapeDtypeStruct(shape, dtype)


def dot(a, b):
    return jnp.dot(a, b, preferred_element_type=F32)


def dot_nt(a, b):
    return lax.dot_general(a, b, (((1,), (1,)), ((), ())), preferred_element_type=F32)


def dot_tn(a, b):
    return lax.dot_general(a, b, (((0,), (0,)), ((), ())), preferred_element_type=F32)


def lanes(parts):
    return jnp.concatenate(parts, axis=1)


def rows_of(parts):
    return jnp.concatenate(parts, axis=0)


def pack_rows(vectors, height=8):
    width = vectors[0].shape[1]
    spot = lax.broadcasted_iota(jnp.int32, (height, width), 0)
    result = jnp.zeros((height, width), F32)
    for index, vector in enumerate(vectors):
        result = jnp.where(spot == index, vector, result)
    return result


def split_low(values):
    high = values.astype(BF).astype(F32)
    return high, values - high


def group_sums(rows):
    first = lax.broadcasted_iota(jnp.int32, (128, 128), 0) >> 4
    second = lax.broadcasted_iota(jnp.int32, (128, 128), 1) >> 4
    ones = (first == second).astype(F32).astype(BF)
    high, rest = split_low(rows)
    middle, low = split_low(rest)
    stacked = rows_of([high, middle, low, jnp.zeros_like(high)]).astype(BF)
    summed = dot(stacked, ones)
    return summed[0:8] + summed[8:16] + summed[16:24]


def col_sum(values):
    return jnp.sum(values, axis=0, keepdims=True)


def moments(values):
    one, two = values[:POS], values[POS:]
    mean = group_sums(pack_rows([col_sum(one), col_sum(two)])) * (1.0 / GROUP_COUNT)
    one, two = one - mean[0:1], two - mean[1:2]
    variance = group_sums(pack_rows([col_sum(one * one), col_sum(two * two)])) * (
        1.0 / GROUP_COUNT
    )
    inverse = lax.rsqrt(variance + EPSILON)
    deviation = jnp.sqrt(variance + EPSILON)
    normed = rows_of([one * inverse[0:1], two * inverse[1:2]])
    stats = pack_rows(
        [mean[0:1], mean[1:2], inverse[0:1], inverse[1:2], deviation[0:1], deviation[1:2]]
    )
    return normed, stats


def renormed(values, stats):
    return rows_of(
        [
            (values[:POS] - stats[0:1]) * stats[2:3],
            (values[POS:] - stats[1:2]) * stats[3:4],
        ]
    )


def norm_back(upstream, normed, stats, gain):
    sides = [(upstream[:POS], normed[:POS]), (upstream[POS:], normed[POS:])]
    plain = [col_sum(u) for u, _ in sides]
    weighted = [col_sum(u * n) for u, n in sides]
    means = group_sums(
        pack_rows([plain[0] * gain, plain[1] * gain, weighted[0] * gain, weighted[1] * gain])
    ) * (1.0 / GROUP_COUNT)
    parts = [
        stats[2 + m : 3 + m] * (u * gain - means[m : m + 1] - n * means[2 + m : 3 + m])
        for m, (u, n) in enumerate(sides)
    ]
    return rows_of(parts), weighted[0] + weighted[1], plain[0] + plain[1]


GAIN, SHIFT, CONV_BIAS, ATTN_BIAS, PROJ_BIAS = 0, 3, 6, 8, 11


def param(ref, index):
    return ref[index : index + 1]


def column_masks(height):
    column = lax.broadcasted_iota(jnp.int32, (height, 128), 0) & (LAT - 1)
    return column >= 1, column <= LAT - 2


def later_rows(values):
    blank = jnp.zeros((LAT, values.shape[1]), values.dtype)
    return rows_of([values[LAT:POS], blank, values[POS + LAT :], blank])


def earlier_rows(values):
    blank = jnp.zeros((LAT, values.shape[1]), values.dtype)
    return rows_of([blank, values[: POS - LAT], blank, values[POS : 2 * POS - LAT]])


def conv_forward(pieces, w_ref):
    full = lanes(pieces)
    height = full.shape[0]
    inner, outer = column_masks(height)
    sums = []
    for col_tap in range(3):
        total = None
        for row_tap in range(3):
            tap = 3 * row_tap + col_tap
            part = dot(full, w_ref[0, :, 128 * tap : 128 * tap + 128])
            if row_tap == 0:
                part = earlier_rows(part)
            elif row_tap == 2:
                part = later_rows(part)
            total = part if total is None else total + part
        sums.append(total)
    left = jnp.where(inner, pltpu.roll(sums[0], 1, 0), 0.0)
    right = jnp.where(outer, pltpu.roll(sums[2], height - 1, 0), 0.0)
    return sums[1] + left + right


def spread_taps(gradient):
    height = gradient.shape[0]
    inner, outer = column_masks(height)
    by_column = [
        jnp.where(outer, pltpu.roll(gradient, height - 1, 0), 0.0),
        gradient,
        jnp.where(inner, pltpu.roll(gradient, 1, 0), 0.0),
    ]
    copies = [None] * 9
    for col_tap in range(3):
        copies[col_tap] = later_rows(by_column[col_tap])
        copies[3 + col_tap] = by_column[col_tap]
        copies[6 + col_tap] = earlier_rows(by_column[col_tap])
    return lanes([c.astype(BF) for c in copies])


def part_row(scalars, part):
    place = scalars[1] ^ part
    block = (place >> 1) ^ scalars[0]
    return place, pl.multiple_of(block * 128 + (place & 1) * 64, 64)


def first_norm_kernel(scalars, x_ref, gain_ref, shift_ref, act_ref, stats_ref):
    normed, stats = moments(x_ref[...].astype(F32))
    pre = normed * gain_ref[0:1] + shift_ref[0:1]
    act_ref[...] = (pre * jax.nn.sigmoid(pre)).astype(BF)
    stats_ref[...] = stats


def code_column(codes):
    grid = rows_of([codes[m] for m in range(codes.shape[0])])
    height = grid.shape[0] * LAT
    high = grid >> 5
    both = lanes([high.astype(F32), (grid - (high << 5)).astype(F32)]).astype(BF)
    lines = lax.broadcasted_iota(jnp.int32, (height, grid.shape[0]), 0) >> 4
    own = (lines == lax.broadcasted_iota(jnp.int32, lines.shape, 1)).astype(F32).astype(BF)
    spread = dot(own, both)
    column = lax.broadcasted_iota(jnp.int32, (height, LAT), 0) & (LAT - 1)
    here = column == lax.broadcasted_iota(jnp.int32, (height, LAT), 1)
    merged = 32.0 * spread[:, :LAT] + spread[:, LAT:]
    return jnp.sum(jnp.where(here, merged, 0.0), axis=1, keepdims=True).astype(jnp.int32)


def start_kernel(scalars, codes_ref, book_ref, cot_ref, _, hot_ref, quant_ref, usage_ref, fixed_ref, start):
    tokens = hot_ref.shape[0]
    hot32 = (
        code_column(codes_ref[...]) == lax.broadcasted_iota(jnp.int32, (tokens, CODES), 1)
    ).astype(F32)
    hot = hot32.astype(BF)
    hot_ref[...] = hot
    counts = col_sum(hot32)
    usage_ref[...] = pack_rows([counts[:, 128 * i : 128 * i + 128] for i in range(8)])
    high, rest = split_low(book_ref[...])
    middle, low = split_low(rest)
    picked = dot_nt(hot, rows_of([high, middle, low]).astype(BF))
    width = book_ref.shape[0]
    quantized = picked[:, :width] + picked[:, width : 2 * width] + picked[:, 2 * width :]
    quant_ref[...] = quantized
    start[...] = cot_ref[...].astype(F32) - 2.0 * BETA * quantized
    for k in range(4):
        row = (scalars[0] ^ k) * 128
        one = start[pl.ds(pl.multiple_of(row, 64), 64), :]
        two = start[pl.ds(pl.multiple_of(row + 64, 64), 64), :]
        high, low = split_low(lanes([one, two]))
        fixed_ref[k, 0:64] = high.astype(BF)
        fixed_ref[k, 64:128] = low.astype(BF)


def conv_weight_kernel(scalars, w_ref, o_ref):
    for k in range(4):
        own = pl.ds(pl.multiple_of((scalars[0] ^ k) * 128, 128), 128)
        for tap in range(9):
            o_ref[0, 128 * k : 128 * k + 128, 128 * tap : 128 * tap + 128] = w_ref[0, tap, own, :]


def attn_weight_kernel(scalars, own_ref, other_ref, o_ref):
    for part in range(PARTS):
        source = (own_ref if part % 2 == 0 else other_ref).at[part // 2]
        _, row = part_row(scalars, part)
        spot = pl.ds(row, 64)
        for k in range(4):
            for m in range(4):
                o_ref[spot, 512 * m + 128 * k : 512 * m + 128 * k + 128] = source[
                    k, :, 128 * m : 128 * m + 128
                ]
        for pair in range(2):
            o_ref[spot, 2048 + 128 * pair : 2176 + 128 * pair] = lanes(
                [source[2 * pair + i, :, 512:576] for i in range(2)]
            )


def conv_one_kernel(
    scalars, a0, a1, a2, a3, w_ref, param_ref, _, hidden_ref, stats_ref, act_ref
):
    hidden = conv_forward([a0[...], a1[...], a2[...], a3[...]], w_ref) + param(
        param_ref, CONV_BIAS
    )
    hidden_ref[...] = hidden
    normed, stats = moments(hidden)
    stats_ref[...] = stats
    pre = normed * param(param_ref, GAIN + 1) + param(param_ref, SHIFT + 1)
    act_ref[...] = (pre * jax.nn.sigmoid(pre)).astype(BF)


def conv_two_kernel(
    scalars, a0, a1, a2, a3, w_ref, param_ref, x_ref, fixed_ref, normed_ref, stats_ref, *pay_refs
):
    residual = x_ref[...].astype(F32) + (
        conv_forward([a0[...], a1[...], a2[...], a3[...]], w_ref) + param(param_ref, CONV_BIAS + 1)
    )
    normed, stats = moments(residual)
    normed_ref[...] = normed
    stats_ref[...] = stats
    gain, shift = param(param_ref, GAIN + 2), param(param_ref, SHIFT + 2)
    for k, ref in enumerate(pay_refs):
        target = scalars[0] ^ k
        own, other = target * 128, (target ^ 1) * 128
        ref[0:128] = (
            normed_ref[pl.ds(pl.multiple_of(other, 128), 128), :] * gain + shift
        ).astype(BF)
        high, low = split_low(normed_ref[pl.ds(pl.multiple_of(own, 128), 128), :])
        ref[128:256] = high.astype(BF)
        ref[256:384] = low.astype(BF)
        is_two = jnp.broadcast_to(target >> 1, (1, 128)) == 1
        mean = jnp.where(is_two, stats[1:2], stats[0:1])
        deviation = jnp.where(is_two, stats[5:6], stats[4:5])
        rows = list(split_low(mean)) + list(split_low(deviation))
        for index in (GAIN + 2, SHIFT + 2, ATTN_BIAS, ATTN_BIAS + 1, ATTN_BIAS + 2, PROJ_BIAS):
            rows.extend(split_low(param(param_ref, index)))
        ref[384:400] = pack_rows(rows, 16).astype(BF)
        ref[400:528] = fixed_ref[k]


def attn_in_kernel(scalars, n0, n1, n2, n3, norm_ref, residual_ref, bias_ref):
    pieces = [n0, n1, n2, n3]
    tails = [n[384:400].astype(F32) for n in pieces]

    def vector(index, width=128):
        row = 2 * index
        return lanes([t[row : row + 1, :width] + t[row + 1 : row + 2, :width] for t in tails])

    mean, deviation, gain, shift = [vector(index) for index in range(4)]
    empty = jnp.zeros((1, 256), F32)
    bias_ref[...] = pack_rows([vector(4), vector(5), vector(6), lanes([vector(7, 64), empty])])
    own = lanes([n[128:256].astype(F32) + n[256:384].astype(F32) for n in pieces])
    residual_ref[...] = own * deviation + mean
    norm_ref[0:128] = (own * gain + shift).astype(BF)
    norm_ref[128:POS] = lanes([n[0:128] for n in pieces])


def attention_kernel(
    scalars, norm_ref, residual_ref, bias_ref, n0, n1, n2, n3, w_ref, *refs
):
    pay_refs = refs[:4]
    out_ref, lat_grad_ref, mixed_ref, att_grad_ref, qg_ref, kg_ref, vg_ref, sums_ref = refs[4:]
    query_bias, value_bias, out_bias = [bias_ref[m : m + 1] for m in range(3)]
    proj_bias = bias_ref[3:4, 0:256]
    pieces = [n0, n1, n2, n3]
    normed = norm_ref[...]
    query = (dot(norm_ref[0:128], w_ref[:, 0:512]) + query_bias).astype(BF)
    keys = dot(normed, w_ref[:, 512:1024]).astype(BF)
    values = (dot(normed, w_ref[:, 1024:1536]) + value_bias).astype(BF)
    scores = dot_nt(query, keys) * SCORE_SCALE
    weights = jnp.exp(scores - jnp.max(scores, axis=1, keepdims=True))
    probs = weights / jnp.sum(weights, axis=1, keepdims=True)
    probs_low = probs.astype(BF)
    mixed = dot(probs_low, values).astype(BF)
    mixed_ref[...] = mixed
    attended = dot(mixed, w_ref[:, 1536:2048]) + out_bias
    output = (residual_ref[...] + attended).astype(BF)
    out_ref[...] = output
    latents = dot(output, w_ref[:, 2048:2304]) + proj_bias
    fixed = []
    for n in pieces:
        both = n[400:464].astype(F32) + n[464:528].astype(F32)
        fixed.append(rows_of([both[:, :64], both[:, 64:]]))
    lat_grad = (lanes(fixed) + 2.0 * BETA * latents).astype(BF)
    blank = jnp.zeros((128, 64), BF)
    for k in range(4):
        lat_grad_ref[:, 128 * k : 128 * k + 128] = lanes([lat_grad[:, 64 * k : 64 * k + 64], blank])
    out_grad = dot_nt(lat_grad, w_ref[:, 2048:2304])
    att_grad = out_grad.astype(BF)
    att_grad_ref[...] = att_grad
    mixed_grad = dot_nt(att_grad, w_ref[:, 1536:2048]).astype(BF)
    probs_grad = dot_nt(mixed_grad, values)
    row_dot = jnp.sum(probs * probs_grad, axis=1, keepdims=True)
    score_grad = (probs * (probs_grad - row_dot)).astype(BF)
    query_grad = (dot(score_grad, keys) * SCORE_SCALE).astype(BF)
    key_grad = (dot_tn(score_grad, query) * SCORE_SCALE).astype(BF)
    value_grad = dot_tn(probs_low, mixed_grad).astype(BF)
    qg_ref[...] = query_grad
    kg_ref[...] = key_grad
    vg_ref[...] = value_grad
    upstream = dot_nt(key_grad, w_ref[:, 512:1024]) + dot_nt(value_grad, w_ref[:, 1024:1536])
    upstream_own = upstream[:128] + dot_nt(query_grad, w_ref[:, 0:512])
    for k in range(4):
        ref = pay_refs[k]
        ref[0:128] = upstream_own[:, 128 * k : 128 * k + 128].astype(ref.dtype)
        ref[128:POS] = upstream[128:, 128 * k : 128 * k + 128].astype(ref.dtype)
        ref[POS : POS + 128] = out_grad[:, 128 * k : 128 * k + 128].astype(ref.dtype)
        piece = latents[:, 64 * k : 64 * k + 64]
        ref[POS + 128 : POS + 192] = lanes([piece[:64], piece[64:]]).astype(ref.dtype)
    sums_ref[...] = pack_rows(
        [
            col_sum(query_grad.astype(F32)),
            col_sum(value_grad.astype(F32)),
            col_sum(att_grad.astype(F32)),
            lanes(
                [
                    part
                    for k in range(4)
                    for part in (
                        col_sum(lat_grad[:, 64 * k : 64 * k + 64].astype(F32)),
                        jnp.zeros((1, 64), F32),
                    )
                ]
            ),
        ]
    )


def attn_grad_kernel(
    scalars,
    norm_ref,
    out_ref,
    lat_grad_ref,
    mixed_ref,
    att_grad_ref,
    qg_ref,
    kg_ref,
    vg_ref,
    sums_ref,
    usage_ref,
    *refs,
):
    keep_refs, send_ref, grads = refs[:4], refs[4], refs[5]
    grads[:, 0:512] = dot_tn(norm_ref[0:128], qg_ref[...]).astype(BF)
    grads[:, 512:1024] = dot_tn(norm_ref[...], kg_ref[...]).astype(BF)
    grads[:, 1024:1536] = dot_tn(norm_ref[...], vg_ref[...]).astype(BF)
    grads[:, 1536:2048] = dot_tn(mixed_ref[...], att_grad_ref[...]).astype(BF)
    grads[:, 2048:2560] = dot_tn(out_ref[...], lat_grad_ref[...]).astype(BF)
    right = lax.broadcasted_iota(jnp.int32, (16, 128), 1) >= 64

    def halves(vectors, offset):
        blank = jnp.zeros((1, 128), F32)
        entries = [blank] * offset
        for vector in vectors:
            entries += [pltpu.roll(vector, 64, 1), vector]
        return jnp.where(right, pack_rows(entries, 16), 0.0)

    biases = []
    for k in range(4):
        vectors = [sums_ref[m : m + 1, 128 * k : 128 * k + 128] for m in range(4)]
        biases.append(halves(vectors, 4))
    tens = jnp.floor(usage_ref[...] * (1.0 / 16.0))
    ones = usage_ref[...] - 16.0 * tens
    for part in range(PARTS):
        place, row = part_row(scalars, part)
        is_first = (jnp.broadcast_to(place, (16, 128)) == 0).astype(F32)
        here = jnp.broadcast_to(place, (8, 128)) == lax.broadcasted_iota(jnp.int32, (8, 128), 0)
        counts = [col_sum(jnp.where(here, digit, 0.0)) for digit in (tens, ones)]
        for k in range(4):
            ref = keep_refs[part // 2].at[k] if part % 2 == 0 else send_ref.at[part // 2, k]
            for m in range(4):
                ref[:, 128 * m : 128 * m + 128] = grads[
                    pl.ds(row, 64), 512 * m + 128 * k : 512 * m + 128 * k + 128
                ]
            extra = biases[k] * is_first
            if k == 0:
                extra = extra + halves(counts, 0)
            block = slice(2048 + 128 * k, 2176 + 128 * k)
            ref[0:16, 512:640] = (grads[pl.ds(row, 16), block].astype(F32) + extra).astype(BF)
            ref[16:64, 512:640] = grads[pl.ds(row + 16, 48), block]


def third_back_kernel(
    scalars,
    p0,
    p1,
    p2,
    p3,
    normed_ref,
    stats_ref,
    param_ref,
    _,
    w_ref,
    residual_ref,
    taps_ref,
    lat_ref,
    small_ref,
    q0,
    q1,
    q2,
    q3,
    up_ref,
    out_ref,
):
    z = scalars[0]
    for near, far, base in ((p0, p1, z), (p2, p3, z ^ 2)):
        first, second = near[0:POS].astype(F32), far[0:POS].astype(F32)
        up_ref[pl.ds(pl.multiple_of(base * 128, 128), 128), :] = first[:128] + second[128:]
        up_ref[pl.ds(pl.multiple_of((base ^ 1) * 128, 128), 128), :] = first[128:] + second[:128]
    for k, ref in enumerate((p0, p1, p2, p3)):
        row = (z ^ k) * 128
        out_ref[pl.ds(pl.multiple_of(row, 128), 128), :] = ref[POS : POS + 128].astype(F32)
        piece = ref[POS + 128 : POS + 192].astype(F32)
        lat_ref[pl.ds(pl.multiple_of(row, 64), 64), :] = piece[:, :64]
        lat_ref[pl.ds(pl.multiple_of(row + 64, 64), 64), :] = piece[:, 64:]
    source, gain_grad, shift_grad = norm_back(
        up_ref[...], normed_ref[...], stats_ref[...], param(param_ref, GAIN + 2)
    )
    residual = out_ref[...] + source
    residual_ref[...] = residual
    low = residual.astype(BF).astype(F32)
    small_ref[...] = pack_rows([gain_grad, shift_grad, col_sum(low)])
    send_taps(low, w_ref, taps_ref, (q0, q1, q2, q3))


def send_taps(gradient, w_ref, taps_ref, piece_refs):
    taps = spread_taps(gradient)
    taps_ref[...] = taps
    for k, ref in enumerate(piece_refs):
        ref[...] = dot_nt(taps, w_ref[0, 128 * k : 128 * k + 128, :]).astype(ref.dtype)


def swish_back(gradient, normed, gain, shift):
    pre = normed * gain + shift
    gate = jax.nn.sigmoid(pre)
    return gradient * (gate * (1.0 + pre * (1.0 - gate)))


def second_back_kernel(
    scalars,
    p0,
    p1,
    p2,
    p3,
    hidden_ref,
    stats_ref,
    param_ref,
    _,
    __,
    w_ref,
    taps_ref,
    small_ref,
    q0,
    q1,
    q2,
    q3,
):
    gradient = p0[...] + p1[...].astype(F32) + p2[...].astype(F32) + p3[...].astype(F32)
    stats = stats_ref[...]
    normed = renormed(hidden_ref[...], stats)
    gain = param(param_ref, GAIN + 1)
    upstream = swish_back(gradient, normed, gain, param(param_ref, SHIFT + 1))
    source, gain_grad, shift_grad = norm_back(upstream, normed, stats, gain)
    low = source.astype(BF).astype(F32)
    small_ref[...] = pack_rows([gain_grad, shift_grad, col_sum(low)])
    send_taps(low, w_ref, taps_ref, (q0, q1, q2, q3))


def first_back_kernel(
    scalars,
    p0,
    p1,
    p2,
    p3,
    x_ref,
    stats_ref,
    param_ref,
    residual_ref,
    _,
    __,
    ___,
    grad_ref,
    small_ref,
):
    gradient = p0[...] + p1[...].astype(F32) + p2[...].astype(F32) + p3[...].astype(F32)
    stats = stats_ref[...]
    normed = renormed(x_ref[...].astype(F32), stats)
    gain = param(param_ref, GAIN)
    upstream = swish_back(gradient, normed, gain, param(param_ref, SHIFT))
    source, gain_grad, shift_grad = norm_back(upstream, normed, stats, gain)
    grad_ref[...] = residual_ref[...] + source
    small_ref[...] = pack_rows([gain_grad, shift_grad])


def conv_one_grad_kernel(scalars, a0, a1, a2, a3, taps_ref, *refs):
    keep_refs, send_ref, grads = refs[:4], refs[4], refs[5]
    full = lanes([a0[...], a1[...], a2[...], a3[...]])
    grads[...] = dot_tn(full, taps_ref[...]).astype(BF)
    for part in range(PARTS):
        _, row = part_row(scalars, part)
        value = grads[pl.ds(row, 64), :]
        if part % 2 == 0:
            keep_refs[part // 2][...] = value
        else:
            send_ref[part // 2] = value


def conv_two_grad_kernel(
    scalars, a0, a1, a2, a3, taps_ref, hot_ref, lat_ref, quant_ref, reset_ref, scale, *refs
):
    keep_refs, send_ref, commit_ref, grads, book = refs[:4], refs[4], refs[5], refs[6], refs[7]
    full = lanes([a0[...], a1[...], a2[...], a3[...]])
    grads[...] = dot_tn(full, taps_ref[...]).astype(BF)
    latents = lat_ref[...]
    difference = latents - quant_ref[...]
    commit_ref[...] = pack_rows([lanes([col_sum(difference * difference), jnp.zeros((1, 64), F32)])])
    high, low = split_low(difference * (-scale))
    sums = dot_tn(lanes([high, low]).astype(BF), hot_ref[...])
    tokens = latents.shape[0]
    where = reset_ref[...] - scalars[2] * tokens
    chosen = (where == lax.broadcasted_iota(jnp.int32, (tokens, CODES), 0)).astype(F32).astype(BF)
    picked = dot_tn(latents.astype(BF), chosen)
    book[0:64] = (sums[:64] + sums[64:]).astype(BF)
    book[64:128] = picked.astype(BF)
    for part in range(PARTS):
        place, row = part_row(scalars, part)
        ref = keep_refs[part // 2] if part % 2 == 0 else send_ref.at[part // 2]
        ref[:, 0:WIDE] = grads[pl.ds(row, 64), :]
        column = pl.ds(pl.multiple_of(place * 128, 128), 128)
        ref[:, WIDE : WIDE + 128] = book[0:64, column]
        ref[:, WIDE + 128 : WIDE + 256] = book[64:128, column]


def finish_two_kernel(
    tokens_all,
    scalars,
    own_ref,
    other_ref,
    book_ref,
    conv_ref,
    gain_ref,
    shift_ref,
    bias_ref,
    commit_ref,
    qkv_ref,
    out_w_ref,
    proj_ref,
    book_grad_ref,
    new_book_ref,
    perplexity_ref,
    attn_bias_ref,
    proj_bias_ref,
    usage,
    proj,
    picked,
):
    extra_sum = jnp.zeros((16, 128), F32)
    total = jnp.zeros((16, 128), F32)
    for part in range(PARTS):
        source = (own_ref if part % 2 == 0 else other_ref).at[part // 2]
        place = scalars[1] ^ part
        rows = pl.ds(pl.multiple_of(place * 64, 64), 64)
        for tap in range(9):
            conv_ref[0, tap, rows, :] = source[:, 128 * tap : 128 * tap + 128].astype(F32)
        column = pl.ds(pl.multiple_of(place * 128, 128), 128)
        book_grad_ref[:, column] = source[:, WIDE : WIDE + 128].astype(F32)
        picked[:, column] = source[:, WIDE + 128 : WIDE + 256].astype(F32)
        for m in range(3):
            qkv_ref[m, rows, :] = source[:, 1408 + 128 * m : 1536 + 128 * m].astype(F32)
        out_w_ref[rows, :] = source[:, 1792:1920].astype(F32)
        proj[rows, :] = source[:, 1920:2048].astype(F32)
        extra = source[0:16, 1920:2048].astype(F32)
        extra_sum = extra_sum + extra
        usage[pl.ds(place, 1), :] = lanes(
            [
                16.0 * extra[0:1, 64:] + extra[2:3, 64:],
                16.0 * extra[1:2, 64:] + extra[3:4, 64:],
            ]
        )
        both = source[0:32, 2048:2176].astype(F32)
        total = total + (both[0:16] + both[16:32])
    for index, row in enumerate((0, 2, 5)):
        gain_ref[index : index + 1] = total[row : row + 1]
        shift_ref[index : index + 1] = total[row + 1 : row + 2]
    bias_ref[0:1] = total[4:5]
    bias_ref[1:2] = total[7:8]
    commit_ref[...] = total[8:9, :64] * (1.0 / tokens_all)
    proj_ref[...] = jnp.transpose(proj[...])[0:64]
    counts = usage[...]
    share = counts * (1.0 / tokens_all)
    terms = share * jnp.log(jnp.maximum(share, 1.0 / tokens_all))
    entropy = jnp.sum(jnp.sum(terms, axis=1, keepdims=True), axis=0, keepdims=True)
    perplexity_ref[...] = jnp.exp(-entropy)
    for block in range(8):
        spot = slice(128 * block, 128 * block + 128)
        new_book_ref[:, spot] = jnp.where(
            counts[block : block + 1] > 0.5, book_ref[:, spot], picked[:, spot]
        )
    for m in range(3):
        attn_bias_ref[m : m + 1] = lanes(
            [extra_sum[4 + 2 * m : 5 + 2 * m, 64:], extra_sum[5 + 2 * m : 6 + 2 * m, 64:]]
        )
    proj_bias_ref[...] = extra_sum[10:11, 64:]


def finish_one_kernel(scalars, own_ref, other_ref, held_ref, conv_ref):
    for part in range(PARTS):
        source = (own_ref if part % 2 == 0 else other_ref).at[part // 2]
        rows = pl.ds(pl.multiple_of((scalars[1] ^ part) * 64, 64), 64)
        for tap in range(9):
            conv_ref[0, tap, rows, :] = source[:, 128 * tap : 128 * tap + 128].astype(F32)


def pair_add_kernel(scalars, k0, k1, k2, k3, get_ref, _, keep_ref, send_ref):
    for i, ref in enumerate((k0, k1, k2, k3)):
        target = (send_ref if i % 2 else keep_ref).at[i // 2]
        target[...] = plus(ref[...], get_ref[i])


def plus(first, second):
    return (first.astype(F32) + second.astype(F32)).astype(BF)


def half_add_kernel(scalars, keep_ref, get_ref, _, own_ref, send_ref):
    own_ref[...] = plus(keep_ref[0], get_ref[0])
    send_ref[...] = plus(keep_ref[1], get_ref[1])


def attn_sum_kernel(scalars, a0, a1, _, keep_ref, send_ref):
    for k in range(2):
        keep_ref[k] = plus(a0[k], a1[k])
        send_ref[k] = plus(a0[2 + k], a1[2 + k])


def tail_first_kernel(
    scalars,
    k0,
    k1,
    k2,
    k3,
    one_get,
    two_keep,
    two_get,
    att_keep,
    att_get,
    _,
    o0,
    o1,
    o2,
    o3,
    two_own,
    two_send,
    att_own,
    att_send,
):
    for i, (ref, out) in enumerate(((k0, o0), (k1, o1), (k2, o2), (k3, o3))):
        out[...] = plus(ref[...], one_get[i])
    two_own[...] = plus(two_keep[0], two_get[0])
    two_send[...] = plus(two_keep[1], two_get[1])
    att_own[...] = plus(att_keep[0], att_get[0])
    att_send[...] = plus(att_keep[1], att_get[1])


def tail_second_kernel(
    scalars,
    o0,
    o1,
    o2,
    o3,
    two_own,
    two_get,
    att_own,
    att_get,
    small_one,
    small_two,
    small_three,
    commit,
    two_ref,
    one_ref,
):
    total = o0[...].astype(F32)
    for ref in (o1, o2, o3):
        total = total + ref[...].astype(F32)
    one_ref[...] = total.astype(BF)
    two_ref[:, 0:1408] = plus(two_own[...], two_get[...])
    two_ref[:, 1408:2048] = plus(att_own[...], att_get[...])
    rows = [small_one[0:1], small_one[1:2]]
    rows += [small_two[m : m + 1] for m in range(3)]
    rows += [small_three[m : m + 1] for m in range(3)]
    rows += [commit[0:1]]
    high, low = split_low(pack_rows(rows, 16))
    two_ref[:, 2048:2176] = rows_of([high, low, jnp.zeros((32, 128), F32)]).astype(BF)


def stack_kernel(scalars, *refs):
    out_ref = refs[-1]
    for k in range(out_ref.shape[0]):
        out_ref[k] = refs[k][...]


def join_kernel(scalars, a0, a1, out_ref):
    out_ref[0:2] = a0[...]
    out_ref[2:4] = a1[...]


def over(axis, array, flip):
    size = lax.axis_size(axis)
    return lax.ppermute(array, axis, [(i, i ^ flip) for i in range(size)])


def flips(array):
    return [over("chan", array, k) for k in (1, 2, 3)]


def plane(array):
    return [array] + [over("dp", array, k) for k in (2, 4, 6)]


def add(*arrays):
    total = arrays[0].astype(F32)
    for array in arrays[1:]:
        total = total + array.astype(F32)
    return total.astype(BF)


def shards(
    latents_in,
    norm_gains,
    norm_shifts,
    conv_weights,
    conv_biases,
    qkv_weights,
    attn_biases,
    out_weight,
    proj_weight,
    proj_bias,
    codebook,
    codes,
    reset_src,
    cotangent,
):
    images = latents_in.shape[0]
    tokens = images * POS
    quarter = tokens // 4
    devices = lax.axis_size("dp")
    tokens_all = tokens * devices
    by_hand = devices == PARTS
    z = lax.axis_index("chan").astype(jnp.int32)
    dp = lax.axis_index("dp").astype(jnp.int32)
    scalars = jnp.stack([z, dp if by_hand else jnp.zeros_like(dp), dp, jnp.zeros_like(dp)])
    x = latents_in.reshape(tokens, 128)
    conv_w = conv_weights.reshape(2, 9, C, 128)

    def whole(shape):
        return pl.BlockSpec(shape, lambda i, n=len(shape): (0,) * n)

    def blocks_call(body, in_specs, out_specs, outs, name, *args, scratch=(), aliases={}):
        return pl.pallas_call(
            body,
            grid=(1,),
            out_shape=outs,
            in_specs=[pl.BlockSpec(memory_space=pltpu.SMEM)] + in_specs,
            out_specs=out_specs,
            scratch_shapes=scratch,
            input_output_aliases=aliases,
            compiler_params=pltpu.CompilerParams(vmem_limit_bytes=VMEM * 2**20),
            cost_estimate=pl.CostEstimate(flops=HEAVY, bytes_accessed=1, transcendentals=0),
            name=name,
        )(scalars, *args)

    act_one, stats_one = call(
        first_norm_kernel,
        [sds((tokens, 128), BF), sds((8, 128), F32)],
        scalars,
        x,
        norm_gains,
        norm_shifts,
        flops=HEAVY,
        name="first_norm",
    )
    pieces_one = [act_one] + flips(act_one)
    rows = scalars[1] * 64
    pack = jnp.concatenate(
        [lax.dynamic_slice(qkv_weights[m], (rows, 0), (64, 128)) for m in range(3)]
        + [
            lax.dynamic_slice(out_weight, (rows, 0), (64, 128)),
            lax.dynamic_slice(proj_weight, (rows, 0), (64, 64)),
            jnp.zeros((64, 64), BF),
        ],
        axis=1,
    )
    if by_hand:
        pack_pair = call(
            stack_kernel,
            [sds((2, 64, 640), BF)],
            scalars,
            pack,
            over("chan", pack, 1),
            name="pack_pair",
        )[0]
        pack_far = over("chan", pack_pair, 2)
    params = jnp.concatenate(
        [
            norm_gains,
            norm_shifts,
            conv_biases,
            attn_biases,
            jnp.pad(proj_bias.reshape(1, 64), ((0, 0), (0, 64))),
            jnp.zeros((4, 128), F32),
        ]
    )
    hot, quantized, usage, fixed = call(
        start_kernel,
        [
            sds((tokens, CODES), BF),
            sds((tokens, 64), F32),
            sds((8, 128), F32),
            sds((4, 128, 128), BF),
        ],
        scalars,
        codes,
        codebook.T,
        cotangent.reshape(tokens, 64),
        stats_one,
        scratch=[pltpu.VMEM((tokens, 64), F32)],
        name="start",
    )
    weights_full = pl.pallas_call(
        conv_weight_kernel,
        grid=(2,),
        out_shape=sds((2, C, WIDE), BF),
        in_specs=[
            pl.BlockSpec(memory_space=pltpu.SMEM),
            pl.BlockSpec((1, 9, C, 128), lambda i: (i, 0, 0, 0)),
        ],
        out_specs=pl.BlockSpec((1, C, WIDE), lambda i: (i, 0, 0)),
        compiler_params=pltpu.CompilerParams(vmem_limit_bytes=VMEM * 2**20),
        cost_estimate=pl.CostEstimate(flops=0, bytes_accessed=1, transcendentals=0),
        name="conv_weight",
    )(scalars, conv_w)

    def conv_call(body, index, outs, name, *args):
        specs = []
        for a in args:
            if a is weights_full:
                specs.append(pl.BlockSpec((1, C, WIDE), lambda i: (index, 0, 0)))
            else:
                specs.append(whole(a.shape))
        scratch = ()
        if body is third_back_kernel:
            scratch = [pltpu.VMEM((tokens, 128), F32), pltpu.VMEM((tokens, 128), F32)]
        return blocks_call(
            body, specs, [whole(o.shape) for o in outs], outs, name, *args, scratch=scratch
        )

    hidden, stats_two, act_two = conv_call(
        conv_one_kernel,
        0,
        [sds((tokens, 128), F32), sds((8, 128), F32), sds((tokens, 128), BF)],
        "conv_one",
        *pieces_one,
        weights_full,
        params,
        usage,
    )
    pieces_two = [act_two] + flips(act_two)
    if by_hand:
        block = call(
            join_kernel, [sds((4, 64, 640), BF)], scalars, pack_pair, pack_far, name="pack_join"
        )[0]
        blocks = [block] + [over("dp", block, k) for k in (2, 4, 6)]
    else:
        packed = jnp.concatenate(
            [qkv_weights[0], qkv_weights[1], qkv_weights[2], out_weight, proj_weight]
            + [jnp.zeros((C, 64), BF)],
            axis=1,
        )
        block = jnp.stack([packed] + flips(packed)).reshape(4, PARTS, 64, 640)
        block = jnp.swapaxes(block, 0, 1)
        block_own, block_other = block[0::2], block[1::2]
    normed_three, stats_three, *pays = conv_call(
        conv_two_kernel,
        1,
        [sds((tokens, 128), F32), sds((8, 128), F32)] + [sds((528, 128), BF)] * 4,
        "conv_two",
        *pieces_two,
        weights_full,
        params,
        x,
        fixed,
    )
    normed_pieces = [pays[0]] + [over("chan", pays[k], k) for k in (1, 2, 3)]
    if by_hand:
        block_own = call(
            stack_kernel,
            [sds((4, 4, 64, 640), BF)],
            scalars,
            *blocks,
            name="pack_plane",
        )[0]
        block_other = over("dp", block_own, 1)
    normed, residual_part, bias_rows = call(
        attn_in_kernel,
        [sds((POS, C), BF), sds((quarter, C), F32), sds((8, C), F32)],
        scalars,
        *normed_pieces,
        flops=HEAVY,
        name="attn_in",
    )
    attn_w = call(
        attn_weight_kernel,
        [sds((C, 2304), BF)],
        scalars,
        block_own,
        block_other,
        name="attn_weight",
    )[0]
    *pays, output, lat_grad, mixed, att_grad, qg, kg, vg, sums = call(
        attention_kernel,
        [sds((POS + 192, 128), F32)]
        + [sds((POS + 192, 128), BF)] * 3
        + [sds((quarter, C), BF)] * 5
        + [sds((POS, C), BF), sds((POS, C), BF), sds((8, C), F32)],
        scalars,
        normed,
        residual_part,
        bias_rows,
        *normed_pieces,
        attn_w,
        flops=HEAVY,
        name="attention",
    )

    back_three = [pays[0]] + [over("chan", pays[k], k) for k in (1, 2, 3)]
    *att_keep, att_send = call(
        attn_grad_kernel,
        [sds((4, 64, 640), BF)] * 4 + [sds((4, 4, 64, 640), BF)],
        scalars,
        normed,
        output,
        lat_grad,
        mixed,
        att_grad,
        qg,
        kg,
        vg,
        sums,
        usage,
        scratch=[pltpu.VMEM((C, 2560), BF)],
        name="attn_grad",
    )

    def pair_sum(keep, send, after, name):
        outs = [sds((2,) + keep[0].shape, BF)] * 2
        got = over("dp", send, 1)
        kept, sent = call(pair_add_kernel, outs, scalars, *keep, got, after, name=name)
        return kept, over("dp", sent, 2)

    if by_hand:
        att_kept, att_got = pair_sum(att_keep, att_send, back_three[1], "attn_pair")
    residual_grad, taps_two, latents, small_three, *pays = conv_call(
        third_back_kernel,
        1,
        [
            sds((tokens, 128), F32),
            sds((tokens, WIDE), BF),
            sds((tokens, 64), F32),
            sds((8, 128), F32),
            sds((tokens, 128), F32),
        ]
        + [sds((tokens, 128), BF)] * 3,
        "third_back",
        *back_three,
        normed_three,
        stats_three,
        params,
        att_kept if by_hand else sums,
        weights_full,
    )
    back_two = [pays[0]] + [over("chan", pays[k], k) for k in (1, 2, 3)]
    book_scale = 2.0 * CODES / tokens_all

    def two_grad(*refs):
        conv_two_grad_kernel(*refs[:10], book_scale, *refs[11:])

    *two_keep, two_send, commit = call(
        two_grad,
        [sds((64, 1408), BF)] * 4 + [sds((4, 64, 1408), BF), sds((8, 128), F32)],
        scalars,
        *pieces_two,
        taps_two,
        hot,
        latents,
        quantized,
        reset_src.reshape(1, CODES),
        back_two[1],
        scratch=[pltpu.VMEM((C, WIDE), BF), pltpu.VMEM((128, CODES), BF)],
        name="conv_two_grad",
    )
    if by_hand:
        att_own, att_sent = call(
            half_add_kernel,
            [sds((4, 64, 640), BF)] * 2,
            scalars,
            att_kept,
            att_got,
            back_two[1],
            name="attn_half",
        )
        att_got = over("dp", att_sent, 4)
    taps_one, small_two, *pays = conv_call(
        second_back_kernel,
        0,
        [sds((tokens, WIDE), BF), sds((8, 128), F32), sds((tokens, 128), F32)]
        + [sds((tokens, 128), BF)] * 3,
        "second_back",
        *back_two,
        hidden,
        stats_two,
        params,
        att_own if by_hand else sums,
        two_keep[0],
        weights_full,
    )
    back_one = [pays[0]] + [over("chan", pays[k], k) for k in (1, 2, 3)]
    *one_keep, one_send = call(
        conv_one_grad_kernel,
        [sds((64, WIDE), BF)] * 4 + [sds((4, 64, WIDE), BF)],
        scalars,
        *pieces_one,
        taps_one,
        scratch=[pltpu.VMEM((C, WIDE), BF)],
        name="conv_one_grad",
    )
    if by_hand:
        two_kept, two_got = pair_sum(two_keep, two_send, back_one[1], "conv_two_pair")
        att_kept, att_sent = call(
            attn_sum_kernel,
            [sds((2, 64, 640), BF)] * 2,
            scalars,
            att_own,
            att_got,
            back_one[1],
            name="attn_sum",
        )
        att_got = over("chan", att_sent, 2)
    grad_latents, small_one = call(
        first_back_kernel,
        [sds((tokens, 128), F32), sds((8, 128), F32)],
        scalars,
        *back_one,
        x,
        stats_one,
        params,
        residual_grad,
        one_keep[0],
        two_kept if by_hand else sums,
        att_kept if by_hand else sums,
        flops=HEAVY,
        name="first_back",
    )

    if by_hand:
        o0, o1, o2, o3, two_own, two_sent, att_own, att_sent = call(
            tail_first_kernel,
            [sds((64, WIDE), BF)] * 4 + [sds((64, 1408), BF)] * 2 + [sds((64, 640), BF)] * 2,
            scalars,
            *one_keep,
            over("dp", one_send, 1),
            two_kept,
            two_got,
            att_kept,
            att_got,
            small_one,
            flops=HEAVY,
            name="tail_first",
        )
        two, one = call(
            tail_second_kernel,
            [sds((64, 2176), BF), sds((64, WIDE), BF)],
            scalars,
            o0,
            over("dp", o1, 2),
            over("dp", o2, 4),
            over("dp", o3, 6),
            two_own,
            over("dp", two_sent, 4),
            att_own,
            over("chan", att_sent, 1),
            small_one,
            small_two,
            small_three,
            commit,
            flops=HEAVY,
            name="tail_second",
        )
        all_two, all_one = plane(two), plane(one)
        two_own = call(
            stack_kernel,
            [sds((4, 64, 2176), BF)],
            scalars,
            *all_two,
            flops=HEAVY,
            name="stack_two",
        )[0]
        two_other = over("dp", two_own, 1)
        one_own = call(stack_kernel, [sds((4, 64, WIDE), BF)], scalars, *all_one, name="stack_one")[0]
        one_other = over("dp", one_own, 1)
    else:

        def total(keep, send):
            parts = jnp.stack([jnp.stack(keep), send]).astype(F32)
            return lax.psum(parts, "dp").astype(BF)

        att_sum = total(att_keep, att_send)
        att_sum = add(att_sum[:, :, 0], *[over("chan", att_sum[:, :, k], k) for k in (1, 2, 3)])
        small = jnp.concatenate([small_one[0:2], small_two[0:3], small_three[0:3], commit[0:1]])
        small = jnp.concatenate([lax.psum(small, "dp"), jnp.zeros((7, 128), F32)])
        high = lax.reduce_precision(small, 8, 7)
        smalls = jnp.concatenate([high, small - high, jnp.zeros((32, 128), F32)]).astype(BF)
        smalls = jnp.zeros((2, 4, 64, 128), BF).at[0, 0].set(smalls)
        two_sum = total(two_keep, two_send)
        two_own, two_other = jnp.concatenate([two_sum, att_sum, smalls], axis=3)
        one_own, one_other = total(one_keep, one_send)

    def finish_two(*refs):
        finish_two_kernel(float(tokens_all), *refs)

    outs = [
        sds((2, 9, C, 128), F32),
        sds((3, 128), F32),
        sds((3, 128), F32),
        sds((2, 128), F32),
        sds((1, 64), F32),
        sds((3, C, 128), F32),
        sds((C, 128), F32),
        sds((64, C), F32),
        sds((64, CODES), F32),
        sds((64, CODES), F32),
        sds((1, 1), F32),
        sds((3, 128), F32),
        sds((1, 64), F32),
    ]
    (
        conv_held,
        gain_grad,
        shift_grad,
        conv_bias_grad,
        commitment,
        qkv_grad,
        out_grad,
        proj_grad,
        book_grad,
        new_codebook,
        perplexity,
        attn_bias_grad,
        proj_bias_grad,
    ) = blocks_call(
        finish_two,
        [whole((4, 64, 2176)), whole((4, 64, 2176)), whole((64, CODES))],
        [pl.BlockSpec((1, 9, C, 128), lambda i: (1, 0, 0, 0))] + [whole(o.shape) for o in outs[1:]],
        outs,
        "finish_two",
        two_own,
        two_other,
        codebook.T,
        scratch=[
            pltpu.VMEM((8, 128), F32),
            pltpu.VMEM((C, 128), F32),
            pltpu.VMEM((64, CODES), F32),
        ],
    )
    conv_grad = blocks_call(
        finish_one_kernel,
        [whole((4, 64, WIDE)), whole((4, 64, WIDE)), pl.BlockSpec(memory_space=pl.ANY)],
        [pl.BlockSpec((1, 9, C, 128), lambda i: (0, 0, 0, 0))],
        [sds((2, 9, C, 128), F32)],
        "finish_one",
        one_own,
        one_other,
        conv_held,
        aliases={3: 0},
    )[0]

    return (
        latents.reshape(images, LAT, LAT, -1),
        commitment.reshape(64),
        perplexity.reshape(()),
        new_codebook.T,
        grad_latents.reshape(images, LAT, LAT, 128),
        gain_grad,
        shift_grad,
        conv_grad.reshape(2, 3, 3, C, 128),
        conv_bias_grad,
        qkv_grad,
        attn_bias_grad,
        out_grad,
        proj_grad.T,
        proj_bias_grad.reshape(64),
        book_grad.T,
    )


def solution(mesh):
    return jax.shard_map(
        shards,
        mesh=mesh,
        in_specs=(
            P("dp", None, None, "chan"),
            P(None, "chan"),
            P(None, "chan"),
            P(None, None, None, None, "chan"),
            P(None, "chan"),
            P(None, None, "chan"),
            P(None, "chan"),
            P(None, "chan"),
            P(None, "chan"),
            P("chan"),
            P(None, "chan"),
            P("dp", None, None),
            P(),
            P("dp", None, None, "chan"),
        ),
        out_specs=(
            P("dp", None, None, "chan"),
            P("chan"),
            P(),
            P(None, "chan"),
            P("dp", None, None, "chan"),
            P(None, "chan"),
            P(None, "chan"),
            P(None, None, None, None, "chan"),
            P(None, "chan"),
            P(None, None, "chan"),
            P(None, "chan"),
            P(None, "chan"),
            P(None, "chan"),
            P("chan"),
            P(None, "chan"),
        ),
        check_vma=False,
    )
```

```python
import jax
import jax.numpy as jnp
from jax import lax
from jax.experimental import pallas as pl
from jax.experimental.pallas import tpu as pltpu
from jax.sharding import PartitionSpec as P

F32 = jnp.float32
BF = jnp.bfloat16
C = 512
CODES = 1024
LAT = 16
POS = LAT * LAT
EPSILON = 1e-06
BETA = 0.25
SCORE_SCALE = float(C) ** (-0.5)
GROUP_COUNT = float(POS * 16)
WIDE = 1152
VMEM = 20
HEAVY = 10**11
PARTS = 8


def call(body, outs, *args, scratch=(), flops=0, name=None, space=pltpu.VMEM, vmem=VMEM):
    result = pl.pallas_call(
        body,
        out_shape=list(outs),
        in_specs=[pl.BlockSpec(memory_space=pltpu.SMEM)]
        + [pl.BlockSpec(memory_space=space)] * (len(args) - 1),
        out_specs=[pl.BlockSpec(memory_space=pltpu.VMEM)] * len(outs),
        scratch_shapes=list(scratch),
        compiler_params=pltpu.CompilerParams(vmem_limit_bytes=vmem * 2**20),
        cost_estimate=pl.CostEstimate(flops=flops, bytes_accessed=1, transcendentals=0),
        name=name,
    )(*args)
    return result


def sds(shape, dtype):
    return jax.ShapeDtypeStruct(shape, dtype)


def dot(a, b):
    return jnp.dot(a, b, preferred_element_type=F32)


def dot_nt(a, b):
    return lax.dot_general(a, b, (((1,), (1,)), ((), ())), preferred_element_type=F32)


def dot_tn(a, b):
    return lax.dot_general(a, b, (((0,), (0,)), ((), ())), preferred_element_type=F32)


def lanes(parts):
    return jnp.concatenate(parts, axis=1)


def rows_of(parts):
    return jnp.concatenate(parts, axis=0)


def pack_rows(vectors, height=8):
    width = vectors[0].shape[1]
    spot = lax.broadcasted_iota(jnp.int32, (height, width), 0)
    result = jnp.zeros((height, width), F32)
    for index, vector in enumerate(vectors):
        result = jnp.where(spot == index, vector, result)
    return result


def split_low(values):
    high = values.astype(BF).astype(F32)
    return high, values - high


def group_sums(rows):
    first = lax.broadcasted_iota(jnp.int32, (128, 128), 0) >> 4
    second = lax.broadcasted_iota(jnp.int32, (128, 128), 1) >> 4
    ones = (first == second).astype(F32).astype(BF)
    high, rest = split_low(rows)
    middle, low = split_low(rest)
    stacked = rows_of([high, middle, low, jnp.zeros_like(high)]).astype(BF)
    summed = dot(stacked, ones)
    return summed[0:8] + summed[8:16] + summed[16:24]


def col_sum(values):
    return jnp.sum(values, axis=0, keepdims=True)


def moments(values):
    one, two = values[:POS], values[POS:]
    mean = group_sums(pack_rows([col_sum(one), col_sum(two)])) * (1.0 / GROUP_COUNT)
    one, two = one - mean[0:1], two - mean[1:2]
    variance = group_sums(pack_rows([col_sum(one * one), col_sum(two * two)])) * (
        1.0 / GROUP_COUNT
    )
    inverse = lax.rsqrt(variance + EPSILON)
    deviation = jnp.sqrt(variance + EPSILON)
    normed = rows_of([one * inverse[0:1], two * inverse[1:2]])
    stats = pack_rows(
        [mean[0:1], mean[1:2], inverse[0:1], inverse[1:2], deviation[0:1], deviation[1:2]]
    )
    return normed, stats


def renormed(values, stats):
    return rows_of(
        [
            (values[:POS] - stats[0:1]) * stats[2:3],
            (values[POS:] - stats[1:2]) * stats[3:4],
        ]
    )


def norm_back(upstream, normed, stats, gain):
    sides = [(upstream[:POS], normed[:POS]), (upstream[POS:], normed[POS:])]
    plain = [col_sum(u) for u, _ in sides]
    weighted = [col_sum(u * n) for u, n in sides]
    means = group_sums(
        pack_rows([plain[0] * gain, plain[1] * gain, weighted[0] * gain, weighted[1] * gain])
    ) * (1.0 / GROUP_COUNT)
    parts = [
        stats[2 + m : 3 + m] * (u * gain - means[m : m + 1] - n * means[2 + m : 3 + m])
        for m, (u, n) in enumerate(sides)
    ]
    return rows_of(parts), weighted[0] + weighted[1], plain[0] + plain[1]


GAIN, SHIFT, CONV_BIAS, ATTN_BIAS, PROJ_BIAS = 0, 3, 6, 8, 11


def param(ref, index):
    return ref[index : index + 1]


def column_masks(height):
    column = lax.broadcasted_iota(jnp.int32, (height, 128), 0) & (LAT - 1)
    return column >= 1, column <= LAT - 2


def later_rows(values):
    blank = jnp.zeros((LAT, values.shape[1]), values.dtype)
    return rows_of([values[LAT:POS], blank, values[POS + LAT :], blank])


def earlier_rows(values):
    blank = jnp.zeros((LAT, values.shape[1]), values.dtype)
    return rows_of([blank, values[: POS - LAT], blank, values[POS : 2 * POS - LAT]])


def conv_forward(pieces, w_ref, z):
    full = lanes(pieces)
    height = full.shape[0]
    inner, outer = column_masks(height)
    blocks = [pl.ds(pl.multiple_of((z ^ k) * 128, 128), 128) for k in range(4)]
    sums = []
    for col_tap in range(3):
        total = None
        for row_tap in range(3):
            tap = 3 * row_tap + col_tap
            part = dot(full, rows_of([w_ref[0, tap, block, :] for block in blocks]))
            if row_tap == 0:
                part = earlier_rows(part)
            elif row_tap == 2:
                part = later_rows(part)
            total = part if total is None else total + part
        sums.append(total)
    left = jnp.where(inner, pltpu.roll(sums[0], 1, 0), 0.0)
    right = jnp.where(outer, pltpu.roll(sums[2], height - 1, 0), 0.0)
    return sums[1] + left + right


def spread_taps(gradient):
    height = gradient.shape[0]
    inner, outer = column_masks(height)
    by_column = [
        jnp.where(outer, pltpu.roll(gradient, height - 1, 0), 0.0),
        gradient,
        jnp.where(inner, pltpu.roll(gradient, 1, 0), 0.0),
    ]
    copies = [None] * 9
    for col_tap in range(3):
        copies[col_tap] = later_rows(by_column[col_tap])
        copies[3 + col_tap] = by_column[col_tap]
        copies[6 + col_tap] = earlier_rows(by_column[col_tap])
    return lanes([c.astype(BF) for c in copies])


def part_row(scalars, part):
    place = scalars[1] ^ part
    block = (place >> 1) ^ scalars[0]
    return place, pl.multiple_of(block * 128 + (place & 1) * 64, 64)


def fetch(pairs, sems):
    copies = [
        pltpu.make_async_copy(source, target, sems.at[i])
        for i, (source, target) in enumerate(pairs)
    ]
    for copy in copies:
        copy.start()
    for copy in copies:
        copy.wait()


def begin_kernel(
    scalars,
    x_any,
    gain_any,
    shift_any,
    conv_b_any,
    attn_b_any,
    proj_b_any,
    qkv_any,
    out_w_any,
    proj_any,
    act_ref,
    stats_ref,
    pack_ref,
    param_ref,
    x_ref,
    gain_ref,
    shift_ref,
    conv_b_ref,
    attn_b_ref,
    proj_b_ref,
    weights,
    proj_ref,
    proj,
    sems,
):
    own = pl.ds(pl.multiple_of(scalars[1] * 64, 64), 64)
    fetch(
        [
            (x_any, x_ref),
            (gain_any, gain_ref),
            (shift_any, shift_ref),
            (conv_b_any, conv_b_ref),
            (attn_b_any, attn_b_ref),
            (proj_b_any, proj_b_ref),
            (out_w_any.at[own, :], weights.at[3]),
            (proj_any, proj_ref),
        ]
        + [(qkv_any.at[m, own, :], weights.at[m]) for m in range(3)],
        sems,
    )
    normed, stats = moments(x_ref[...].astype(F32))
    pre = normed * gain_ref[0:1] + shift_ref[0:1]
    act_ref[...] = (pre * jax.nn.sigmoid(pre)).astype(BF)
    stats_ref[...] = stats
    for m in range(4):
        pack_ref[:, 128 * m : 128 * m + 128] = weights[m]
    proj[...] = jnp.transpose(proj_ref[...].astype(F32))
    pack_ref[:, 512:640] = lanes([proj[own, :], jnp.zeros((64, 64), F32)]).astype(BF)
    rows = [gain_ref[m : m + 1] for m in range(3)] + [shift_ref[m : m + 1] for m in range(3)]
    rows += [conv_b_ref[m : m + 1] for m in range(2)] + [attn_b_ref[m : m + 1] for m in range(3)]
    rows += [lanes([proj_b_ref[...], jnp.zeros_like(proj_b_ref[...])])]
    param_ref[...] = pack_rows(rows, 16)


def code_column(codes):
    grid = rows_of([codes[m] for m in range(codes.shape[0])])
    height = grid.shape[0] * LAT
    high = grid >> 5
    both = lanes([high.astype(F32), (grid - (high << 5)).astype(F32)]).astype(BF)
    lines = lax.broadcasted_iota(jnp.int32, (height, grid.shape[0]), 0) >> 4
    own = (lines == lax.broadcasted_iota(jnp.int32, lines.shape, 1)).astype(F32).astype(BF)
    spread = dot(own, both)
    column = lax.broadcasted_iota(jnp.int32, (height, LAT), 0) & (LAT - 1)
    here = column == lax.broadcasted_iota(jnp.int32, (height, LAT), 1)
    merged = 32.0 * spread[:, :LAT] + spread[:, LAT:]
    return jnp.sum(jnp.where(here, merged, 0.0), axis=1, keepdims=True).astype(jnp.int32)


def start_kernel(scalars, codes_ref, book_ref, cot_ref, _, hot_ref, quant_ref, usage_ref, fixed_ref, start):
    tokens = hot_ref.shape[0]
    hot32 = (
        code_column(codes_ref[...]) == lax.broadcasted_iota(jnp.int32, (tokens, CODES), 1)
    ).astype(F32)
    hot = hot32.astype(BF)
    hot_ref[...] = hot
    counts = col_sum(hot32)
    usage_ref[...] = pack_rows([counts[:, 128 * i : 128 * i + 128] for i in range(8)])
    high, rest = split_low(book_ref[...])
    middle, low = split_low(rest)
    picked = dot_nt(hot, rows_of([high, middle, low]).astype(BF))
    width = book_ref.shape[0]
    quantized = picked[:, :width] + picked[:, width : 2 * width] + picked[:, 2 * width :]
    quant_ref[...] = quantized
    start[...] = cot_ref[...].astype(F32) - 2.0 * BETA * quantized
    for k in range(4):
        row = (scalars[0] ^ k) * 128
        one = start[pl.ds(pl.multiple_of(row, 64), 64), :]
        two = start[pl.ds(pl.multiple_of(row + 64, 64), 64), :]
        fixed_ref[k] = lanes([one, two]).astype(BF)


def attn_weight_kernel(scalars, own_ref, other_ref, o_ref):
    for part in range(PARTS):
        source = (own_ref if part % 2 == 0 else other_ref).at[part // 2]
        _, row = part_row(scalars, part)
        spot = pl.ds(row, 64)
        for k in range(4):
            for m in range(4):
                o_ref[spot, 512 * m + 128 * k : 512 * m + 128 * k + 128] = source[
                    k, :, 128 * m : 128 * m + 128
                ]
        for pair in range(2):
            o_ref[spot, 2048 + 128 * pair : 2176 + 128 * pair] = lanes(
                [source[2 * pair + i, :, 512:576] for i in range(2)]
            )


def conv_one_kernel(
    scalars, a0, a1, a2, a3, w_ref, param_ref, _, hidden_ref, stats_ref, act_ref
):
    pieces = [a0[...], a1[...], a2[...], a3[...]]
    hidden = conv_forward(pieces, w_ref, scalars[0]) + param(param_ref, CONV_BIAS)
    hidden_ref[...] = hidden
    normed, stats = moments(hidden)
    stats_ref[...] = stats
    pre = normed * param(param_ref, GAIN + 1) + param(param_ref, SHIFT + 1)
    act_ref[...] = (pre * jax.nn.sigmoid(pre)).astype(BF)


def conv_two_kernel(
    scalars, a0, a1, a2, a3, w_ref, param_ref, x_ref, fixed_ref, normed_ref, stats_ref, *pay_refs
):
    residual = x_ref[...].astype(F32) + (
        conv_forward([a0[...], a1[...], a2[...], a3[...]], w_ref, scalars[0])
        + param(param_ref, CONV_BIAS + 1)
    )
    normed, stats = moments(residual)
    normed_ref[...] = normed
    stats_ref[...] = stats
    gain, shift = param(param_ref, GAIN + 2), param(param_ref, SHIFT + 2)
    for k, ref in enumerate(pay_refs):
        target = scalars[0] ^ k
        own, other = target * 128, (target ^ 1) * 128
        ref[0:128] = (
            normed_ref[pl.ds(pl.multiple_of(other, 128), 128), :] * gain + shift
        ).astype(BF)
        high, low = split_low(normed_ref[pl.ds(pl.multiple_of(own, 128), 128), :])
        ref[128:256] = high.astype(BF)
        ref[256:384] = low.astype(BF)
        is_two = jnp.broadcast_to(target >> 1, (1, 128)) == 1
        mean = jnp.where(is_two, stats[1:2], stats[0:1])
        deviation = jnp.where(is_two, stats[5:6], stats[4:5])
        rows = list(split_low(mean)) + list(split_low(deviation))
        for index in (GAIN + 2, SHIFT + 2, ATTN_BIAS, ATTN_BIAS + 1, ATTN_BIAS + 2, PROJ_BIAS):
            rows.extend(split_low(param(param_ref, index)))
        ref[384:400] = pack_rows(rows, 16).astype(BF)
        ref[400:464] = fixed_ref[k]


def attn_in_kernel(scalars, n0, n1, n2, n3, norm_ref, residual_ref, bias_ref):
    pieces = [n0, n1, n2, n3]
    tails = [n[384:400].astype(F32) for n in pieces]

    def vector(index, width=128):
        row = 2 * index
        return lanes([t[row : row + 1, :width] + t[row + 1 : row + 2, :width] for t in tails])

    mean, deviation, gain, shift = [vector(index) for index in range(4)]
    empty = jnp.zeros((1, 256), F32)
    bias_ref[...] = pack_rows([vector(4), vector(5), vector(6), lanes([vector(7, 64), empty])])
    own = lanes([n[128:256].astype(F32) + n[256:384].astype(F32) for n in pieces])
    residual_ref[...] = own * deviation + mean
    norm_ref[0:128] = (own * gain + shift).astype(BF)
    norm_ref[128:POS] = lanes([n[0:128] for n in pieces])


def attention_kernel(
    scalars, norm_ref, residual_ref, bias_ref, n0, n1, n2, n3, w_ref, *refs
):
    pay_refs = refs[:4]
    out_ref, lat_grad_ref, mixed_ref, att_grad_ref, qg_ref, kg_ref, vg_ref, sums_ref = refs[4:]
    query_bias, value_bias, out_bias = [bias_ref[m : m + 1] for m in range(3)]
    proj_bias = bias_ref[3:4, 0:256]
    pieces = [n0, n1, n2, n3]
    normed = norm_ref[...]
    query = (dot(norm_ref[0:128], w_ref[:, 0:512]) + query_bias).astype(BF)
    keys = dot(normed, w_ref[:, 512:1024]).astype(BF)
    values = (dot(normed, w_ref[:, 1024:1536]) + value_bias).astype(BF)
    scores = dot_nt(query, keys) * SCORE_SCALE
    weights = jnp.exp(scores - jnp.max(scores, axis=1, keepdims=True))
    probs = weights / jnp.sum(weights, axis=1, keepdims=True)
    probs_low = probs.astype(BF)
    mixed = dot(probs_low, values).astype(BF)
    mixed_ref[...] = mixed
    attended = dot(mixed, w_ref[:, 1536:2048]) + out_bias
    output = (residual_ref[...] + attended).astype(BF)
    out_ref[...] = output
    latents = dot(output, w_ref[:, 2048:2304]) + proj_bias
    fixed = []
    for n in pieces:
        both = n[400:464].astype(F32)
        fixed.append(rows_of([both[:, :64], both[:, 64:]]))
    lat_grad = (lanes(fixed) + 2.0 * BETA * latents).astype(BF)
    blank = jnp.zeros((128, 64), BF)
    for k in range(4):
        lat_grad_ref[:, 128 * k : 128 * k + 128] = lanes([lat_grad[:, 64 * k : 64 * k + 64], blank])
    out_grad = dot_nt(lat_grad, w_ref[:, 2048:2304])
    att_grad = out_grad.astype(BF)
    att_grad_ref[...] = att_grad
    mixed_grad = dot_nt(att_grad, w_ref[:, 1536:2048]).astype(BF)
    probs_grad = dot_nt(mixed_grad, values)
    row_dot = jnp.sum(probs * probs_grad, axis=1, keepdims=True)
    score_grad = (probs * (probs_grad - row_dot)).astype(BF)
    query_grad = (dot(score_grad, keys) * SCORE_SCALE).astype(BF)
    key_grad = (dot_tn(score_grad, query) * SCORE_SCALE).astype(BF)
    value_grad = dot_tn(probs_low, mixed_grad).astype(BF)
    qg_ref[...] = query_grad
    kg_ref[...] = key_grad
    vg_ref[...] = value_grad
    upstream = dot_nt(key_grad, w_ref[:, 512:1024]) + dot_nt(value_grad, w_ref[:, 1024:1536])
    upstream_own = upstream[:128] + dot_nt(query_grad, w_ref[:, 0:512])
    for k in range(4):
        ref = pay_refs[k]
        ref[0:128] = upstream_own[:, 128 * k : 128 * k + 128].astype(ref.dtype)
        ref[128:POS] = upstream[128:, 128 * k : 128 * k + 128].astype(ref.dtype)
        ref[POS : POS + 128] = out_grad[:, 128 * k : 128 * k + 128].astype(ref.dtype)
        piece = latents[:, 64 * k : 64 * k + 64]
        ref[POS + 128 : POS + 192] = lanes([piece[:64], piece[64:]]).astype(ref.dtype)
    sums_ref[...] = pack_rows(
        [
            col_sum(query_grad.astype(F32)),
            col_sum(value_grad.astype(F32)),
            col_sum(att_grad.astype(F32)),
            lanes(
                [
                    part
                    for k in range(4)
                    for part in (
                        col_sum(lat_grad[:, 64 * k : 64 * k + 64].astype(F32)),
                        jnp.zeros((1, 64), F32),
                    )
                ]
            ),
        ]
    )


def attn_grad_kernel(
    scalars,
    norm_ref,
    out_ref,
    lat_grad_ref,
    mixed_ref,
    att_grad_ref,
    qg_ref,
    kg_ref,
    vg_ref,
    sums_ref,
    usage_ref,
    *refs,
):
    keep_refs, send_ref, grads = refs[:4], refs[4], refs[5]
    grads[:, 0:512] = dot_tn(norm_ref[0:128], qg_ref[...]).astype(BF)
    grads[:, 512:1024] = dot_tn(norm_ref[...], kg_ref[...]).astype(BF)
    grads[:, 1024:1536] = dot_tn(norm_ref[...], vg_ref[...]).astype(BF)
    grads[:, 1536:2048] = dot_tn(mixed_ref[...], att_grad_ref[...]).astype(BF)
    grads[:, 2048:2560] = dot_tn(out_ref[...], lat_grad_ref[...]).astype(BF)
    right = lax.broadcasted_iota(jnp.int32, (16, 128), 1) >= 64

    def halves(vectors, offset):
        blank = jnp.zeros((1, 128), F32)
        entries = [blank] * offset
        for vector in vectors:
            entries += [pltpu.roll(vector, 64, 1), vector]
        return jnp.where(right, pack_rows(entries, 16), 0.0)

    biases = []
    for k in range(4):
        vectors = [sums_ref[m : m + 1, 128 * k : 128 * k + 128] for m in range(4)]
        biases.append(halves(vectors, 4))
    tens = jnp.floor(usage_ref[...] * (1.0 / 16.0))
    ones = usage_ref[...] - 16.0 * tens
    for part in range(PARTS):
        place, row = part_row(scalars, part)
        is_first = (jnp.broadcast_to(place, (16, 128)) == 0).astype(F32)
        here = jnp.broadcast_to(place, (8, 128)) == lax.broadcasted_iota(jnp.int32, (8, 128), 0)
        counts = [col_sum(jnp.where(here, digit, 0.0)) for digit in (tens, ones)]
        for k in range(4):
            ref = keep_refs[part // 2].at[k] if part % 2 == 0 else send_ref.at[part // 2, k]
            for m in range(4):
                ref[:, 128 * m : 128 * m + 128] = grads[
                    pl.ds(row, 64), 512 * m + 128 * k : 512 * m + 128 * k + 128
                ]
            extra = biases[k] * is_first
            if k == 0:
                extra = extra + halves(counts, 0)
            block = slice(2048 + 128 * k, 2176 + 128 * k)
            ref[0:16, 512:640] = (grads[pl.ds(row, 16), block].astype(F32) + extra).astype(BF)
            ref[16:64, 512:640] = grads[pl.ds(row + 16, 48), block]


def third_back_kernel(
    scalars,
    p0,
    p1,
    p2,
    p3,
    normed_ref,
    stats_ref,
    param_ref,
    _,
    w_ref,
    residual_ref,
    taps_ref,
    lat_ref,
    small_ref,
    q0,
    q1,
    q2,
    q3,
    up_ref,
    out_ref,
):
    z = scalars[0]
    for near, far, base in ((p0, p1, z), (p2, p3, z ^ 2)):
        first, second = near[0:POS].astype(F32), far[0:POS].astype(F32)
        up_ref[pl.ds(pl.multiple_of(base * 128, 128), 128), :] = first[:128] + second[128:]
        up_ref[pl.ds(pl.multiple_of((base ^ 1) * 128, 128), 128), :] = first[128:] + second[:128]
    for k, ref in enumerate((p0, p1, p2, p3)):
        row = (z ^ k) * 128
        out_ref[pl.ds(pl.multiple_of(row, 128), 128), :] = ref[POS : POS + 128].astype(F32)
        piece = ref[POS + 128 : POS + 192].astype(F32)
        lat_ref[pl.ds(pl.multiple_of(row, 64), 64), :] = piece[:, :64]
        lat_ref[pl.ds(pl.multiple_of(row + 64, 64), 64), :] = piece[:, 64:]
    source, gain_grad, shift_grad = norm_back(
        up_ref[...], normed_ref[...], stats_ref[...], param(param_ref, GAIN + 2)
    )
    residual = out_ref[...] + source
    residual_ref[...] = residual
    low = residual.astype(BF).astype(F32)
    small_ref[...] = pack_rows([gain_grad, shift_grad, col_sum(low)])
    send_taps(low, w_ref, scalars[0], taps_ref, (q0, q1, q2, q3))


def send_taps(gradient, w_ref, z, taps_ref, piece_refs):
    taps = spread_taps(gradient)
    taps_ref[...] = taps
    for k, ref in enumerate(piece_refs):
        block = pl.ds(pl.multiple_of((z ^ k) * 128, 128), 128)
        weights = lanes([w_ref[0, tap, block, :] for tap in range(9)])
        ref[...] = dot_nt(taps, weights).astype(ref.dtype)


def swish_back(gradient, normed, gain, shift):
    pre = normed * gain + shift
    gate = jax.nn.sigmoid(pre)
    return gradient * (gate * (1.0 + pre * (1.0 - gate)))


def second_back_kernel(
    scalars,
    p0,
    p1,
    p2,
    p3,
    hidden_ref,
    stats_ref,
    param_ref,
    _,
    __,
    w_ref,
    taps_ref,
    small_ref,
    q0,
    q1,
    q2,
    q3,
):
    gradient = p0[...] + p1[...].astype(F32) + p2[...].astype(F32) + p3[...].astype(F32)
    stats = stats_ref[...]
    normed = renormed(hidden_ref[...], stats)
    gain = param(param_ref, GAIN + 1)
    upstream = swish_back(gradient, normed, gain, param(param_ref, SHIFT + 1))
    source, gain_grad, shift_grad = norm_back(upstream, normed, stats, gain)
    low = source.astype(BF).astype(F32)
    small_ref[...] = pack_rows([gain_grad, shift_grad, col_sum(low)])
    send_taps(low, w_ref, scalars[0], taps_ref, (q0, q1, q2, q3))


def first_back_kernel(
    scalars,
    p0,
    p1,
    p2,
    p3,
    x_ref,
    stats_ref,
    param_ref,
    residual_ref,
    _,
    __,
    ___,
    grad_ref,
    small_ref,
):
    gradient = p0[...] + p1[...].astype(F32) + p2[...].astype(F32) + p3[...].astype(F32)
    stats = stats_ref[...]
    normed = renormed(x_ref[...].astype(F32), stats)
    gain = param(param_ref, GAIN)
    upstream = swish_back(gradient, normed, gain, param(param_ref, SHIFT))
    source, gain_grad, shift_grad = norm_back(upstream, normed, stats, gain)
    grad_ref[...] = residual_ref[...] + source
    small_ref[...] = pack_rows([gain_grad, shift_grad])


def conv_one_grad_kernel(scalars, a0, a1, a2, a3, taps_ref, *refs):
    keep_refs, send_ref, grads = refs[:4], refs[4], refs[5]
    full = lanes([a0[...], a1[...], a2[...], a3[...]])
    grads[...] = dot_tn(full, taps_ref[...]).astype(BF)
    for part in range(PARTS):
        _, row = part_row(scalars, part)
        value = grads[pl.ds(row, 64), :]
        if part % 2 == 0:
            keep_refs[part // 2][...] = value
        else:
            send_ref[part // 2] = value


def conv_two_grad_kernel(
    scalars, a0, a1, a2, a3, taps_ref, hot_ref, lat_ref, quant_ref, reset_ref, scale, *refs
):
    keep_refs, send_ref, commit_ref, grads, book = refs[:4], refs[4], refs[5], refs[6], refs[7]
    full = lanes([a0[...], a1[...], a2[...], a3[...]])
    grads[...] = dot_tn(full, taps_ref[...]).astype(BF)
    latents = lat_ref[...]
    difference = latents - quant_ref[...]
    commit_ref[...] = pack_rows([lanes([col_sum(difference * difference), jnp.zeros((1, 64), F32)])])
    high, low = split_low(difference * (-scale))
    sums = dot_tn(lanes([high, low]).astype(BF), hot_ref[...])
    tokens = latents.shape[0]
    where = reset_ref[...] - scalars[2] * tokens
    chosen = (where == lax.broadcasted_iota(jnp.int32, (tokens, CODES), 0)).astype(F32).astype(BF)
    picked = dot_tn(latents.astype(BF), chosen)
    book[0:64] = (sums[:64] + sums[64:]).astype(BF)
    book[64:128] = picked.astype(BF)
    for part in range(PARTS):
        place, row = part_row(scalars, part)
        ref = keep_refs[part // 2] if part % 2 == 0 else send_ref.at[part // 2]
        ref[:, 0:WIDE] = grads[pl.ds(row, 64), :]
        column = pl.ds(pl.multiple_of(place * 128, 128), 128)
        ref[:, WIDE : WIDE + 128] = book[0:64, column]
        ref[:, WIDE + 128 : WIDE + 256] = book[64:128, column]


def finish_two_kernel(scalars, own_ref, other_ref, conv_ref, book_grad_ref, picked_ref):
    for part in range(PARTS):
        source = (own_ref if part % 2 == 0 else other_ref).at[part // 2]
        place = scalars[1] ^ part
        rows = pl.ds(pl.multiple_of(place * 64, 64), 64)
        for tap in range(9):
            conv_ref[0, tap, rows, :] = source[:, 128 * tap : 128 * tap + 128].astype(F32)
        column = pl.ds(pl.multiple_of(place * 128, 128), 128)
        book_grad_ref[:, column] = source[:, WIDE : WIDE + 128].astype(F32)
        picked_ref[:, column] = source[:, WIDE + 128 : WIDE + 256].astype(F32)


def finish_last_kernel(
    tokens_all,
    scalars,
    own_ref,
    other_ref,
    picked,
    book_ref,
    held_ref,
    conv_ref,
    gain_ref,
    shift_ref,
    bias_ref,
    commit_ref,
    qkv_ref,
    out_w_ref,
    proj_ref,
    new_book_ref,
    perplexity_ref,
    attn_bias_ref,
    proj_bias_ref,
    usage,
    proj,
):
    extra_sum = jnp.zeros((16, 128), F32)
    total = jnp.zeros((16, 128), F32)
    for part in range(PARTS):
        source = (own_ref if part % 2 == 0 else other_ref).at[part // 2]
        place = scalars[1] ^ part
        rows = pl.ds(pl.multiple_of(place * 64, 64), 64)
        for tap in range(9):
            conv_ref[0, tap, rows, :] = source[:, 128 * tap : 128 * tap + 128].astype(F32)
        for m in range(3):
            qkv_ref[m, rows, :] = source[:, 1152 + 128 * m : 1280 + 128 * m].astype(F32)
        out_w_ref[rows, :] = source[:, 1536:1664].astype(F32)
        proj[rows, :] = source[:, 1664:1792].astype(F32)
        extra = source[0:16, 1664:1792].astype(F32)
        extra_sum = extra_sum + extra
        usage[pl.ds(place, 1), :] = lanes(
            [
                16.0 * extra[0:1, 64:] + extra[2:3, 64:],
                16.0 * extra[1:2, 64:] + extra[3:4, 64:],
            ]
        )
        both = source[0:32, 1792:1920].astype(F32)
        total = total + (both[0:16] + both[16:32])
    for index, row in enumerate((0, 2, 5)):
        gain_ref[index : index + 1] = total[row : row + 1]
        shift_ref[index : index + 1] = total[row + 1 : row + 2]
    bias_ref[0:1] = total[4:5]
    bias_ref[1:2] = total[7:8]
    commit_ref[...] = total[8:9, :64] * (1.0 / tokens_all)
    proj_ref[...] = jnp.transpose(proj[...])[0:64]
    counts = usage[...]
    share = counts * (1.0 / tokens_all)
    terms = share * jnp.log(jnp.maximum(share, 1.0 / tokens_all))
    entropy = jnp.sum(jnp.sum(terms, axis=1, keepdims=True), axis=0, keepdims=True)
    perplexity_ref[...] = jnp.exp(-entropy)
    for block in range(8):
        spot = slice(128 * block, 128 * block + 128)
        new_book_ref[:, spot] = jnp.where(
            counts[block : block + 1] > 0.5, book_ref[:, spot], picked[:, spot]
        )
    for m in range(3):
        attn_bias_ref[m : m + 1] = lanes(
            [extra_sum[4 + 2 * m : 5 + 2 * m, 64:], extra_sum[5 + 2 * m : 6 + 2 * m, 64:]]
        )
    proj_bias_ref[...] = extra_sum[10:11, 64:]


def pair_add_kernel(scalars, k0, k1, k2, k3, get_ref, _, keep_ref, send_ref):
    for i, ref in enumerate((k0, k1, k2, k3)):
        target = (send_ref if i % 2 else keep_ref).at[i // 2]
        target[...] = plus(ref[...], get_ref[i])


def plus(first, second):
    return (first.astype(F32) + second.astype(F32)).astype(BF)


def half_add_kernel(scalars, keep_ref, get_ref, _, own_ref, send_ref):
    own_ref[...] = plus(keep_ref[0], get_ref[0])
    send_ref[...] = plus(keep_ref[1], get_ref[1])


def attn_sum_kernel(scalars, a0, a1, _, keep_ref, send_ref):
    for k in range(4):
        (send_ref if k % 2 else keep_ref)[k // 2] = plus(a0[k], a1[k])


def tail_first_kernel(
    scalars,
    k0,
    k1,
    k2,
    k3,
    one_get,
    two_own,
    two_get,
    att_keep,
    att_get,
    _,
    o0,
    o1,
    o2,
    o3,
    two_ref,
    att_own,
    att_send,
):
    for i, (ref, out) in enumerate(((k0, o0), (k1, o1), (k2, o2), (k3, o3))):
        out[...] = plus(ref[...], one_get[i])
    two_ref[...] = plus(two_own[...], two_get[...])
    att_own[...] = plus(att_keep[0], att_get[0])
    att_send[...] = plus(att_keep[1], att_get[1])


def last_kernel(
    scalars, o0, o1, o2, o3, att_own, att_get, small_one, small_two, small_three, commit, last_ref
):
    total = o0[...].astype(F32)
    for ref in (o1, o2, o3):
        total = total + ref[...].astype(F32)
    last_ref[:, 0:WIDE] = total.astype(BF)
    last_ref[:, 1152:1792] = plus(att_own[...], att_get[...])
    rows = [small_one[0:1], small_one[1:2]]
    rows += [small_two[m : m + 1] for m in range(3)]
    rows += [small_three[m : m + 1] for m in range(3)]
    rows += [commit[0:1]]
    high, low = split_low(pack_rows(rows, 16))
    last_ref[:, 1792:1920] = rows_of([high, low, jnp.zeros((32, 128), F32)]).astype(BF)


def stack_kernel(scalars, *refs):
    out_ref = refs[-1]
    for k in range(out_ref.shape[0]):
        out_ref[k] = refs[k][...]


def over(axis, array, flip):
    size = lax.axis_size(axis)
    return lax.ppermute(array, axis, [(i, i ^ flip) for i in range(size)])


def flips(array):
    return [over("chan", array, k) for k in (1, 2, 3)]


def plane(array):
    return [array] + [over("dp", array, k) for k in (2, 4, 6)]


def add(*arrays):
    total = arrays[0].astype(F32)
    for array in arrays[1:]:
        total = total + array.astype(F32)
    return total.astype(BF)


def shards(
    latents_in,
    norm_gains,
    norm_shifts,
    conv_weights,
    conv_biases,
    qkv_weights,
    attn_biases,
    out_weight,
    proj_weight,
    proj_bias,
    codebook,
    codes,
    reset_src,
    cotangent,
):
    images = latents_in.shape[0]
    tokens = images * POS
    quarter = tokens // 4
    devices = lax.axis_size("dp")
    tokens_all = tokens * devices
    by_hand = devices == PARTS
    z = lax.axis_index("chan").astype(jnp.int32)
    dp = lax.axis_index("dp").astype(jnp.int32)
    scalars = jnp.stack([z, dp if by_hand else jnp.zeros_like(dp), dp, jnp.zeros_like(dp)])
    x = latents_in.reshape(tokens, 128)
    conv_w = conv_weights.reshape(2, 9, C, 128)

    def whole(shape):
        return pl.BlockSpec(shape, lambda i, n=len(shape): (0,) * n)

    def blocks_call(body, in_specs, out_specs, outs, name, *args, scratch=(), aliases={}):
        return pl.pallas_call(
            body,
            grid=(1,),
            out_shape=outs,
            in_specs=[pl.BlockSpec(memory_space=pltpu.SMEM)] + in_specs,
            out_specs=out_specs,
            scratch_shapes=scratch,
            input_output_aliases=aliases,
            compiler_params=pltpu.CompilerParams(vmem_limit_bytes=VMEM * 2**20),
            cost_estimate=pl.CostEstimate(flops=HEAVY, bytes_accessed=1, transcendentals=0),
            name=name,
        )(scalars, *args)

    act_one, stats_one, pack, params = call(
        begin_kernel,
        [
            sds((tokens, 128), BF),
            sds((8, 128), F32),
            sds((64, 640), BF),
            sds((16, 128), F32),
        ],
        scalars,
        x,
        norm_gains,
        norm_shifts,
        conv_biases,
        attn_biases,
        proj_bias.reshape(1, 64),
        qkv_weights,
        out_weight,
        proj_weight.T,
        scratch=[
            pltpu.VMEM((tokens, 128), BF),
            pltpu.VMEM((3, 128), F32),
            pltpu.VMEM((3, 128), F32),
            pltpu.VMEM((2, 128), F32),
            pltpu.VMEM((3, 128), F32),
            pltpu.VMEM((1, 64), F32),
            pltpu.VMEM((4, 64, 128), BF),
            pltpu.VMEM((64, C), BF),
            pltpu.VMEM((C, 64), F32),
            pltpu.SemaphoreType.DMA((11,)),
        ],
        flops=HEAVY,
        space=pl.ANY,
        vmem=60,
        name="begin",
    )
    pieces_one = [act_one] + flips(act_one)
    packs = [pack] + flips(pack)
    hot, quantized, usage, fixed = call(
        start_kernel,
        [
            sds((tokens, CODES), BF),
            sds((tokens, 64), F32),
            sds((8, 128), F32),
            sds((4, 64, 128), BF),
        ],
        scalars,
        codes,
        codebook.T,
        cotangent.reshape(tokens, 64),
        stats_one,
        scratch=[pltpu.VMEM((tokens, 64), F32)],
        name="start",
    )
    def conv_call(body, index, outs, name, *args):
        specs = []
        for a in args:
            if a is conv_w:
                specs.append(pl.BlockSpec((1, 9, C, 128), lambda i: (index, 0, 0, 0)))
            else:
                specs.append(whole(a.shape))
        scratch = ()
        if body is third_back_kernel:
            scratch = [pltpu.VMEM((tokens, 128), F32), pltpu.VMEM((tokens, 128), F32)]
        return blocks_call(
            body, specs, [whole(o.shape) for o in outs], outs, name, *args, scratch=scratch
        )

    hidden, stats_two, act_two = conv_call(
        conv_one_kernel,
        0,
        [sds((tokens, 128), F32), sds((8, 128), F32), sds((tokens, 128), BF)],
        "conv_one",
        *pieces_one,
        conv_w,
        params,
        usage,
    )
    pieces_two = [act_two] + flips(act_two)
    if by_hand:
        block = call(
            stack_kernel,
            [sds((4, 64, 640), BF)],
            scalars,
            *packs,
            flops=HEAVY,
            name="pack_join",
        )[0]
        blocks = [block] + [over("dp", block, k) for k in (2, 4, 6)]
    else:
        packed = jnp.concatenate(
            [qkv_weights[0], qkv_weights[1], qkv_weights[2], out_weight, proj_weight]
            + [jnp.zeros((C, 64), BF)],
            axis=1,
        )
        block = jnp.stack([packed] + flips(packed)).reshape(4, PARTS, 64, 640)
        block = jnp.swapaxes(block, 0, 1)
        block_own, block_other = block[0::2], block[1::2]
    normed_three, stats_three, *pays = conv_call(
        conv_two_kernel,
        1,
        [sds((tokens, 128), F32), sds((8, 128), F32)] + [sds((464, 128), BF)] * 4,
        "conv_two",
        *pieces_two,
        conv_w,
        params,
        x,
        fixed,
    )
    normed_pieces = [pays[0]] + [over("chan", pays[k], k) for k in (1, 2, 3)]
    if by_hand:
        block_own = call(
            stack_kernel,
            [sds((4, 4, 64, 640), BF)],
            scalars,
            *blocks,
            name="pack_plane",
        )[0]
        block_other = over("dp", block_own, 1)
    normed, residual_part, bias_rows = call(
        attn_in_kernel,
        [sds((POS, C), BF), sds((quarter, C), F32), sds((8, C), F32)],
        scalars,
        *normed_pieces,
        flops=HEAVY,
        name="attn_in",
    )
    attn_w = call(
        attn_weight_kernel,
        [sds((C, 2304), BF)],
        scalars,
        block_own,
        block_other,
        name="attn_weight",
    )[0]
    *pays, output, lat_grad, mixed, att_grad, qg, kg, vg, sums = call(
        attention_kernel,
        [sds((POS + 192, 128), F32)]
        + [sds((POS + 192, 128), BF)] * 3
        + [sds((quarter, C), BF)] * 5
        + [sds((POS, C), BF), sds((POS, C), BF), sds((8, C), F32)],
        scalars,
        normed,
        residual_part,
        bias_rows,
        *normed_pieces,
        attn_w,
        flops=HEAVY,
        name="attention",
    )

    back_three = [pays[0]] + [over("chan", pays[k], k) for k in (1, 2, 3)]
    *att_keep, att_send = call(
        attn_grad_kernel,
        [sds((4, 64, 640), BF)] * 4 + [sds((4, 4, 64, 640), BF)],
        scalars,
        normed,
        output,
        lat_grad,
        mixed,
        att_grad,
        qg,
        kg,
        vg,
        sums,
        usage,
        scratch=[pltpu.VMEM((C, 2560), BF)],
        name="attn_grad",
    )

    def pair_sum(keep, send, after, name):
        outs = [sds((2,) + keep[0].shape, BF)] * 2
        got = over("dp", send, 1)
        kept, sent = call(pair_add_kernel, outs, scalars, *keep, got, after, name=name)
        return kept, over("dp", sent, 2)

    if by_hand:
        att_kept, att_got = pair_sum(att_keep, att_send, back_three[1], "attn_pair")
    residual_grad, taps_two, latents, small_three, *pays = conv_call(
        third_back_kernel,
        1,
        [
            sds((tokens, 128), F32),
            sds((tokens, WIDE), BF),
            sds((tokens, 64), F32),
            sds((8, 128), F32),
            sds((tokens, 128), F32),
        ]
        + [sds((tokens, 128), BF)] * 3,
        "third_back",
        *back_three,
        normed_three,
        stats_three,
        params,
        att_kept if by_hand else sums,
        conv_w,
    )
    back_two = [pays[0]] + [over("chan", pays[k], k) for k in (1, 2, 3)]
    book_scale = 2.0 * CODES / tokens_all

    def two_grad(*refs):
        conv_two_grad_kernel(*refs[:10], book_scale, *refs[10:])

    *two_keep, two_send, commit = call(
        two_grad,
        [sds((64, 1408), BF)] * 4 + [sds((4, 64, 1408), BF), sds((8, 128), F32)],
        scalars,
        *pieces_two,
        taps_two,
        hot,
        latents,
        quantized,
        reset_src.reshape(1, CODES),
        scratch=[pltpu.VMEM((C, WIDE), BF), pltpu.VMEM((128, CODES), BF)],
        name="conv_two_grad",
    )
    if by_hand:
        att_own, att_sent = call(
            half_add_kernel,
            [sds((4, 64, 640), BF)] * 2,
            scalars,
            att_kept,
            att_got,
            small_three,
            flops=HEAVY,
            name="attn_half",
        )
        att_got = over("dp", att_sent, 4)
        two_kept, two_got = pair_sum(two_keep, two_send, att_own, "conv_two_pair")
    taps_one, small_two, *pays = conv_call(
        second_back_kernel,
        0,
        [sds((tokens, WIDE), BF), sds((8, 128), F32), sds((tokens, 128), F32)]
        + [sds((tokens, 128), BF)] * 3,
        "second_back",
        *back_two,
        hidden,
        stats_two,
        params,
        att_own if by_hand else sums,
        two_kept if by_hand else sums,
        conv_w,
    )
    back_one = [pays[0]] + [over("chan", pays[k], k) for k in (1, 2, 3)]
    *one_keep, one_send = call(
        conv_one_grad_kernel,
        [sds((64, WIDE), BF)] * 4 + [sds((4, 64, WIDE), BF)],
        scalars,
        *pieces_one,
        taps_one,
        scratch=[pltpu.VMEM((C, WIDE), BF)],
        name="conv_one_grad",
    )
    if by_hand:
        two_own, two_sent = call(
            half_add_kernel,
            [sds((64, 1408), BF)] * 2,
            scalars,
            two_kept,
            two_got,
            back_one[1],
            name="conv_two_half",
        )
        two_got = over("dp", two_sent, 4)
        att_kept, att_sent = call(
            attn_sum_kernel,
            [sds((2, 64, 640), BF)] * 2,
            scalars,
            att_own,
            att_got,
            back_one[1],
            name="attn_sum",
        )
        att_got = over("chan", att_sent, 1)
    grad_latents, small_one = call(
        first_back_kernel,
        [sds((tokens, 128), F32), sds((8, 128), F32)],
        scalars,
        *back_one,
        x,
        stats_one,
        params,
        residual_grad,
        one_keep[0],
        two_own if by_hand else sums,
        att_kept if by_hand else sums,
        flops=HEAVY,
        name="first_back",
    )

    if by_hand:
        o0, o1, o2, o3, two, att_own, att_sent = call(
            tail_first_kernel,
            [sds((64, WIDE), BF)] * 4 + [sds((64, 1408), BF)] + [sds((64, 640), BF)] * 2,
            scalars,
            *one_keep,
            over("dp", one_send, 1),
            two_own,
            two_got,
            att_kept,
            att_got,
            small_one,
            flops=HEAVY,
            name="tail_first",
        )
        last = call(
            last_kernel,
            [sds((64, 1920), BF)],
            scalars,
            o0,
            over("dp", o1, 2),
            over("dp", o2, 4),
            over("dp", o3, 6),
            att_own,
            over("chan", att_sent, 2),
            small_one,
            small_two,
            small_three,
            commit,
            flops=HEAVY,
            name="last",
        )[0]

        def chip(array, name, *after, flops=0):
            parts = plane(array)
            outs = [sds((4,) + array.shape, BF)]
            return call(stack_kernel, outs, scalars, *parts, *after, flops=flops, name=name)[0]

        two_own = chip(two, "stack_two", last, flops=HEAVY)
        two_other = over("dp", two_own, 1)
        last_own = chip(last, "stack_last", flops=HEAVY)
        last_other = over("dp", last_own, 1)
    else:

        def total(keep, send):
            parts = jnp.stack([jnp.stack(keep), send]).astype(F32)
            return lax.psum(parts, "dp").astype(BF)

        att_sum = total(att_keep, att_send)
        att_sum = add(att_sum[:, :, 0], *[over("chan", att_sum[:, :, k], k) for k in (1, 2, 3)])
        small = jnp.concatenate([small_one[0:2], small_two[0:3], small_three[0:3], commit[0:1]])
        small = jnp.concatenate([lax.psum(small, "dp"), jnp.zeros((7, 128), F32)])
        high = lax.reduce_precision(small, 8, 7)
        smalls = jnp.concatenate([high, small - high, jnp.zeros((32, 128), F32)]).astype(BF)
        smalls = jnp.zeros((2, 4, 64, 128), BF).at[0, 0].set(smalls)
        two_own, two_other = total(two_keep, two_send)
        one_sum = total(one_keep, one_send)
        last_own, last_other = jnp.concatenate([one_sum, att_sum, smalls], axis=3)

    conv_held, book_grad, picked = blocks_call(
        finish_two_kernel,
        [whole((4, 64, 1408)), whole((4, 64, 1408))],
        [
            pl.BlockSpec((1, 9, C, 128), lambda i: (1, 0, 0, 0)),
            whole((64, CODES)),
            whole((64, CODES)),
        ],
        [sds((2, 9, C, 128), F32), sds((64, CODES), F32), sds((64, CODES), F32)],
        "finish_two",
        two_own,
        two_other,
    )

    def finish_last(*refs):
        finish_last_kernel(float(tokens_all), *refs)

    outs = [
        sds((2, 9, C, 128), F32),
        sds((3, 128), F32),
        sds((3, 128), F32),
        sds((2, 128), F32),
        sds((1, 64), F32),
        sds((3, C, 128), F32),
        sds((C, 128), F32),
        sds((64, C), F32),
        sds((64, CODES), F32),
        sds((1, 1), F32),
        sds((3, 128), F32),
        sds((1, 64), F32),
    ]
    (
        conv_grad,
        gain_grad,
        shift_grad,
        conv_bias_grad,
        commitment,
        qkv_grad,
        out_grad,
        proj_grad,
        new_codebook,
        perplexity,
        attn_bias_grad,
        proj_bias_grad,
    ) = blocks_call(
        finish_last,
        [whole((4, 64, 1920)), whole((4, 64, 1920)), whole((64, CODES)), whole((64, CODES))]
        + [pl.BlockSpec(memory_space=pl.ANY)],
        [pl.BlockSpec((1, 9, C, 128), lambda i: (0, 0, 0, 0))] + [whole(o.shape) for o in outs[1:]],
        outs,
        "finish_last",
        last_own,
        last_other,
        picked,
        codebook.T,
        conv_held,
        scratch=[pltpu.VMEM((8, 128), F32), pltpu.VMEM((C, 128), F32)],
        aliases={5: 0},
    )

    return (
        latents.reshape(images, LAT, LAT, -1),
        commitment.reshape(64),
        perplexity.reshape(()),
        new_codebook.T,
        grad_latents.reshape(images, LAT, LAT, 128),
        gain_grad,
        shift_grad,
        conv_grad.reshape(2, 3, 3, C, 128),
        conv_bias_grad,
        qkv_grad,
        attn_bias_grad,
        out_grad,
        proj_grad.T,
        proj_bias_grad.reshape(64),
        book_grad.T,
    )


def solution(mesh):
    return jax.shard_map(
        shards,
        mesh=mesh,
        in_specs=(
            P("dp", None, None, "chan"),
            P(None, "chan"),
            P(None, "chan"),
            P(None, None, None, None, "chan"),
            P(None, "chan"),
            P(None, None, "chan"),
            P(None, "chan"),
            P(None, "chan"),
            P(None, "chan"),
            P("chan"),
            P(None, "chan"),
            P("dp", None, None),
            P(),
            P("dp", None, None, "chan"),
        ),
        out_specs=(
            P("dp", None, None, "chan"),
            P("chan"),
            P(),
            P(None, "chan"),
            P("dp", None, None, "chan"),
            P(None, "chan"),
            P(None, "chan"),
            P(None, None, None, None, "chan"),
            P(None, "chan"),
            P(None, None, "chan"),
            P(None, "chan"),
            P(None, "chan"),
            P(None, "chan"),
            P("chan"),
            P(None, "chan"),
        ),
        check_vma=False,
    )
```

```python
import jax
import jax.numpy as jnp
from jax import lax
from jax.experimental import pallas as pl
from jax.experimental.pallas import tpu as pltpu
from jax.sharding import PartitionSpec as P

F32 = jnp.float32
BF = jnp.bfloat16
C = 512
CODES = 1024
LAT = 16
POS = LAT * LAT
EPSILON = 1e-06
BETA = 0.25
SCORE_SCALE = float(C) ** (-0.5)
GROUP_COUNT = float(POS * 16)
WIDE = 1152
VMEM = 20
HEAVY = 10**11
PARTS = 8


def call(body, outs, *args, scratch=(), flops=0, name=None, space=pltpu.VMEM, vmem=VMEM):
    result = pl.pallas_call(
        body,
        out_shape=list(outs),
        in_specs=[pl.BlockSpec(memory_space=pltpu.SMEM)]
        + [pl.BlockSpec(memory_space=space)] * (len(args) - 1),
        out_specs=[pl.BlockSpec(memory_space=pltpu.VMEM)] * len(outs),
        scratch_shapes=list(scratch),
        compiler_params=pltpu.CompilerParams(vmem_limit_bytes=vmem * 2**20),
        cost_estimate=pl.CostEstimate(flops=flops, bytes_accessed=1, transcendentals=0),
        name=name,
    )(*args)
    return result


def sds(shape, dtype):
    return jax.ShapeDtypeStruct(shape, dtype)


def dot(a, b):
    return jnp.dot(a, b, preferred_element_type=F32)


def dot_nt(a, b):
    return lax.dot_general(a, b, (((1,), (1,)), ((), ())), preferred_element_type=F32)


def dot_tn(a, b):
    return lax.dot_general(a, b, (((0,), (0,)), ((), ())), preferred_element_type=F32)


def lanes(parts):
    return jnp.concatenate(parts, axis=1)


def rows_of(parts):
    return jnp.concatenate(parts, axis=0)


def pack_rows(vectors, height=8):
    width = vectors[0].shape[1]
    spot = lax.broadcasted_iota(jnp.int32, (height, width), 0)
    result = jnp.zeros((height, width), F32)
    for index, vector in enumerate(vectors):
        result = jnp.where(spot == index, vector, result)
    return result


def split_low(values):
    high = values.astype(BF).astype(F32)
    return high, values - high


def group_sums(rows):
    first = lax.broadcasted_iota(jnp.int32, (128, 128), 0) >> 4
    second = lax.broadcasted_iota(jnp.int32, (128, 128), 1) >> 4
    ones = (first == second).astype(F32).astype(BF)
    high, rest = split_low(rows)
    middle, low = split_low(rest)
    stacked = rows_of([high, middle, low, jnp.zeros_like(high)]).astype(BF)
    summed = dot(stacked, ones)
    return summed[0:8] + summed[8:16] + summed[16:24]


def col_sum(values):
    return jnp.sum(values, axis=0, keepdims=True)


def moments(values):
    one, two = values[:POS], values[POS:]
    mean = group_sums(pack_rows([col_sum(one), col_sum(two)])) * (1.0 / GROUP_COUNT)
    one, two = one - mean[0:1], two - mean[1:2]
    variance = group_sums(pack_rows([col_sum(one * one), col_sum(two * two)])) * (
        1.0 / GROUP_COUNT
    )
    inverse = lax.rsqrt(variance + EPSILON)
    deviation = jnp.sqrt(variance + EPSILON)
    normed = rows_of([one * inverse[0:1], two * inverse[1:2]])
    stats = pack_rows(
        [mean[0:1], mean[1:2], inverse[0:1], inverse[1:2], deviation[0:1], deviation[1:2]]
    )
    return normed, stats


def renormed(values, stats):
    return rows_of(
        [
            (values[:POS] - stats[0:1]) * stats[2:3],
            (values[POS:] - stats[1:2]) * stats[3:4],
        ]
    )


def norm_back(upstream, normed, stats, gain):
    sides = [(upstream[:POS], normed[:POS]), (upstream[POS:], normed[POS:])]
    plain = [col_sum(u) for u, _ in sides]
    weighted = [col_sum(u * n) for u, n in sides]
    means = group_sums(
        pack_rows([plain[0] * gain, plain[1] * gain, weighted[0] * gain, weighted[1] * gain])
    ) * (1.0 / GROUP_COUNT)
    parts = [
        stats[2 + m : 3 + m] * (u * gain - means[m : m + 1] - n * means[2 + m : 3 + m])
        for m, (u, n) in enumerate(sides)
    ]
    return rows_of(parts), weighted[0] + weighted[1], plain[0] + plain[1]


GAIN, SHIFT, CONV_BIAS, ATTN_BIAS, PROJ_BIAS = 0, 3, 6, 8, 11


def param(ref, index):
    return ref[index : index + 1]


def column_masks(height):
    column = lax.broadcasted_iota(jnp.int32, (height, 128), 0) & (LAT - 1)
    return column >= 1, column <= LAT - 2


def later_rows(values):
    blank = jnp.zeros((LAT, values.shape[1]), values.dtype)
    return rows_of([values[LAT:POS], blank, values[POS + LAT :], blank])


def earlier_rows(values):
    blank = jnp.zeros((LAT, values.shape[1]), values.dtype)
    return rows_of([blank, values[: POS - LAT], blank, values[POS : 2 * POS - LAT]])


def conv_forward(pieces, w_ref, z):
    full = lanes(pieces)
    height = full.shape[0]
    inner, outer = column_masks(height)
    blocks = [pl.ds(pl.multiple_of((z ^ k) * 128, 128), 128) for k in range(4)]
    weights = lanes(
        [rows_of([w_ref[0, tap, block, :] for block in blocks]) for tap in range(9)]
    )
    every = dot(full, weights)
    sums = []
    for col_tap in range(3):
        total = None
        for row_tap in range(3):
            tap = 3 * row_tap + col_tap
            part = every[:, 128 * tap : 128 * tap + 128]
            if row_tap == 0:
                part = earlier_rows(part)
            elif row_tap == 2:
                part = later_rows(part)
            total = part if total is None else total + part
        sums.append(total)
    left = jnp.where(inner, pltpu.roll(sums[0], 1, 0), 0.0)
    right = jnp.where(outer, pltpu.roll(sums[2], height - 1, 0), 0.0)
    return sums[1] + left + right


def spread_taps(gradient):
    height = gradient.shape[0]
    inner, outer = column_masks(height)
    by_column = [
        jnp.where(outer, pltpu.roll(gradient, height - 1, 0), 0.0),
        gradient,
        jnp.where(inner, pltpu.roll(gradient, 1, 0), 0.0),
    ]
    copies = [None] * 9
    for col_tap in range(3):
        copies[col_tap] = later_rows(by_column[col_tap])
        copies[3 + col_tap] = by_column[col_tap]
        copies[6 + col_tap] = earlier_rows(by_column[col_tap])
    return lanes([c.astype(BF) for c in copies])


def part_row(scalars, part):
    place = scalars[1] ^ part
    block = (place >> 1) ^ scalars[0]
    return place, pl.multiple_of(block * 128 + (place & 1) * 64, 64)


def fetch(pairs, sems):
    copies = [
        pltpu.make_async_copy(source, target, sems.at[i])
        for i, (source, target) in enumerate(pairs)
    ]
    for copy in copies:
        copy.start()
    for copy in copies:
        copy.wait()


def begin_kernel(
    scalars,
    x_any,
    gain_any,
    shift_any,
    conv_b_any,
    attn_b_any,
    proj_b_any,
    qkv_any,
    out_w_any,
    proj_any,
    act_ref,
    stats_ref,
    pack_ref,
    param_ref,
    x_ref,
    gain_ref,
    shift_ref,
    conv_b_ref,
    attn_b_ref,
    proj_b_ref,
    weights,
    proj_ref,
    proj,
    sems,
):
    own = pl.ds(pl.multiple_of(scalars[1] * 64, 64), 64)
    fetch(
        [
            (x_any, x_ref),
            (gain_any, gain_ref),
            (shift_any, shift_ref),
            (conv_b_any, conv_b_ref),
            (attn_b_any, attn_b_ref),
            (proj_b_any, proj_b_ref),
            (out_w_any.at[own, :], weights.at[3]),
            (proj_any, proj_ref),
        ]
        + [(qkv_any.at[m, own, :], weights.at[m]) for m in range(3)],
        sems,
    )
    normed, stats = moments(x_ref[...].astype(F32))
    pre = normed * gain_ref[0:1] + shift_ref[0:1]
    act_ref[...] = (pre * jax.nn.sigmoid(pre)).astype(BF)
    stats_ref[...] = stats
    for m in range(4):
        pack_ref[:, 128 * m : 128 * m + 128] = weights[m]
    proj[...] = jnp.transpose(proj_ref[...].astype(F32))
    pack_ref[:, 512:640] = lanes([proj[own, :], jnp.zeros((64, 64), F32)]).astype(BF)
    rows = [gain_ref[m : m + 1] for m in range(3)] + [shift_ref[m : m + 1] for m in range(3)]
    rows += [conv_b_ref[m : m + 1] for m in range(2)] + [attn_b_ref[m : m + 1] for m in range(3)]
    rows += [lanes([proj_b_ref[...], jnp.zeros_like(proj_b_ref[...])])]
    param_ref[...] = pack_rows(rows, 16)


def code_column(codes):
    grid = rows_of([codes[m] for m in range(codes.shape[0])])
    height = grid.shape[0] * LAT
    high = grid >> 5
    both = lanes([high.astype(F32), (grid - (high << 5)).astype(F32)]).astype(BF)
    lines = lax.broadcasted_iota(jnp.int32, (height, grid.shape[0]), 0) >> 4
    own = (lines == lax.broadcasted_iota(jnp.int32, lines.shape, 1)).astype(F32).astype(BF)
    spread = dot(own, both)
    column = lax.broadcasted_iota(jnp.int32, (height, LAT), 0) & (LAT - 1)
    here = column == lax.broadcasted_iota(jnp.int32, (height, LAT), 1)
    merged = 32.0 * spread[:, :LAT] + spread[:, LAT:]
    return jnp.sum(jnp.where(here, merged, 0.0), axis=1, keepdims=True).astype(jnp.int32)


def start_kernel(scalars, codes_ref, book_ref, cot_ref, _, hot_ref, quant_ref, usage_ref, fixed_ref, start):
    tokens = hot_ref.shape[0]
    hot32 = (
        code_column(codes_ref[...]) == lax.broadcasted_iota(jnp.int32, (tokens, CODES), 1)
    ).astype(F32)
    hot = hot32.astype(BF)
    hot_ref[...] = hot
    counts = col_sum(hot32)
    usage_ref[...] = pack_rows([counts[:, 128 * i : 128 * i + 128] for i in range(8)])
    high, rest = split_low(book_ref[...])
    middle, low = split_low(rest)
    picked = dot_nt(hot, rows_of([high, middle, low]).astype(BF))
    width = book_ref.shape[0]
    quantized = picked[:, :width] + picked[:, width : 2 * width] + picked[:, 2 * width :]
    quant_ref[...] = quantized
    start[...] = cot_ref[...].astype(F32) - 2.0 * BETA * quantized
    for k in range(4):
        row = (scalars[0] ^ k) * 128
        one = start[pl.ds(pl.multiple_of(row, 64), 64), :]
        two = start[pl.ds(pl.multiple_of(row + 64, 64), 64), :]
        fixed_ref[k] = lanes([one, two]).astype(BF)


def attn_weight_kernel(scalars, own_ref, other_ref, o_ref):
    for part in range(PARTS):
        source = (own_ref if part % 2 == 0 else other_ref).at[part // 2]
        _, row = part_row(scalars, part)
        spot = pl.ds(row, 64)
        for k in range(4):
            for m in range(4):
                o_ref[spot, 512 * m + 128 * k : 512 * m + 128 * k + 128] = source[
                    k, :, 128 * m : 128 * m + 128
                ]
        for pair in range(2):
            o_ref[spot, 2048 + 128 * pair : 2176 + 128 * pair] = lanes(
                [source[2 * pair + i, :, 512:576] for i in range(2)]
            )


def conv_one_kernel(
    scalars, a0, a1, a2, a3, w_ref, param_ref, _, hidden_ref, stats_ref, act_ref
):
    pieces = [a0[...], a1[...], a2[...], a3[...]]
    hidden = conv_forward(pieces, w_ref, scalars[0]) + param(param_ref, CONV_BIAS)
    hidden_ref[...] = hidden
    normed, stats = moments(hidden)
    stats_ref[...] = stats
    pre = normed * param(param_ref, GAIN + 1) + param(param_ref, SHIFT + 1)
    act_ref[...] = (pre * jax.nn.sigmoid(pre)).astype(BF)


def conv_two_kernel(
    scalars, a0, a1, a2, a3, w_ref, param_ref, x_ref, fixed_ref, normed_ref, stats_ref, *pay_refs
):
    residual = x_ref[...].astype(F32) + (
        conv_forward([a0[...], a1[...], a2[...], a3[...]], w_ref, scalars[0])
        + param(param_ref, CONV_BIAS + 1)
    )
    normed, stats = moments(residual)
    normed_ref[...] = normed
    stats_ref[...] = stats
    gain, shift = param(param_ref, GAIN + 2), param(param_ref, SHIFT + 2)
    for k, ref in enumerate(pay_refs):
        target = scalars[0] ^ k
        own, other = target * 128, (target ^ 1) * 128
        ref[0:128] = (
            normed_ref[pl.ds(pl.multiple_of(other, 128), 128), :] * gain + shift
        ).astype(BF)
        high, low = split_low(normed_ref[pl.ds(pl.multiple_of(own, 128), 128), :])
        ref[128:256] = high.astype(BF)
        ref[256:384] = low.astype(BF)
        is_two = jnp.broadcast_to(target >> 1, (1, 128)) == 1
        mean = jnp.where(is_two, stats[1:2], stats[0:1])
        deviation = jnp.where(is_two, stats[5:6], stats[4:5])
        rows = list(split_low(mean)) + list(split_low(deviation))
        for index in (GAIN + 2, SHIFT + 2, ATTN_BIAS, ATTN_BIAS + 1, ATTN_BIAS + 2, PROJ_BIAS):
            rows.extend(split_low(param(param_ref, index)))
        ref[384:400] = pack_rows(rows, 16).astype(BF)
        ref[400:464] = fixed_ref[k]


def attn_in_kernel(scalars, n0, n1, n2, n3, norm_ref, residual_ref, bias_ref):
    pieces = [n0, n1, n2, n3]
    tails = [n[384:400].astype(F32) for n in pieces]

    def vector(index, width=128):
        row = 2 * index
        return lanes([t[row : row + 1, :width] + t[row + 1 : row + 2, :width] for t in tails])

    mean, deviation, gain, shift = [vector(index) for index in range(4)]
    empty = jnp.zeros((1, 256), F32)
    bias_ref[...] = pack_rows([vector(4), vector(5), vector(6), lanes([vector(7, 64), empty])])
    own = lanes([n[128:256].astype(F32) + n[256:384].astype(F32) for n in pieces])
    residual_ref[...] = own * deviation + mean
    norm_ref[0:128] = (own * gain + shift).astype(BF)
    norm_ref[128:POS] = lanes([n[0:128] for n in pieces])


def attention_kernel(
    scalars, norm_ref, residual_ref, bias_ref, n0, n1, n2, n3, w_ref, *refs
):
    pay_refs = refs[:4]
    out_ref, lat_grad_ref, mixed_ref, att_grad_ref, qg_ref, kg_ref, vg_ref, sums_ref = refs[4:]
    query_bias, value_bias, out_bias = [bias_ref[m : m + 1] for m in range(3)]
    proj_bias = bias_ref[3:4, 0:256]
    pieces = [n0, n1, n2, n3]
    normed = norm_ref[...]
    query = (dot(norm_ref[0:128], w_ref[:, 0:512]) + query_bias).astype(BF)
    keys = dot(normed, w_ref[:, 512:1024]).astype(BF)
    values = (dot(normed, w_ref[:, 1024:1536]) + value_bias).astype(BF)
    scores = dot_nt(query, keys) * SCORE_SCALE
    weights = jnp.exp(scores - jnp.max(scores, axis=1, keepdims=True))
    probs = weights / jnp.sum(weights, axis=1, keepdims=True)
    probs_low = probs.astype(BF)
    mixed = dot(probs_low, values).astype(BF)
    mixed_ref[...] = mixed
    attended = dot(mixed, w_ref[:, 1536:2048]) + out_bias
    output = (residual_ref[...] + attended).astype(BF)
    out_ref[...] = output
    latents = dot(output, w_ref[:, 2048:2304]) + proj_bias
    fixed = []
    for n in pieces:
        both = n[400:464].astype(F32)
        fixed.append(rows_of([both[:, :64], both[:, 64:]]))
    lat_grad = (lanes(fixed) + 2.0 * BETA * latents).astype(BF)
    blank = jnp.zeros((128, 64), BF)
    for k in range(4):
        lat_grad_ref[:, 128 * k : 128 * k + 128] = lanes([lat_grad[:, 64 * k : 64 * k + 64], blank])
    out_grad = dot_nt(lat_grad, w_ref[:, 2048:2304])
    att_grad = out_grad.astype(BF)
    att_grad_ref[...] = att_grad
    mixed_grad = dot_nt(att_grad, w_ref[:, 1536:2048]).astype(BF)
    probs_grad = dot_nt(mixed_grad, values)
    row_dot = jnp.sum(probs * probs_grad, axis=1, keepdims=True)
    score_grad = (probs * (probs_grad - row_dot)).astype(BF)
    query_grad = (dot(score_grad, keys) * SCORE_SCALE).astype(BF)
    key_grad = (dot_tn(score_grad, query) * SCORE_SCALE).astype(BF)
    value_grad = dot_tn(probs_low, mixed_grad).astype(BF)
    qg_ref[...] = query_grad
    kg_ref[...] = key_grad
    vg_ref[...] = value_grad
    upstream = dot_nt(key_grad, w_ref[:, 512:1024]) + dot_nt(value_grad, w_ref[:, 1024:1536])
    upstream_own = upstream[:128] + dot_nt(query_grad, w_ref[:, 0:512])
    for k in range(4):
        ref = pay_refs[k]
        ref[0:128] = upstream_own[:, 128 * k : 128 * k + 128].astype(ref.dtype)
        ref[128:POS] = upstream[128:, 128 * k : 128 * k + 128].astype(ref.dtype)
        ref[POS : POS + 128] = out_grad[:, 128 * k : 128 * k + 128].astype(ref.dtype)
        piece = latents[:, 64 * k : 64 * k + 64]
        ref[POS + 128 : POS + 192] = lanes([piece[:64], piece[64:]]).astype(ref.dtype)
    sums_ref[...] = pack_rows(
        [
            col_sum(query_grad.astype(F32)),
            col_sum(value_grad.astype(F32)),
            col_sum(att_grad.astype(F32)),
            lanes(
                [
                    part
                    for k in range(4)
                    for part in (
                        col_sum(lat_grad[:, 64 * k : 64 * k + 64].astype(F32)),
                        jnp.zeros((1, 64), F32),
                    )
                ]
            ),
        ]
    )


def attn_grad_kernel(
    scalars,
    norm_ref,
    out_ref,
    lat_grad_ref,
    mixed_ref,
    att_grad_ref,
    qg_ref,
    kg_ref,
    vg_ref,
    sums_ref,
    usage_ref,
    *refs,
):
    keep_refs, send_ref, grads = refs[:4], refs[4], refs[5]
    grads[:, 0:512] = dot_tn(norm_ref[0:128], qg_ref[...]).astype(BF)
    grads[:, 512:1024] = dot_tn(norm_ref[...], kg_ref[...]).astype(BF)
    grads[:, 1024:1536] = dot_tn(norm_ref[...], vg_ref[...]).astype(BF)
    grads[:, 1536:2048] = dot_tn(mixed_ref[...], att_grad_ref[...]).astype(BF)
    grads[:, 2048:2560] = dot_tn(out_ref[...], lat_grad_ref[...]).astype(BF)
    right = lax.broadcasted_iota(jnp.int32, (16, 128), 1) >= 64

    def halves(vectors, offset):
        blank = jnp.zeros((1, 128), F32)
        entries = [blank] * offset
        for vector in vectors:
            entries += [pltpu.roll(vector, 64, 1), vector]
        return jnp.where(right, pack_rows(entries, 16), 0.0)

    biases = []
    for k in range(4):
        vectors = [sums_ref[m : m + 1, 128 * k : 128 * k + 128] for m in range(4)]
        biases.append(halves(vectors, 4))
    tens = jnp.floor(usage_ref[...] * (1.0 / 16.0))
    ones = usage_ref[...] - 16.0 * tens
    for part in range(PARTS):
        place, row = part_row(scalars, part)
        is_first = (jnp.broadcast_to(place, (16, 128)) == 0).astype(F32)
        here = jnp.broadcast_to(place, (8, 128)) == lax.broadcasted_iota(jnp.int32, (8, 128), 0)
        counts = [col_sum(jnp.where(here, digit, 0.0)) for digit in (tens, ones)]
        for k in range(4):
            ref = keep_refs[part // 2].at[k] if part % 2 == 0 else send_ref.at[part // 2, k]
            for m in range(4):
                ref[:, 128 * m : 128 * m + 128] = grads[
                    pl.ds(row, 64), 512 * m + 128 * k : 512 * m + 128 * k + 128
                ]
            extra = biases[k] * is_first
            if k == 0:
                extra = extra + halves(counts, 0)
            block = slice(2048 + 128 * k, 2176 + 128 * k)
            ref[0:16, 512:640] = (grads[pl.ds(row, 16), block].astype(F32) + extra).astype(BF)
            ref[16:64, 512:640] = grads[pl.ds(row + 16, 48), block]


def third_back_kernel(
    scalars,
    p0,
    p1,
    p2,
    p3,
    normed_ref,
    stats_ref,
    param_ref,
    _,
    w_ref,
    residual_ref,
    taps_ref,
    lat_ref,
    small_ref,
    q0,
    q1,
    q2,
    q3,
    up_ref,
    out_ref,
):
    z = scalars[0]
    for near, far, base in ((p0, p1, z), (p2, p3, z ^ 2)):
        first, second = near[0:POS].astype(F32), far[0:POS].astype(F32)
        up_ref[pl.ds(pl.multiple_of(base * 128, 128), 128), :] = first[:128] + second[128:]
        up_ref[pl.ds(pl.multiple_of((base ^ 1) * 128, 128), 128), :] = first[128:] + second[:128]
    for k, ref in enumerate((p0, p1, p2, p3)):
        row = (z ^ k) * 128
        out_ref[pl.ds(pl.multiple_of(row, 128), 128), :] = ref[POS : POS + 128].astype(F32)
        piece = ref[POS + 128 : POS + 192].astype(F32)
        lat_ref[pl.ds(pl.multiple_of(row, 64), 64), :] = piece[:, :64]
        lat_ref[pl.ds(pl.multiple_of(row + 64, 64), 64), :] = piece[:, 64:]
    source, gain_grad, shift_grad = norm_back(
        up_ref[...], normed_ref[...], stats_ref[...], param(param_ref, GAIN + 2)
    )
    residual = out_ref[...] + source
    residual_ref[...] = residual
    low = residual.astype(BF).astype(F32)
    small_ref[...] = pack_rows([gain_grad, shift_grad, col_sum(low)])
    send_taps(low, w_ref, scalars[0], taps_ref, (q0, q1, q2, q3))


def send_taps(gradient, w_ref, z, taps_ref, piece_refs):
    taps = spread_taps(gradient)
    taps_ref[...] = taps
    rows = []
    for k in range(4):
        block = pl.ds(pl.multiple_of((z ^ k) * 128, 128), 128)
        rows.append(lanes([w_ref[0, tap, block, :] for tap in range(9)]))
    every = dot_nt(taps, rows_of(rows))
    for k, ref in enumerate(piece_refs):
        ref[...] = every[:, 128 * k : 128 * k + 128].astype(ref.dtype)


def swish_back(gradient, normed, gain, shift):
    pre = normed * gain + shift
    gate = jax.nn.sigmoid(pre)
    return gradient * (gate * (1.0 + pre * (1.0 - gate)))


def second_back_kernel(
    scalars,
    p0,
    p1,
    p2,
    p3,
    hidden_ref,
    stats_ref,
    param_ref,
    _,
    __,
    w_ref,
    taps_ref,
    small_ref,
    q0,
    q1,
    q2,
    q3,
):
    gradient = p0[...] + p1[...].astype(F32) + p2[...].astype(F32) + p3[...].astype(F32)
    stats = stats_ref[...]
    normed = renormed(hidden_ref[...], stats)
    gain = param(param_ref, GAIN + 1)
    upstream = swish_back(gradient, normed, gain, param(param_ref, SHIFT + 1))
    source, gain_grad, shift_grad = norm_back(upstream, normed, stats, gain)
    low = source.astype(BF).astype(F32)
    small_ref[...] = pack_rows([gain_grad, shift_grad, col_sum(low)])
    send_taps(low, w_ref, scalars[0], taps_ref, (q0, q1, q2, q3))


def first_back_kernel(
    scalars,
    p0,
    p1,
    p2,
    p3,
    x_ref,
    stats_ref,
    param_ref,
    residual_ref,
    _,
    __,
    ___,
    grad_ref,
    small_ref,
):
    gradient = p0[...] + p1[...].astype(F32) + p2[...].astype(F32) + p3[...].astype(F32)
    stats = stats_ref[...]
    normed = renormed(x_ref[...].astype(F32), stats)
    gain = param(param_ref, GAIN)
    upstream = swish_back(gradient, normed, gain, param(param_ref, SHIFT))
    source, gain_grad, shift_grad = norm_back(upstream, normed, stats, gain)
    grad_ref[...] = residual_ref[...] + source
    small_ref[...] = pack_rows([gain_grad, shift_grad])


def conv_one_grad_kernel(scalars, a0, a1, a2, a3, taps_ref, *refs):
    keep_refs, send_ref, grads = refs[:4], refs[4], refs[5]
    full = lanes([a0[...], a1[...], a2[...], a3[...]])
    grads[...] = dot_tn(full, taps_ref[...]).astype(BF)
    for part in range(PARTS):
        _, row = part_row(scalars, part)
        value = grads[pl.ds(row, 64), :]
        if part % 2 == 0:
            keep_refs[part // 2][...] = value
        else:
            send_ref[part // 2] = value


def conv_two_grad_kernel(
    scalars, a0, a1, a2, a3, taps_ref, hot_ref, lat_ref, quant_ref, reset_ref, scale, *refs
):
    keep_refs, send_ref, commit_ref, grads, book = refs[:4], refs[4], refs[5], refs[6], refs[7]
    full = lanes([a0[...], a1[...], a2[...], a3[...]])
    grads[...] = dot_tn(full, taps_ref[...]).astype(BF)
    latents = lat_ref[...]
    difference = latents - quant_ref[...]
    commit_ref[...] = pack_rows([lanes([col_sum(difference * difference), jnp.zeros((1, 64), F32)])])
    high, low = split_low(difference * (-scale))
    sums = dot_tn(lanes([high, low]).astype(BF), hot_ref[...])
    tokens = latents.shape[0]
    where = reset_ref[...] - scalars[2] * tokens
    chosen = (where == lax.broadcasted_iota(jnp.int32, (tokens, CODES), 0)).astype(F32).astype(BF)
    picked = dot_tn(latents.astype(BF), chosen)
    book[0:64] = (sums[:64] + sums[64:]).astype(BF)
    book[64:128] = picked.astype(BF)
    for part in range(PARTS):
        place, row = part_row(scalars, part)
        ref = keep_refs[part // 2] if part % 2 == 0 else send_ref.at[part // 2]
        ref[:, 0:WIDE] = grads[pl.ds(row, 64), :]
        column = pl.ds(pl.multiple_of(place * 128, 128), 128)
        ref[:, WIDE : WIDE + 128] = book[0:64, column]
        ref[:, WIDE + 128 : WIDE + 256] = book[64:128, column]


def finish_two_kernel(scalars, own_ref, other_ref, conv_ref, book_grad_ref, picked_ref):
    for part in range(PARTS):
        source = (own_ref if part % 2 == 0 else other_ref).at[part // 2]
        place = scalars[1] ^ part
        rows = pl.ds(pl.multiple_of(place * 64, 64), 64)
        for tap in range(9):
            conv_ref[0, tap, rows, :] = source[:, 128 * tap : 128 * tap + 128].astype(F32)
        column = pl.ds(pl.multiple_of(place * 128, 128), 128)
        book_grad_ref[:, column] = source[:, WIDE : WIDE + 128].astype(F32)
        picked_ref[:, column] = source[:, WIDE + 128 : WIDE + 256].astype(F32)


def finish_last_kernel(
    tokens_all,
    scalars,
    own_ref,
    other_ref,
    picked,
    book_ref,
    held_ref,
    conv_ref,
    gain_ref,
    shift_ref,
    bias_ref,
    commit_ref,
    qkv_ref,
    out_w_ref,
    proj_ref,
    new_book_ref,
    perplexity_ref,
    attn_bias_ref,
    proj_bias_ref,
    usage,
    proj,
):
    extra_sum = jnp.zeros((16, 128), F32)
    total = jnp.zeros((9, 128), F32)
    for part in range(PARTS):
        source = (own_ref if part % 2 == 0 else other_ref).at[part // 2]
        place = scalars[1] ^ part
        rows = pl.ds(pl.multiple_of(place * 64, 64), 64)
        for tap in range(9):
            conv_ref[0, tap, rows, :] = source[:, 128 * tap : 128 * tap + 128].astype(F32)
        for m in range(3):
            qkv_ref[m, rows, :] = source[:, 1152 + 128 * m : 1280 + 128 * m].astype(F32)
        out_w_ref[rows, :] = source[:, 1536:1664].astype(F32)
        proj[rows, :] = source[:, 1664:1792].astype(F32)
        extra = source[0:16, 1664:1792].astype(F32)
        extra_sum = extra_sum + extra
        usage[pl.ds(place, 1), :] = lanes(
            [
                16.0 * extra[0:1, 64:] + extra[2:3, 64:],
                16.0 * extra[1:2, 64:] + extra[3:4, 64:],
            ]
        )
        both = source[16:64, 1728:1792].astype(F32)
        both = both[0:18] + both[18:36]
        total = total + lanes([both[0:9], both[9:18]])
    for index, row in enumerate((0, 2, 5)):
        gain_ref[index : index + 1] = total[row : row + 1]
        shift_ref[index : index + 1] = total[row + 1 : row + 2]
    bias_ref[0:1] = total[4:5]
    bias_ref[1:2] = total[7:8]
    commit_ref[...] = total[8:9, :64] * (1.0 / tokens_all)
    proj_ref[...] = jnp.transpose(proj[...])[0:64]
    counts = usage[...]
    share = counts * (1.0 / tokens_all)
    terms = share * jnp.log(jnp.maximum(share, 1.0 / tokens_all))
    entropy = jnp.sum(jnp.sum(terms, axis=1, keepdims=True), axis=0, keepdims=True)
    perplexity_ref[...] = jnp.exp(-entropy)
    for block in range(8):
        spot = slice(128 * block, 128 * block + 128)
        new_book_ref[:, spot] = jnp.where(
            counts[block : block + 1] > 0.5, book_ref[:, spot], picked[:, spot]
        )
    for m in range(3):
        attn_bias_ref[m : m + 1] = lanes(
            [extra_sum[4 + 2 * m : 5 + 2 * m, 64:], extra_sum[5 + 2 * m : 6 + 2 * m, 64:]]
        )
    proj_bias_ref[...] = extra_sum[10:11, 64:]


def pair_add_kernel(scalars, k0, k1, k2, k3, get_ref, _, keep_ref, send_ref):
    for i, ref in enumerate((k0, k1, k2, k3)):
        target = (send_ref if i % 2 else keep_ref).at[i // 2]
        target[...] = plus(ref[...], get_ref[i])


def plus(first, second):
    return (first.astype(F32) + second.astype(F32)).astype(BF)


def half_add_kernel(scalars, keep_ref, get_ref, _, own_ref, send_ref):
    own_ref[...] = plus(keep_ref[0], get_ref[0])
    send_ref[...] = plus(keep_ref[1], get_ref[1])


def attn_sum_kernel(scalars, a0, a1, _, keep_ref, send_ref):
    for k in range(4):
        (send_ref if k % 2 else keep_ref)[k // 2] = plus(a0[k], a1[k])


def pass_kernel(scalars, a0, a1, a2, _, b0, b1, b2):
    for source, target in ((a0, b0), (a1, b1), (a2, b2)):
        target[...] = source[...]


def add_kernel(scalars, k0, k1, k2, k3, get_ref, _, *sum_refs):
    for i, ref in enumerate((k0, k1, k2, k3)):
        sum_refs[i][...] = plus(ref[...], get_ref[i])


def two_sum_kernel(scalars, a0, a1, _, sum_ref):
    sum_ref[...] = plus(a0[...], a1[...])


def last_kernel(
    scalars, o0, o1, o2, o3, att_own, att_get, small_one, small_two, small_three, commit, last_ref
):
    total = o0[...].astype(F32)
    for ref in (o1, o2, o3):
        total = total + ref[...].astype(F32)
    last_ref[:, 0:WIDE] = total.astype(BF)
    last_ref[:, 1152:1664] = plus(att_own[:, 0:512], att_get[:, 0:512])
    rows = [small_one[0:1], small_one[1:2]]
    rows += [small_two[m : m + 1] for m in range(3)]
    rows += [small_three[m : m + 1] for m in range(3)]
    rows += [commit[0:1]]
    high, low = split_low(pack_rows(rows, 16))
    blank = jnp.zeros((48, 64), F32)
    small = rows_of([high[:9, :64], high[:9, 64:], low[:9, :64], low[:9, 64:], jnp.zeros((12, 64), F32)])
    small = lanes([blank, small])
    block = att_own[:, 512:640].astype(F32) + att_get[:, 512:640].astype(F32)
    last_ref[0:16, 1664:1792] = block[0:16].astype(BF)
    last_ref[16:64, 1664:1792] = (block[16:64] + small).astype(BF)


def stack_kernel(scalars, *refs):
    out_ref = refs[-1]
    for k in range(out_ref.shape[0]):
        out_ref[k] = refs[k][...]


def over(axis, array, flip):
    size = lax.axis_size(axis)
    return lax.ppermute(array, axis, [(i, i ^ flip) for i in range(size)])


def flips(array):
    return [over("chan", array, k) for k in (1, 2, 3)]


def plane(array):
    return [array] + [over("dp", array, k) for k in (2, 4, 6)]


def add(*arrays):
    total = arrays[0].astype(F32)
    for array in arrays[1:]:
        total = total + array.astype(F32)
    return total.astype(BF)


def shards(
    latents_in,
    norm_gains,
    norm_shifts,
    conv_weights,
    conv_biases,
    qkv_weights,
    attn_biases,
    out_weight,
    proj_weight,
    proj_bias,
    codebook,
    codes,
    reset_src,
    cotangent,
):
    images = latents_in.shape[0]
    tokens = images * POS
    quarter = tokens // 4
    devices = lax.axis_size("dp")
    tokens_all = tokens * devices
    by_hand = devices == PARTS
    z = lax.axis_index("chan").astype(jnp.int32)
    dp = lax.axis_index("dp").astype(jnp.int32)
    scalars = jnp.stack([z, dp if by_hand else jnp.zeros_like(dp), dp, jnp.zeros_like(dp)])
    x = latents_in.reshape(tokens, 128)
    conv_w = conv_weights.reshape(2, 9, C, 128)

    def whole(shape):
        return pl.BlockSpec(shape, lambda i, n=len(shape): (0,) * n)

    def blocks_call(body, in_specs, out_specs, outs, name, *args, scratch=(), aliases={}):
        return pl.pallas_call(
            body,
            grid=(1,),
            out_shape=outs,
            in_specs=[pl.BlockSpec(memory_space=pltpu.SMEM)] + in_specs,
            out_specs=out_specs,
            scratch_shapes=scratch,
            input_output_aliases=aliases,
            compiler_params=pltpu.CompilerParams(vmem_limit_bytes=VMEM * 2**20),
            cost_estimate=pl.CostEstimate(flops=HEAVY, bytes_accessed=1, transcendentals=0),
            name=name,
        )(scalars, *args)

    act_one, stats_one, pack, params = call(
        begin_kernel,
        [
            sds((tokens, 128), BF),
            sds((8, 128), F32),
            sds((64, 640), BF),
            sds((16, 128), F32),
        ],
        scalars,
        x,
        norm_gains,
        norm_shifts,
        conv_biases,
        attn_biases,
        proj_bias.reshape(1, 64),
        qkv_weights,
        out_weight,
        proj_weight.T,
        scratch=[
            pltpu.VMEM((tokens, 128), BF),
            pltpu.VMEM((3, 128), F32),
            pltpu.VMEM((3, 128), F32),
            pltpu.VMEM((2, 128), F32),
            pltpu.VMEM((3, 128), F32),
            pltpu.VMEM((1, 64), F32),
            pltpu.VMEM((4, 64, 128), BF),
            pltpu.VMEM((64, C), BF),
            pltpu.VMEM((C, 64), F32),
            pltpu.SemaphoreType.DMA((11,)),
        ],
        flops=HEAVY,
        space=pl.ANY,
        vmem=60,
        name="begin",
    )
    pieces_one = [act_one] + flips(act_one)
    packs = [pack] + flips(pack)
    hot, quantized, usage, fixed = call(
        start_kernel,
        [
            sds((tokens, CODES), BF),
            sds((tokens, 64), F32),
            sds((8, 128), F32),
            sds((4, 64, 128), BF),
        ],
        scalars,
        codes,
        codebook.T,
        cotangent.reshape(tokens, 64),
        stats_one,
        scratch=[pltpu.VMEM((tokens, 64), F32)],
        name="start",
    )
    def conv_call(body, index, outs, name, *args):
        specs = []
        for a in args:
            if a is conv_w:
                specs.append(pl.BlockSpec((1, 9, C, 128), lambda i: (index, 0, 0, 0)))
            else:
                specs.append(whole(a.shape))
        scratch = ()
        if body is third_back_kernel:
            scratch = [pltpu.VMEM((tokens, 128), F32), pltpu.VMEM((tokens, 128), F32)]
        return blocks_call(
            body, specs, [whole(o.shape) for o in outs], outs, name, *args, scratch=scratch
        )

    hidden, stats_two, act_two = conv_call(
        conv_one_kernel,
        0,
        [sds((tokens, 128), F32), sds((8, 128), F32), sds((tokens, 128), BF)],
        "conv_one",
        *pieces_one,
        conv_w,
        params,
        usage,
    )
    pieces_two = [act_two] + flips(act_two)
    if by_hand:
        block = call(
            stack_kernel,
            [sds((4, 64, 640), BF)],
            scalars,
            *packs,
            flops=HEAVY,
            name="pack_join",
        )[0]
        blocks = [block] + [over("dp", block, k) for k in (2, 4, 6)]
    else:
        packed = jnp.concatenate(
            [qkv_weights[0], qkv_weights[1], qkv_weights[2], out_weight, proj_weight]
            + [jnp.zeros((C, 64), BF)],
            axis=1,
        )
        block = jnp.stack([packed] + flips(packed)).reshape(4, PARTS, 64, 640)
        block = jnp.swapaxes(block, 0, 1)
        block_own, block_other = block[0::2], block[1::2]
    normed_three, stats_three, *pays = conv_call(
        conv_two_kernel,
        1,
        [sds((tokens, 128), F32), sds((8, 128), F32)] + [sds((464, 128), BF)] * 4,
        "conv_two",
        *pieces_two,
        conv_w,
        params,
        x,
        fixed,
    )
    normed_pieces = [pays[0]] + [over("chan", pays[k], k) for k in (1, 2, 3)]
    if by_hand:
        block_own = call(
            stack_kernel,
            [sds((4, 4, 64, 640), BF)],
            scalars,
            *blocks,
            name="pack_plane",
        )[0]
        block_other = over("dp", block_own, 1)
    normed, residual_part, bias_rows = call(
        attn_in_kernel,
        [sds((POS, C), BF), sds((quarter, C), F32), sds((8, C), F32)],
        scalars,
        *normed_pieces,
        flops=HEAVY,
        name="attn_in",
    )
    attn_w = call(
        attn_weight_kernel,
        [sds((C, 2304), BF)],
        scalars,
        block_own,
        block_other,
        name="attn_weight",
    )[0]
    *pays, output, lat_grad, mixed, att_grad, qg, kg, vg, sums = call(
        attention_kernel,
        [sds((POS + 192, 128), F32)]
        + [sds((POS + 192, 128), BF)] * 3
        + [sds((quarter, C), BF)] * 5
        + [sds((POS, C), BF), sds((POS, C), BF), sds((8, C), F32)],
        scalars,
        normed,
        residual_part,
        bias_rows,
        *normed_pieces,
        attn_w,
        flops=HEAVY,
        name="attention",
    )

    back_three = [pays[0]] + [over("chan", pays[k], k) for k in (1, 2, 3)]
    *att_keep, att_send = call(
        attn_grad_kernel,
        [sds((4, 64, 640), BF)] * 4 + [sds((4, 4, 64, 640), BF)],
        scalars,
        normed,
        output,
        lat_grad,
        mixed,
        att_grad,
        qg,
        kg,
        vg,
        sums,
        usage,
        scratch=[pltpu.VMEM((C, 2560), BF)],
        name="attn_grad",
    )

    def pair_sum(keep, send, after, name):
        outs = [sds((2,) + keep[0].shape, BF)] * 2
        got = over("dp", send, 1)
        kept, sent = call(pair_add_kernel, outs, scalars, *keep, got, after, name=name)
        return kept, over("dp", sent, 2)

    if by_hand:
        att_kept, att_got = pair_sum(att_keep, att_send, back_three[1], "attn_pair")
    residual_grad, taps_two, latents, small_three, *pays = conv_call(
        third_back_kernel,
        1,
        [
            sds((tokens, 128), F32),
            sds((tokens, WIDE), BF),
            sds((tokens, 64), F32),
            sds((8, 128), F32),
            sds((tokens, 128), F32),
        ]
        + [sds((tokens, 128), BF)] * 3,
        "third_back",
        *back_three,
        normed_three,
        stats_three,
        params,
        att_kept if by_hand else sums,
        conv_w,
    )
    back_two = [pays[0]] + [over("chan", pays[k], k) for k in (1, 2, 3)]
    book_scale = 2.0 * CODES / tokens_all

    def two_grad(*refs):
        conv_two_grad_kernel(*refs[:10], book_scale, *refs[10:])

    *two_keep, two_send, commit = call(
        two_grad,
        [sds((64, 1408), BF)] * 4 + [sds((4, 64, 1408), BF), sds((8, 128), F32)],
        scalars,
        *pieces_two,
        taps_two,
        hot,
        latents,
        quantized,
        reset_src.reshape(1, CODES),
        scratch=[pltpu.VMEM((C, WIDE), BF), pltpu.VMEM((128, CODES), BF)],
        name="conv_two_grad",
    )
    if by_hand:
        att_own, att_sent = call(
            half_add_kernel,
            [sds((4, 64, 640), BF)] * 2,
            scalars,
            att_kept,
            att_got,
            small_three,
            flops=HEAVY,
            name="attn_half",
        )
        att_got = over("dp", att_sent, 4)
        two_kept, two_got = pair_sum(two_keep, two_send, att_own, "conv_two_pair")
    taps_one, small_two, *pays = conv_call(
        second_back_kernel,
        0,
        [sds((tokens, WIDE), BF), sds((8, 128), F32), sds((tokens, 128), F32)]
        + [sds((tokens, 128), BF)] * 3,
        "second_back",
        *back_two,
        hidden,
        stats_two,
        params,
        att_own if by_hand else sums,
        two_kept if by_hand else sums,
        conv_w,
    )
    *one_keep, one_send = call(
        conv_one_grad_kernel,
        [sds((64, WIDE), BF)] * 4 + [sds((4, 64, WIDE), BF)],
        scalars,
        *pieces_one,
        taps_one,
        scratch=[pltpu.VMEM((C, WIDE), BF)],
        name="conv_one_grad",
    )
    one_got = over("dp", one_send, 1) if by_hand else one_send
    pays[1:] = call(
        pass_kernel,
        [sds((tokens, 128), BF)] * 3,
        scalars,
        *pays[1:],
        one_keep[0],
        flops=HEAVY,
        name="pass_on",
    )
    back_one = [pays[0]] + [over("chan", pays[k], k) for k in (1, 2, 3)]
    if by_hand:
        att_kept, att_sent = call(
            attn_sum_kernel,
            [sds((2, 64, 640), BF)] * 2,
            scalars,
            att_own,
            att_got,
            small_two,
            name="attn_sum",
        )
        att_got = over("chan", att_sent, 1)
        two_own, two_sent = call(
            half_add_kernel,
            [sds((64, 1408), BF)] * 2,
            scalars,
            two_kept,
            two_got,
            att_kept,
            name="conv_two_half",
        )
        two_got = over("dp", two_sent, 4)
        one_parts = call(
            add_kernel,
            [sds((64, WIDE), BF)] * 4,
            scalars,
            *one_keep,
            one_got,
            att_kept,
            name="conv_one_add",
        )
        one_parts = [one_parts[0]] + [over("dp", one_parts[i], 2 * i) for i in (1, 2, 3)]
        att_own, att_sent = call(
            half_add_kernel,
            [sds((64, 640), BF)] * 2,
            scalars,
            att_kept,
            att_got,
            two_own,
            name="attn_last",
        )
        att_got = over("chan", att_sent, 2)
    grad_latents, small_one = call(
        first_back_kernel,
        [sds((tokens, 128), F32), sds((8, 128), F32)],
        scalars,
        *back_one,
        x,
        stats_one,
        params,
        residual_grad,
        one_parts[0] if by_hand else sums,
        two_own if by_hand else sums,
        att_own if by_hand else sums,
        flops=HEAVY,
        name="first_back",
    )

    if by_hand:
        two = call(
            two_sum_kernel,
            [sds((64, 1408), BF)],
            scalars,
            two_own,
            two_got,
            small_one,
            name="conv_two_sum",
        )[0]
        last = call(
            last_kernel,
            [sds((64, 1792), BF)],
            scalars,
            *one_parts,
            att_own,
            att_got,
            small_one,
            small_two,
            small_three,
            commit,
            flops=HEAVY,
            name="last",
        )[0]

        def chip(array, name, *after, flops=0):
            parts = plane(array)
            outs = [sds((4,) + array.shape, BF)]
            return call(stack_kernel, outs, scalars, *parts, *after, flops=flops, name=name)[0]

        two_own = chip(two, "stack_two", last, flops=HEAVY)
        two_other = over("dp", two_own, 1)
        last_own = chip(last, "stack_last", flops=HEAVY)
        last_other = over("dp", last_own, 1)
    else:

        def total(keep, send):
            parts = jnp.stack([jnp.stack(keep), send]).astype(F32)
            return lax.psum(parts, "dp").astype(BF)

        att_sum = total(att_keep, att_send)
        att_sum = add(att_sum[:, :, 0], *[over("chan", att_sum[:, :, k], k) for k in (1, 2, 3)])
        small = jnp.concatenate([small_one[0:2], small_two[0:3], small_three[0:3], commit[0:1]])
        small = jnp.concatenate([lax.psum(small, "dp"), jnp.zeros((7, 128), F32)])
        high = lax.reduce_precision(small, 8, 7)
        halves = [v[:9, c : c + 64] for v in (high, small - high) for c in (0, 64)]
        smalls = jnp.concatenate(halves + [jnp.zeros((12, 64), F32)]).astype(BF)
        att_sum = att_sum.at[0, 0, 16:64, 576:640].add(smalls)
        two_own, two_other = total(two_keep, two_send)
        one_sum = total(one_keep, one_send)
        last_own, last_other = jnp.concatenate([one_sum, att_sum], axis=3)

    conv_held, book_grad, picked = blocks_call(
        finish_two_kernel,
        [whole((4, 64, 1408)), whole((4, 64, 1408))],
        [
            pl.BlockSpec((1, 9, C, 128), lambda i: (1, 0, 0, 0)),
            whole((64, CODES)),
            whole((64, CODES)),
        ],
        [sds((2, 9, C, 128), F32), sds((64, CODES), F32), sds((64, CODES), F32)],
        "finish_two",
        two_own,
        two_other,
    )

    def finish_last(*refs):
        finish_last_kernel(float(tokens_all), *refs)

    outs = [
        sds((2, 9, C, 128), F32),
        sds((3, 128), F32),
        sds((3, 128), F32),
        sds((2, 128), F32),
        sds((1, 64), F32),
        sds((3, C, 128), F32),
        sds((C, 128), F32),
        sds((64, C), F32),
        sds((64, CODES), F32),
        sds((1, 1), F32),
        sds((3, 128), F32),
        sds((1, 64), F32),
    ]
    (
        conv_grad,
        gain_grad,
        shift_grad,
        conv_bias_grad,
        commitment,
        qkv_grad,
        out_grad,
        proj_grad,
        new_codebook,
        perplexity,
        attn_bias_grad,
        proj_bias_grad,
    ) = blocks_call(
        finish_last,
        [whole((4, 64, 1792)), whole((4, 64, 1792)), whole((64, CODES)), whole((64, CODES))]
        + [pl.BlockSpec(memory_space=pl.ANY)],
        [pl.BlockSpec((1, 9, C, 128), lambda i: (0, 0, 0, 0))] + [whole(o.shape) for o in outs[1:]],
        outs,
        "finish_last",
        last_own,
        last_other,
        picked,
        codebook.T,
        conv_held,
        scratch=[pltpu.VMEM((8, 128), F32), pltpu.VMEM((C, 128), F32)],
        aliases={5: 0},
    )

    return (
        latents.reshape(images, LAT, LAT, -1),
        commitment.reshape(64),
        perplexity.reshape(()),
        new_codebook.T,
        grad_latents.reshape(images, LAT, LAT, 128),
        gain_grad,
        shift_grad,
        conv_grad.reshape(2, 3, 3, C, 128),
        conv_bias_grad,
        qkv_grad,
        attn_bias_grad,
        out_grad,
        proj_grad.T,
        proj_bias_grad.reshape(64),
        book_grad.T,
    )


def solution(mesh):
    return jax.shard_map(
        shards,
        mesh=mesh,
        in_specs=(
            P("dp", None, None, "chan"),
            P(None, "chan"),
            P(None, "chan"),
            P(None, None, None, None, "chan"),
            P(None, "chan"),
            P(None, None, "chan"),
            P(None, "chan"),
            P(None, "chan"),
            P(None, "chan"),
            P("chan"),
            P(None, "chan"),
            P("dp", None, None),
            P(),
            P("dp", None, None, "chan"),
        ),
        out_specs=(
            P("dp", None, None, "chan"),
            P("chan"),
            P(),
            P(None, "chan"),
            P("dp", None, None, "chan"),
            P(None, "chan"),
            P(None, "chan"),
            P(None, None, None, None, "chan"),
            P(None, "chan"),
            P(None, None, "chan"),
            P(None, "chan"),
            P(None, "chan"),
            P(None, "chan"),
            P("chan"),
            P(None, "chan"),
        ),
        check_vma=False,
    )
```

```python
import jax
import jax.numpy as jnp
from jax import lax
from jax.experimental import pallas as pl
from jax.experimental.pallas import tpu as pltpu
from jax.sharding import PartitionSpec as P

F32 = jnp.float32
BF = jnp.bfloat16
C = 512
CODES = 1024
LAT = 16
POS = LAT * LAT
EPSILON = 1e-06
BETA = 0.25
SCORE_SCALE = float(C) ** (-0.5)
GROUP_COUNT = float(POS * 16)
WIDE = 1152
VMEM = 20
HEAVY = 10**11
PARTS = 8


def call(body, outs, *args, scratch=(), flops=0, name=None, space=pltpu.VMEM, vmem=VMEM):
    result = pl.pallas_call(
        body,
        out_shape=list(outs),
        in_specs=[pl.BlockSpec(memory_space=pltpu.SMEM)]
        + [pl.BlockSpec(memory_space=space)] * (len(args) - 1),
        out_specs=[pl.BlockSpec(memory_space=pltpu.VMEM)] * len(outs),
        scratch_shapes=list(scratch),
        compiler_params=pltpu.CompilerParams(vmem_limit_bytes=vmem * 2**20),
        cost_estimate=pl.CostEstimate(flops=flops, bytes_accessed=1, transcendentals=0),
        name=name,
    )(*args)
    return result


def sds(shape, dtype):
    return jax.ShapeDtypeStruct(shape, dtype)


def dot(a, b):
    return jnp.dot(a, b, preferred_element_type=F32)


def dot_nt(a, b):
    return lax.dot_general(a, b, (((1,), (1,)), ((), ())), preferred_element_type=F32)


def dot_tn(a, b):
    return lax.dot_general(a, b, (((0,), (0,)), ((), ())), preferred_element_type=F32)


def lanes(parts):
    return jnp.concatenate(parts, axis=1)


def rows_of(parts):
    return jnp.concatenate(parts, axis=0)


def pack_rows(vectors, height=8):
    width = vectors[0].shape[1]
    spot = lax.broadcasted_iota(jnp.int32, (height, width), 0)
    result = jnp.zeros((height, width), F32)
    for index, vector in enumerate(vectors):
        result = jnp.where(spot == index, vector, result)
    return result


def split_low(values):
    high = values.astype(BF).astype(F32)
    return high, values - high


def group_sums(rows):
    first = lax.broadcasted_iota(jnp.int32, (128, 128), 0) >> 4
    second = lax.broadcasted_iota(jnp.int32, (128, 128), 1) >> 4
    ones = (first == second).astype(F32).astype(BF)
    high, rest = split_low(rows)
    middle, low = split_low(rest)
    stacked = rows_of([high, middle, low, jnp.zeros_like(high)]).astype(BF)
    summed = dot(stacked, ones)
    return summed[0:8] + summed[8:16] + summed[16:24]


def col_sum(values):
    return jnp.sum(values, axis=0, keepdims=True)


def moments(values):
    one, two = values[:POS], values[POS:]
    mean = group_sums(pack_rows([col_sum(one), col_sum(two)])) * (1.0 / GROUP_COUNT)
    one, two = one - mean[0:1], two - mean[1:2]
    variance = group_sums(pack_rows([col_sum(one * one), col_sum(two * two)])) * (
        1.0 / GROUP_COUNT
    )
    inverse = lax.rsqrt(variance + EPSILON)
    deviation = jnp.sqrt(variance + EPSILON)
    normed = rows_of([one * inverse[0:1], two * inverse[1:2]])
    stats = pack_rows(
        [mean[0:1], mean[1:2], inverse[0:1], inverse[1:2], deviation[0:1], deviation[1:2]]
    )
    return normed, stats


def renormed(values, stats):
    return rows_of(
        [
            (values[:POS] - stats[0:1]) * stats[2:3],
            (values[POS:] - stats[1:2]) * stats[3:4],
        ]
    )


def norm_back(upstream, normed, stats, gain):
    sides = [(upstream[:POS], normed[:POS]), (upstream[POS:], normed[POS:])]
    plain = [col_sum(u) for u, _ in sides]
    weighted = [col_sum(u * n) for u, n in sides]
    means = group_sums(
        pack_rows([plain[0] * gain, plain[1] * gain, weighted[0] * gain, weighted[1] * gain])
    ) * (1.0 / GROUP_COUNT)
    parts = [
        stats[2 + m : 3 + m] * (u * gain - means[m : m + 1] - n * means[2 + m : 3 + m])
        for m, (u, n) in enumerate(sides)
    ]
    return rows_of(parts), weighted[0] + weighted[1], plain[0] + plain[1]


GAIN, SHIFT, CONV_BIAS, ATTN_BIAS, PROJ_BIAS = 0, 3, 6, 8, 11


def param(ref, index):
    return ref[index : index + 1]


def column_masks(height):
    column = lax.broadcasted_iota(jnp.int32, (height, 128), 0) & (LAT - 1)
    return column >= 1, column <= LAT - 2


def later_rows(values):
    blank = jnp.zeros((LAT, values.shape[1]), values.dtype)
    return rows_of([values[LAT:POS], blank, values[POS + LAT :], blank])


def earlier_rows(values):
    blank = jnp.zeros((LAT, values.shape[1]), values.dtype)
    return rows_of([blank, values[: POS - LAT], blank, values[POS : 2 * POS - LAT]])


def conv_forward(pieces, w_ref, z):
    full = lanes(pieces)
    height = full.shape[0]
    inner, outer = column_masks(height)
    blocks = [pl.ds(pl.multiple_of((z ^ k) * 128, 128), 128) for k in range(4)]
    weights = lanes(
        [rows_of([w_ref[0, tap, block, :] for block in blocks]) for tap in range(9)]
    )
    every = dot(full, weights)
    sums = []
    for col_tap in range(3):
        total = None
        for row_tap in range(3):
            tap = 3 * row_tap + col_tap
            part = every[:, 128 * tap : 128 * tap + 128]
            if row_tap == 0:
                part = earlier_rows(part)
            elif row_tap == 2:
                part = later_rows(part)
            total = part if total is None else total + part
        sums.append(total)
    left = jnp.where(inner, pltpu.roll(sums[0], 1, 0), 0.0)
    right = jnp.where(outer, pltpu.roll(sums[2], height - 1, 0), 0.0)
    return sums[1] + left + right


def spread_taps(gradient):
    height = gradient.shape[0]
    inner, outer = column_masks(height)
    by_column = [
        jnp.where(outer, pltpu.roll(gradient, height - 1, 0), 0.0),
        gradient,
        jnp.where(inner, pltpu.roll(gradient, 1, 0), 0.0),
    ]
    copies = [None] * 9
    for col_tap in range(3):
        copies[col_tap] = later_rows(by_column[col_tap])
        copies[3 + col_tap] = by_column[col_tap]
        copies[6 + col_tap] = earlier_rows(by_column[col_tap])
    return lanes([c.astype(BF) for c in copies])


def part_row(scalars, part):
    place = scalars[1] ^ part
    block = (place >> 1) ^ scalars[0]
    return place, pl.multiple_of(block * 128 + (place & 1) * 64, 64)


def fetch(pairs, sems):
    copies = [
        pltpu.make_async_copy(source, target, sems.at[i])
        for i, (source, target) in enumerate(pairs)
    ]
    for copy in copies:
        copy.start()
    for copy in copies:
        copy.wait()


def begin_kernel(
    scalars,
    x_any,
    gain_any,
    shift_any,
    conv_b_any,
    attn_b_any,
    proj_b_any,
    qkv_any,
    out_w_any,
    proj_any,
    act_ref,
    stats_ref,
    pack_ref,
    param_ref,
    x_ref,
    gain_ref,
    shift_ref,
    conv_b_ref,
    attn_b_ref,
    proj_b_ref,
    weights,
    proj_ref,
    proj,
    sems,
):
    own = pl.ds(pl.multiple_of(scalars[1] * 64, 64), 64)
    fetch(
        [
            (x_any, x_ref),
            (gain_any, gain_ref),
            (shift_any, shift_ref),
            (conv_b_any, conv_b_ref),
            (attn_b_any, attn_b_ref),
            (proj_b_any, proj_b_ref),
            (out_w_any.at[own, :], weights.at[3]),
            (proj_any, proj_ref),
        ]
        + [(qkv_any.at[m, own, :], weights.at[m]) for m in range(3)],
        sems,
    )
    normed, stats = moments(x_ref[...].astype(F32))
    pre = normed * gain_ref[0:1] + shift_ref[0:1]
    act_ref[...] = (pre * jax.nn.sigmoid(pre)).astype(BF)
    stats_ref[...] = stats
    for m in range(4):
        pack_ref[:, 128 * m : 128 * m + 128] = weights[m]
    proj[...] = jnp.transpose(proj_ref[...].astype(F32))
    pack_ref[:, 512:640] = lanes([proj[own, :], jnp.zeros((64, 64), F32)]).astype(BF)
    rows = [gain_ref[m : m + 1] for m in range(3)] + [shift_ref[m : m + 1] for m in range(3)]
    rows += [conv_b_ref[m : m + 1] for m in range(2)] + [attn_b_ref[m : m + 1] for m in range(3)]
    rows += [lanes([proj_b_ref[...], jnp.zeros_like(proj_b_ref[...])])]
    param_ref[...] = pack_rows(rows, 16)


def code_column(codes):
    grid = rows_of([codes[m] for m in range(codes.shape[0])])
    height = grid.shape[0] * LAT
    high = grid >> 5
    both = lanes([high.astype(F32), (grid - (high << 5)).astype(F32)]).astype(BF)
    lines = lax.broadcasted_iota(jnp.int32, (height, grid.shape[0]), 0) >> 4
    own = (lines == lax.broadcasted_iota(jnp.int32, lines.shape, 1)).astype(F32).astype(BF)
    spread = dot(own, both)
    column = lax.broadcasted_iota(jnp.int32, (height, LAT), 0) & (LAT - 1)
    here = column == lax.broadcasted_iota(jnp.int32, (height, LAT), 1)
    merged = 32.0 * spread[:, :LAT] + spread[:, LAT:]
    return jnp.sum(jnp.where(here, merged, 0.0), axis=1, keepdims=True).astype(jnp.int32)


def start_kernel(scalars, codes_ref, book_ref, cot_ref, _, hot_ref, quant_ref, usage_ref, fixed_ref, start):
    tokens = hot_ref.shape[0]
    hot32 = (
        code_column(codes_ref[...]) == lax.broadcasted_iota(jnp.int32, (tokens, CODES), 1)
    ).astype(F32)
    hot = hot32.astype(BF)
    hot_ref[...] = hot
    counts = col_sum(hot32)
    usage_ref[...] = pack_rows([counts[:, 128 * i : 128 * i + 128] for i in range(8)])
    high, rest = split_low(book_ref[...])
    middle, low = split_low(rest)
    picked = dot_nt(hot, rows_of([high, middle, low]).astype(BF))
    width = book_ref.shape[0]
    quantized = picked[:, :width] + picked[:, width : 2 * width] + picked[:, 2 * width :]
    quant_ref[...] = quantized
    start[...] = cot_ref[...].astype(F32) - 2.0 * BETA * quantized
    for k in range(4):
        row = (scalars[0] ^ k) * 128
        one = start[pl.ds(pl.multiple_of(row, 64), 64), :]
        two = start[pl.ds(pl.multiple_of(row + 64, 64), 64), :]
        fixed_ref[k] = lanes([one, two]).astype(BF)


def lay_weights(scalars, own_ref, other_ref, o_ref):
    for part in range(PARTS):
        source = (own_ref if part % 2 == 0 else other_ref).at[part // 2]
        _, row = part_row(scalars, part)
        spot = pl.ds(row, 64)
        for k in range(4):
            for m in range(4):
                o_ref[spot, 512 * m + 128 * k : 512 * m + 128 * k + 128] = source[
                    k, :, 128 * m : 128 * m + 128
                ]
        for pair in range(2):
            o_ref[spot, 2048 + 128 * pair : 2176 + 128 * pair] = lanes(
                [source[2 * pair + i, :, 512:576] for i in range(2)]
            )


def conv_one_kernel(
    scalars, a0, a1, a2, a3, w_ref, param_ref, _, hidden_ref, stats_ref, act_ref
):
    pieces = [a0[...], a1[...], a2[...], a3[...]]
    hidden = conv_forward(pieces, w_ref, scalars[0]) + param(param_ref, CONV_BIAS)
    hidden_ref[...] = hidden
    normed, stats = moments(hidden)
    stats_ref[...] = stats
    pre = normed * param(param_ref, GAIN + 1) + param(param_ref, SHIFT + 1)
    act_ref[...] = (pre * jax.nn.sigmoid(pre)).astype(BF)


def conv_two_kernel(
    scalars, a0, a1, a2, a3, w_ref, param_ref, x_ref, fixed_ref, normed_ref, stats_ref, *pay_refs
):
    residual = x_ref[...].astype(F32) + (
        conv_forward([a0[...], a1[...], a2[...], a3[...]], w_ref, scalars[0])
        + param(param_ref, CONV_BIAS + 1)
    )
    normed, stats = moments(residual)
    normed_ref[...] = normed
    stats_ref[...] = stats
    gain, shift = param(param_ref, GAIN + 2), param(param_ref, SHIFT + 2)
    for k, ref in enumerate(pay_refs):
        target = scalars[0] ^ k
        own, other = target * 128, (target ^ 1) * 128
        ref[0:128] = (
            normed_ref[pl.ds(pl.multiple_of(other, 128), 128), :] * gain + shift
        ).astype(BF)
        high, low = split_low(normed_ref[pl.ds(pl.multiple_of(own, 128), 128), :])
        ref[128:256] = high.astype(BF)
        ref[256:384] = low.astype(BF)
        is_two = jnp.broadcast_to(target >> 1, (1, 128)) == 1
        mean = jnp.where(is_two, stats[1:2], stats[0:1])
        deviation = jnp.where(is_two, stats[5:6], stats[4:5])
        rows = list(split_low(mean)) + list(split_low(deviation))
        for index in (GAIN + 2, SHIFT + 2, ATTN_BIAS, ATTN_BIAS + 1, ATTN_BIAS + 2, PROJ_BIAS):
            rows.extend(split_low(param(param_ref, index)))
        ref[384:400] = pack_rows(rows, 16).astype(BF)
        ref[400:464] = fixed_ref[k]


def attn_in_kernel(scalars, n0, n1, n2, n3, norm_ref, residual_ref, bias_ref):
    pieces = [n0, n1, n2, n3]
    tails = [n[384:400].astype(F32) for n in pieces]

    def vector(index, width=128):
        row = 2 * index
        return lanes([t[row : row + 1, :width] + t[row + 1 : row + 2, :width] for t in tails])

    mean, deviation, gain, shift = [vector(index) for index in range(4)]
    empty = jnp.zeros((1, 256), F32)
    bias_ref[...] = pack_rows([vector(4), vector(5), vector(6), lanes([vector(7, 64), empty])])
    own = lanes([n[128:256].astype(F32) + n[256:384].astype(F32) for n in pieces])
    residual_ref[...] = own * deviation + mean
    norm_ref[0:128] = (own * gain + shift).astype(BF)
    norm_ref[128:POS] = lanes([n[0:128] for n in pieces])


def attention_kernel(
    scalars,
    norm_ref,
    residual_ref,
    bias_ref,
    n0,
    n1,
    n2,
    n3,
    own_ref,
    other_ref,
    usage_ref,
    *refs,
):
    pay_refs, keep_refs, send_ref = refs[:4], refs[4:8], refs[8]
    w_ref, grads, lat_grad_ref, sums_ref = refs[9:]
    lay_weights(scalars, own_ref, other_ref, w_ref)
    query_bias, value_bias, out_bias = [bias_ref[m : m + 1] for m in range(3)]
    proj_bias = bias_ref[3:4, 0:256]
    pieces = [n0, n1, n2, n3]
    normed = norm_ref[...]
    query = (dot(norm_ref[0:128], w_ref[:, 0:512]) + query_bias).astype(BF)
    keys = dot(normed, w_ref[:, 512:1024]).astype(BF)
    values = (dot(normed, w_ref[:, 1024:1536]) + value_bias).astype(BF)
    scores = dot_nt(query, keys) * SCORE_SCALE
    weights = jnp.exp(scores - jnp.max(scores, axis=1, keepdims=True))
    probs = weights / jnp.sum(weights, axis=1, keepdims=True)
    probs_low = probs.astype(BF)
    mixed = dot(probs_low, values).astype(BF)
    attended = dot(mixed, w_ref[:, 1536:2048]) + out_bias
    output = (residual_ref[...] + attended).astype(BF)
    latents = dot(output, w_ref[:, 2048:2304]) + proj_bias
    fixed = []
    for n in pieces:
        both = n[400:464].astype(F32)
        fixed.append(rows_of([both[:, :64], both[:, 64:]]))
    lat_grad = (lanes(fixed) + 2.0 * BETA * latents).astype(BF)
    blank = jnp.zeros((128, 64), BF)
    for k in range(4):
        lat_grad_ref[:, 128 * k : 128 * k + 128] = lanes([lat_grad[:, 64 * k : 64 * k + 64], blank])
    out_grad = dot_nt(lat_grad, w_ref[:, 2048:2304])
    att_grad = out_grad.astype(BF)
    mixed_grad = dot_nt(att_grad, w_ref[:, 1536:2048]).astype(BF)
    probs_grad = dot_nt(mixed_grad, values)
    row_dot = jnp.sum(probs * probs_grad, axis=1, keepdims=True)
    score_grad = (probs * (probs_grad - row_dot)).astype(BF)
    query_grad = (dot(score_grad, keys) * SCORE_SCALE).astype(BF)
    key_grad = (dot_tn(score_grad, query) * SCORE_SCALE).astype(BF)
    value_grad = dot_tn(probs_low, mixed_grad).astype(BF)
    upstream = dot_nt(key_grad, w_ref[:, 512:1024]) + dot_nt(value_grad, w_ref[:, 1024:1536])
    upstream_own = upstream[:128] + dot_nt(query_grad, w_ref[:, 0:512])
    for k in range(4):
        ref = pay_refs[k]
        ref[0:128] = upstream_own[:, 128 * k : 128 * k + 128].astype(ref.dtype)
        ref[128:POS] = upstream[128:, 128 * k : 128 * k + 128].astype(ref.dtype)
        ref[POS : POS + 128] = out_grad[:, 128 * k : 128 * k + 128].astype(ref.dtype)
        piece = latents[:, 64 * k : 64 * k + 64]
        ref[POS + 128 : POS + 192] = lanes([piece[:64], piece[64:]]).astype(ref.dtype)
    sums_ref[...] = pack_rows(
        [
            col_sum(query_grad.astype(F32)),
            col_sum(value_grad.astype(F32)),
            col_sum(att_grad.astype(F32)),
            lanes(
                [
                    part
                    for k in range(4)
                    for part in (
                        col_sum(lat_grad[:, 64 * k : 64 * k + 64].astype(F32)),
                        jnp.zeros((1, 64), F32),
                    )
                ]
            ),
        ]
    )
    grads[:, 0:512] = dot_tn(norm_ref[0:128], query_grad).astype(BF)
    grads[:, 512:1024] = dot_tn(normed, key_grad).astype(BF)
    grads[:, 1024:1536] = dot_tn(normed, value_grad).astype(BF)
    grads[:, 1536:2048] = dot_tn(mixed, att_grad).astype(BF)
    grads[:, 2048:2560] = dot_tn(output, lat_grad_ref[...]).astype(BF)
    right = lax.broadcasted_iota(jnp.int32, (16, 128), 1) >= 64

    def halves(vectors, offset):
        blank = jnp.zeros((1, 128), F32)
        entries = [blank] * offset
        for vector in vectors:
            entries += [pltpu.roll(vector, 64, 1), vector]
        return jnp.where(right, pack_rows(entries, 16), 0.0)

    biases = []
    for k in range(4):
        vectors = [sums_ref[m : m + 1, 128 * k : 128 * k + 128] for m in range(4)]
        biases.append(halves(vectors, 4))
    tens = jnp.floor(usage_ref[...] * (1.0 / 16.0))
    ones = usage_ref[...] - 16.0 * tens
    for part in range(PARTS):
        place, row = part_row(scalars, part)
        is_first = (jnp.broadcast_to(place, (16, 128)) == 0).astype(F32)
        here = jnp.broadcast_to(place, (8, 128)) == lax.broadcasted_iota(jnp.int32, (8, 128), 0)
        counts = [col_sum(jnp.where(here, digit, 0.0)) for digit in (tens, ones)]
        for k in range(4):
            ref = keep_refs[part // 2].at[k] if part % 2 == 0 else send_ref.at[part // 2, k]
            for m in range(4):
                ref[:, 128 * m : 128 * m + 128] = grads[
                    pl.ds(row, 64), 512 * m + 128 * k : 512 * m + 128 * k + 128
                ]
            extra = biases[k] * is_first
            if k == 0:
                extra = extra + halves(counts, 0)
            block = slice(2048 + 128 * k, 2176 + 128 * k)
            ref[0:16, 512:640] = (grads[pl.ds(row, 16), block].astype(F32) + extra).astype(BF)
            ref[16:64, 512:640] = grads[pl.ds(row + 16, 48), block]


def third_back_kernel(
    scalars,
    p0,
    p1,
    p2,
    p3,
    normed_ref,
    stats_ref,
    param_ref,
    _,
    w_ref,
    residual_ref,
    taps_ref,
    lat_ref,
    small_ref,
    q0,
    q1,
    q2,
    q3,
    up_ref,
    out_ref,
):
    z = scalars[0]
    for near, far, base in ((p0, p1, z), (p2, p3, z ^ 2)):
        first, second = near[0:POS].astype(F32), far[0:POS].astype(F32)
        up_ref[pl.ds(pl.multiple_of(base * 128, 128), 128), :] = first[:128] + second[128:]
        up_ref[pl.ds(pl.multiple_of((base ^ 1) * 128, 128), 128), :] = first[128:] + second[:128]
    for k, ref in enumerate((p0, p1, p2, p3)):
        row = (z ^ k) * 128
        out_ref[pl.ds(pl.multiple_of(row, 128), 128), :] = ref[POS : POS + 128].astype(F32)
        piece = ref[POS + 128 : POS + 192].astype(F32)
        lat_ref[pl.ds(pl.multiple_of(row, 64), 64), :] = piece[:, :64]
        lat_ref[pl.ds(pl.multiple_of(row + 64, 64), 64), :] = piece[:, 64:]
    source, gain_grad, shift_grad = norm_back(
        up_ref[...], normed_ref[...], stats_ref[...], param(param_ref, GAIN + 2)
    )
    residual = out_ref[...] + source
    residual_ref[...] = residual
    low = residual.astype(BF).astype(F32)
    small_ref[...] = pack_rows([gain_grad, shift_grad, col_sum(low)])
    send_taps(low, w_ref, scalars[0], taps_ref, (q0, q1, q2, q3))


def send_taps(gradient, w_ref, z, taps_ref, piece_refs):
    taps = spread_taps(gradient)
    taps_ref[...] = taps
    rows = []
    for k in range(4):
        block = pl.ds(pl.multiple_of((z ^ k) * 128, 128), 128)
        rows.append(lanes([w_ref[0, tap, block, :] for tap in range(9)]))
    every = dot_nt(taps, rows_of(rows))
    for k, ref in enumerate(piece_refs):
        ref[...] = every[:, 128 * k : 128 * k + 128].astype(ref.dtype)


def swish_back(gradient, normed, gain, shift):
    pre = normed * gain + shift
    gate = jax.nn.sigmoid(pre)
    return gradient * (gate * (1.0 + pre * (1.0 - gate)))


def second_back_kernel(
    scalars,
    p0,
    p1,
    p2,
    p3,
    hidden_ref,
    stats_ref,
    param_ref,
    _,
    __,
    a0,
    a1,
    a2,
    a3,
    w_ref,
    small_ref,
    q0,
    q1,
    q2,
    q3,
    *refs,
):
    keep_refs, send_ref, grads, taps_ref = refs[:4], refs[4], refs[5], refs[6]
    gradient = p0[...] + p1[...].astype(F32) + p2[...].astype(F32) + p3[...].astype(F32)
    stats = stats_ref[...]
    normed = renormed(hidden_ref[...], stats)
    gain = param(param_ref, GAIN + 1)
    upstream = swish_back(gradient, normed, gain, param(param_ref, SHIFT + 1))
    source, gain_grad, shift_grad = norm_back(upstream, normed, stats, gain)
    low = source.astype(BF).astype(F32)
    small_ref[...] = pack_rows([gain_grad, shift_grad, col_sum(low)])
    send_taps(low, w_ref, scalars[0], taps_ref, (q0, q1, q2, q3))
    full = lanes([a0[...], a1[...], a2[...], a3[...]])
    grads[...] = dot_tn(full, taps_ref[...]).astype(BF)
    for part in range(PARTS):
        _, row = part_row(scalars, part)
        value = grads[pl.ds(row, 64), :]
        if part % 2 == 0:
            keep_refs[part // 2][...] = value
        else:
            send_ref[part // 2] = value


def first_back_kernel(
    scalars,
    p0,
    p1,
    p2,
    p3,
    x_ref,
    stats_ref,
    param_ref,
    residual_ref,
    _,
    __,
    ___,
    grad_ref,
    small_ref,
):
    gradient = p0[...] + p1[...].astype(F32) + p2[...].astype(F32) + p3[...].astype(F32)
    stats = stats_ref[...]
    normed = renormed(x_ref[...].astype(F32), stats)
    gain = param(param_ref, GAIN)
    upstream = swish_back(gradient, normed, gain, param(param_ref, SHIFT))
    source, gain_grad, shift_grad = norm_back(upstream, normed, stats, gain)
    grad_ref[...] = residual_ref[...] + source
    small_ref[...] = pack_rows([gain_grad, shift_grad])


def conv_two_grad_kernel(
    scalars, a0, a1, a2, a3, taps_ref, hot_ref, lat_ref, quant_ref, reset_ref, scale, *refs
):
    keep_refs, send_ref, commit_ref, grads, book = refs[:4], refs[4], refs[5], refs[6], refs[7]
    full = lanes([a0[...], a1[...], a2[...], a3[...]])
    grads[...] = dot_tn(full, taps_ref[...]).astype(BF)
    latents = lat_ref[...]
    difference = latents - quant_ref[...]
    commit_ref[...] = pack_rows([lanes([col_sum(difference * difference), jnp.zeros((1, 64), F32)])])
    high, low = split_low(difference * (-scale))
    sums = dot_tn(lanes([high, low]).astype(BF), hot_ref[...])
    tokens = latents.shape[0]
    where = reset_ref[...] - scalars[2] * tokens
    chosen = (where == lax.broadcasted_iota(jnp.int32, (tokens, CODES), 0)).astype(F32).astype(BF)
    picked = dot_tn(latents.astype(BF), chosen)
    book[0:64] = (sums[:64] + sums[64:]).astype(BF)
    book[64:128] = picked.astype(BF)
    for part in range(PARTS):
        place, row = part_row(scalars, part)
        ref = keep_refs[part // 2] if part % 2 == 0 else send_ref.at[part // 2]
        ref[:, 0:WIDE] = grads[pl.ds(row, 64), :]
        column = pl.ds(pl.multiple_of(place * 128, 128), 128)
        ref[:, WIDE : WIDE + 128] = book[0:64, column]
        ref[:, WIDE + 128 : WIDE + 256] = book[64:128, column]


def finish_two_kernel(scalars, own_ref, other_ref, conv_ref, book_grad_ref, picked_ref):
    for part in range(PARTS):
        source = (own_ref if part % 2 == 0 else other_ref).at[part // 2]
        place = scalars[1] ^ part
        rows = pl.ds(pl.multiple_of(place * 64, 64), 64)
        for tap in range(9):
            conv_ref[0, tap, rows, :] = source[:, 128 * tap : 128 * tap + 128].astype(F32)
        column = pl.ds(pl.multiple_of(place * 128, 128), 128)
        book_grad_ref[:, column] = source[:, WIDE : WIDE + 128].astype(F32)
        picked_ref[:, column] = source[:, WIDE + 128 : WIDE + 256].astype(F32)


def finish_last_kernel(
    tokens_all,
    scalars,
    own_ref,
    other_ref,
    picked,
    book_ref,
    held_ref,
    conv_ref,
    gain_ref,
    shift_ref,
    bias_ref,
    commit_ref,
    qkv_ref,
    out_w_ref,
    proj_ref,
    new_book_ref,
    perplexity_ref,
    attn_bias_ref,
    proj_bias_ref,
    usage,
    proj,
):
    extra_sum = jnp.zeros((16, 128), F32)
    total = jnp.zeros((9, 128), F32)
    for part in range(PARTS):
        source = (own_ref if part % 2 == 0 else other_ref).at[part // 2]
        place = scalars[1] ^ part
        rows = pl.ds(pl.multiple_of(place * 64, 64), 64)
        for tap in range(9):
            conv_ref[0, tap, rows, :] = source[:, 128 * tap : 128 * tap + 128].astype(F32)
        for m in range(3):
            qkv_ref[m, rows, :] = source[:, 1152 + 128 * m : 1280 + 128 * m].astype(F32)
        out_w_ref[rows, :] = source[:, 1536:1664].astype(F32)
        proj[rows, :] = source[:, 1664:1792].astype(F32)
        extra = source[0:16, 1664:1792].astype(F32)
        extra_sum = extra_sum + extra
        usage[pl.ds(place, 1), :] = lanes(
            [
                16.0 * extra[0:1, 64:] + extra[2:3, 64:],
                16.0 * extra[1:2, 64:] + extra[3:4, 64:],
            ]
        )
        both = source[16:64, 1728:1792].astype(F32)
        both = both[0:18] + both[18:36]
        total = total + lanes([both[0:9], both[9:18]])
    for index, row in enumerate((0, 2, 5)):
        gain_ref[index : index + 1] = total[row : row + 1]
        shift_ref[index : index + 1] = total[row + 1 : row + 2]
    bias_ref[0:1] = total[4:5]
    bias_ref[1:2] = total[7:8]
    commit_ref[...] = total[8:9, :64] * (1.0 / tokens_all)
    proj_ref[...] = jnp.transpose(proj[...])[0:64]
    counts = usage[...]
    share = counts * (1.0 / tokens_all)
    terms = share * jnp.log(jnp.maximum(share, 1.0 / tokens_all))
    entropy = jnp.sum(jnp.sum(terms, axis=1, keepdims=True), axis=0, keepdims=True)
    perplexity_ref[...] = jnp.exp(-entropy)
    for block in range(8):
        spot = slice(128 * block, 128 * block + 128)
        new_book_ref[:, spot] = jnp.where(
            counts[block : block + 1] > 0.5, book_ref[:, spot], picked[:, spot]
        )
    for m in range(3):
        attn_bias_ref[m : m + 1] = lanes(
            [extra_sum[4 + 2 * m : 5 + 2 * m, 64:], extra_sum[5 + 2 * m : 6 + 2 * m, 64:]]
        )
    proj_bias_ref[...] = extra_sum[10:11, 64:]


def pair_add_kernel(scalars, k0, k1, k2, k3, get_ref, _, keep_ref, send_ref):
    for i, ref in enumerate((k0, k1, k2, k3)):
        target = (send_ref if i % 2 else keep_ref).at[i // 2]
        target[...] = plus(ref[...], get_ref[i])


def plus(first, second):
    return (first.astype(F32) + second.astype(F32)).astype(BF)


def half_add_kernel(scalars, keep_ref, get_ref, _, own_ref, send_ref):
    own_ref[...] = plus(keep_ref[0], get_ref[0])
    send_ref[...] = plus(keep_ref[1], get_ref[1])


def attn_sum_kernel(scalars, a0, a1, _, keep_ref, send_ref):
    for k in range(4):
        (send_ref if k % 2 else keep_ref)[k // 2] = plus(a0[k], a1[k])


def pass_kernel(scalars, a0, a1, a2, _, b0, b1, b2):
    for source, target in ((a0, b0), (a1, b1), (a2, b2)):
        target[...] = source[...]


def add_kernel(scalars, k0, k1, k2, k3, get_ref, _, *sum_refs):
    for i, ref in enumerate((k0, k1, k2, k3)):
        sum_refs[i][...] = plus(ref[...], get_ref[i])


def two_sum_kernel(scalars, a0, a1, _, sum_ref):
    sum_ref[...] = plus(a0[...], a1[...])


def last_kernel(
    scalars, o0, o1, o2, o3, att_own, att_get, small_one, small_two, small_three, commit, last_ref
):
    total = o0[...].astype(F32)
    for ref in (o1, o2, o3):
        total = total + ref[...].astype(F32)
    last_ref[:, 0:WIDE] = total.astype(BF)
    last_ref[:, 1152:1664] = plus(att_own[:, 0:512], att_get[:, 0:512])
    rows = [small_one[0:1], small_one[1:2]]
    rows += [small_two[m : m + 1] for m in range(3)]
    rows += [small_three[m : m + 1] for m in range(3)]
    rows += [commit[0:1]]
    high, low = split_low(pack_rows(rows, 16))
    blank = jnp.zeros((48, 64), F32)
    small = rows_of([high[:9, :64], high[:9, 64:], low[:9, :64], low[:9, 64:], jnp.zeros((12, 64), F32)])
    small = lanes([blank, small])
    block = att_own[:, 512:640].astype(F32) + att_get[:, 512:640].astype(F32)
    last_ref[0:16, 1664:1792] = block[0:16].astype(BF)
    last_ref[16:64, 1664:1792] = (block[16:64] + small).astype(BF)


def stack_kernel(scalars, *refs):
    out_ref = refs[-1]
    for k in range(out_ref.shape[0]):
        out_ref[k] = refs[k][...]


def over(axis, array, flip):
    size = lax.axis_size(axis)
    return lax.ppermute(array, axis, [(i, i ^ flip) for i in range(size)])


def flips(array):
    return [over("chan", array, k) for k in (1, 2, 3)]


def plane(array):
    return [array] + [over("dp", array, k) for k in (2, 4, 6)]


def add(*arrays):
    total = arrays[0].astype(F32)
    for array in arrays[1:]:
        total = total + array.astype(F32)
    return total.astype(BF)


def shards(
    latents_in,
    norm_gains,
    norm_shifts,
    conv_weights,
    conv_biases,
    qkv_weights,
    attn_biases,
    out_weight,
    proj_weight,
    proj_bias,
    codebook,
    codes,
    reset_src,
    cotangent,
):
    images = latents_in.shape[0]
    tokens = images * POS
    quarter = tokens // 4
    devices = lax.axis_size("dp")
    tokens_all = tokens * devices
    by_hand = devices == PARTS
    z = lax.axis_index("chan").astype(jnp.int32)
    dp = lax.axis_index("dp").astype(jnp.int32)
    scalars = jnp.stack([z, dp if by_hand else jnp.zeros_like(dp), dp, jnp.zeros_like(dp)])
    x = latents_in.reshape(tokens, 128)
    conv_w = conv_weights.reshape(2, 9, C, 128)

    def whole(shape):
        return pl.BlockSpec(shape, lambda i, n=len(shape): (0,) * n)

    def blocks_call(body, in_specs, out_specs, outs, name, *args, scratch=(), aliases={}):
        return pl.pallas_call(
            body,
            grid=(1,),
            out_shape=outs,
            in_specs=[pl.BlockSpec(memory_space=pltpu.SMEM)] + in_specs,
            out_specs=out_specs,
            scratch_shapes=scratch,
            input_output_aliases=aliases,
            compiler_params=pltpu.CompilerParams(vmem_limit_bytes=VMEM * 2**20),
            cost_estimate=pl.CostEstimate(flops=HEAVY, bytes_accessed=1, transcendentals=0),
            name=name,
        )(scalars, *args)

    act_one, stats_one, pack, params = call(
        begin_kernel,
        [
            sds((tokens, 128), BF),
            sds((8, 128), F32),
            sds((64, 640), BF),
            sds((16, 128), F32),
        ],
        scalars,
        x,
        norm_gains,
        norm_shifts,
        conv_biases,
        attn_biases,
        proj_bias.reshape(1, 64),
        qkv_weights,
        out_weight,
        proj_weight.T,
        scratch=[
            pltpu.VMEM((tokens, 128), BF),
            pltpu.VMEM((3, 128), F32),
            pltpu.VMEM((3, 128), F32),
            pltpu.VMEM((2, 128), F32),
            pltpu.VMEM((3, 128), F32),
            pltpu.VMEM((1, 64), F32),
            pltpu.VMEM((4, 64, 128), BF),
            pltpu.VMEM((64, C), BF),
            pltpu.VMEM((C, 64), F32),
            pltpu.SemaphoreType.DMA((11,)),
        ],
        flops=HEAVY,
        space=pl.ANY,
        vmem=60,
        name="begin",
    )
    pieces_one = [act_one] + flips(act_one)
    packs = [pack] + flips(pack)
    hot, quantized, usage, fixed = call(
        start_kernel,
        [
            sds((tokens, CODES), BF),
            sds((tokens, 64), F32),
            sds((8, 128), F32),
            sds((4, 64, 128), BF),
        ],
        scalars,
        codes,
        codebook.T,
        cotangent.reshape(tokens, 64),
        stats_one,
        scratch=[pltpu.VMEM((tokens, 64), F32)],
        name="start",
    )
    def conv_call(body, index, outs, name, *args):
        specs = []
        for a in args:
            if a is conv_w:
                specs.append(pl.BlockSpec((1, 9, C, 128), lambda i: (index, 0, 0, 0)))
            else:
                specs.append(whole(a.shape))
        scratch = ()
        if body is third_back_kernel:
            scratch = [pltpu.VMEM((tokens, 128), F32), pltpu.VMEM((tokens, 128), F32)]
        if body is second_back_kernel:
            scratch = [pltpu.VMEM((C, WIDE), BF), pltpu.VMEM((tokens, WIDE), BF)]
        return blocks_call(
            body, specs, [whole(o.shape) for o in outs], outs, name, *args, scratch=scratch
        )

    hidden, stats_two, act_two = conv_call(
        conv_one_kernel,
        0,
        [sds((tokens, 128), F32), sds((8, 128), F32), sds((tokens, 128), BF)],
        "conv_one",
        *pieces_one,
        conv_w,
        params,
        usage,
    )
    pieces_two = [act_two] + flips(act_two)
    if by_hand:
        block = call(
            stack_kernel,
            [sds((4, 64, 640), BF)],
            scalars,
            *packs,
            flops=HEAVY,
            name="pack_join",
        )[0]
        blocks = [block] + [over("dp", block, k) for k in (2, 4, 6)]
    else:
        packed = jnp.concatenate(
            [qkv_weights[0], qkv_weights[1], qkv_weights[2], out_weight, proj_weight]
            + [jnp.zeros((C, 64), BF)],
            axis=1,
        )
        block = jnp.stack([packed] + flips(packed)).reshape(4, PARTS, 64, 640)
        block = jnp.swapaxes(block, 0, 1)
        block_own, block_other = block[0::2], block[1::2]
    normed_three, stats_three, *pays = conv_call(
        conv_two_kernel,
        1,
        [sds((tokens, 128), F32), sds((8, 128), F32)] + [sds((464, 128), BF)] * 4,
        "conv_two",
        *pieces_two,
        conv_w,
        params,
        x,
        fixed,
    )
    normed_pieces = [pays[0]] + [over("chan", pays[k], k) for k in (1, 2, 3)]
    if by_hand:
        block_own = call(
            stack_kernel,
            [sds((4, 4, 64, 640), BF)],
            scalars,
            *blocks,
            name="pack_plane",
        )[0]
        block_other = over("dp", block_own, 1)
    normed, residual_part, bias_rows = call(
        attn_in_kernel,
        [sds((POS, C), BF), sds((quarter, C), F32), sds((8, C), F32)],
        scalars,
        *normed_pieces,
        flops=HEAVY,
        name="attn_in",
    )
    *pays, k0, k1, k2, k3, att_send = call(
        attention_kernel,
        [sds((POS + 192, 128), F32)]
        + [sds((POS + 192, 128), BF)] * 3
        + [sds((4, 64, 640), BF)] * 4
        + [sds((4, 4, 64, 640), BF)],
        scalars,
        normed,
        residual_part,
        bias_rows,
        *normed_pieces,
        block_own,
        block_other,
        usage,
        scratch=[
            pltpu.VMEM((C, 2304), BF),
            pltpu.VMEM((C, 2560), BF),
            pltpu.VMEM((quarter, C), BF),
            pltpu.VMEM((8, C), F32),
        ],
        flops=HEAVY,
        name="attention",
    )
    att_keep = [k0, k1, k2, k3]

    back_three = [pays[0]] + [over("chan", pays[k], k) for k in (1, 2, 3)]
    def pair_sum(keep, send, after, name):
        outs = [sds((2,) + keep[0].shape, BF)] * 2
        got = over("dp", send, 1)
        kept, sent = call(pair_add_kernel, outs, scalars, *keep, got, after, name=name)
        return kept, over("dp", sent, 2)

    if by_hand:
        att_kept, att_got = pair_sum(att_keep, att_send, back_three[1], "attn_pair")
    residual_grad, taps_two, latents, small_three, *pays = conv_call(
        third_back_kernel,
        1,
        [
            sds((tokens, 128), F32),
            sds((tokens, WIDE), BF),
            sds((tokens, 64), F32),
            sds((8, 128), F32),
            sds((tokens, 128), F32),
        ]
        + [sds((tokens, 128), BF)] * 3,
        "third_back",
        *back_three,
        normed_three,
        stats_three,
        params,
        att_kept if by_hand else bias_rows,
        conv_w,
    )
    back_two = [pays[0]] + [over("chan", pays[k], k) for k in (1, 2, 3)]
    book_scale = 2.0 * CODES / tokens_all

    def two_grad(*refs):
        conv_two_grad_kernel(*refs[:10], book_scale, *refs[10:])

    *two_keep, two_send, commit = call(
        two_grad,
        [sds((64, 1408), BF)] * 4 + [sds((4, 64, 1408), BF), sds((8, 128), F32)],
        scalars,
        *pieces_two,
        taps_two,
        hot,
        latents,
        quantized,
        reset_src.reshape(1, CODES),
        scratch=[pltpu.VMEM((C, WIDE), BF), pltpu.VMEM((128, CODES), BF)],
        name="conv_two_grad",
    )
    if by_hand:
        att_own, att_sent = call(
            half_add_kernel,
            [sds((4, 64, 640), BF)] * 2,
            scalars,
            att_kept,
            att_got,
            small_three,
            flops=HEAVY,
            name="attn_half",
        )
        att_got = over("dp", att_sent, 4)
        two_kept, two_got = pair_sum(two_keep, two_send, att_own, "conv_two_pair")
    small_two, *pays = conv_call(
        second_back_kernel,
        0,
        [sds((8, 128), F32), sds((tokens, 128), F32)]
        + [sds((tokens, 128), BF)] * 3
        + [sds((64, WIDE), BF)] * 4
        + [sds((4, 64, WIDE), BF)],
        "second_back",
        *back_two,
        hidden,
        stats_two,
        params,
        att_own if by_hand else bias_rows,
        two_kept if by_hand else bias_rows,
        *pieces_one,
        conv_w,
    )
    *one_keep, one_send = pays[4:]
    pays = pays[:4]
    one_got = over("dp", one_send, 1) if by_hand else one_send
    pays[1:] = call(
        pass_kernel,
        [sds((tokens, 128), BF)] * 3,
        scalars,
        *pays[1:],
        one_keep[0],
        flops=HEAVY,
        name="pass_on",
    )
    back_one = [pays[0]] + [over("chan", pays[k], k) for k in (1, 2, 3)]
    if by_hand:
        att_kept, att_sent = call(
            attn_sum_kernel,
            [sds((2, 64, 640), BF)] * 2,
            scalars,
            att_own,
            att_got,
            small_two,
            name="attn_sum",
        )
        att_got = over("chan", att_sent, 1)
        two_own, two_sent = call(
            half_add_kernel,
            [sds((64, 1408), BF)] * 2,
            scalars,
            two_kept,
            two_got,
            att_kept,
            name="conv_two_half",
        )
        two_got = over("dp", two_sent, 4)
        one_parts = call(
            add_kernel,
            [sds((64, WIDE), BF)] * 4,
            scalars,
            *one_keep,
            one_got,
            att_kept,
            name="conv_one_add",
        )
        one_parts = [one_parts[0]] + [over("dp", one_parts[i], 2 * i) for i in (1, 2, 3)]
        att_own, att_sent = call(
            half_add_kernel,
            [sds((64, 640), BF)] * 2,
            scalars,
            att_kept,
            att_got,
            two_own,
            name="attn_last",
        )
        att_got = over("chan", att_sent, 2)
        two = call(
            two_sum_kernel,
            [sds((64, 1408), BF)],
            scalars,
            two_own,
            two_got,
            one_parts[0],
            name="conv_two_sum",
        )[0]
    grad_latents, small_one = call(
        first_back_kernel,
        [sds((tokens, 128), F32), sds((8, 128), F32)],
        scalars,
        *back_one,
        x,
        stats_one,
        params,
        residual_grad,
        one_parts[0] if by_hand else bias_rows,
        two if by_hand else bias_rows,
        att_own if by_hand else bias_rows,
        flops=HEAVY,
        name="first_back",
    )

    if by_hand:
        last = call(
            last_kernel,
            [sds((64, 1792), BF)],
            scalars,
            *one_parts,
            att_own,
            att_got,
            small_one,
            small_two,
            small_three,
            commit,
            flops=HEAVY,
            name="last",
        )[0]

        def chip(array, name, *after, flops=0):
            parts = plane(array)
            outs = [sds((4,) + array.shape, BF)]
            return call(stack_kernel, outs, scalars, *parts, *after, flops=flops, name=name)[0]

        two_own = chip(two, "stack_two", last, flops=HEAVY)
        two_other = over("dp", two_own, 1)
        last_own = chip(last, "stack_last", flops=HEAVY)
        last_other = over("dp", last_own, 1)
    else:

        def total(keep, send):
            parts = jnp.stack([jnp.stack(keep), send]).astype(F32)
            return lax.psum(parts, "dp").astype(BF)

        att_sum = total(att_keep, att_send)
        att_sum = add(att_sum[:, :, 0], *[over("chan", att_sum[:, :, k], k) for k in (1, 2, 3)])
        small = jnp.concatenate([small_one[0:2], small_two[0:3], small_three[0:3], commit[0:1]])
        small = jnp.concatenate([lax.psum(small, "dp"), jnp.zeros((7, 128), F32)])
        high = lax.reduce_precision(small, 8, 7)
        halves = [v[:9, c : c + 64] for v in (high, small - high) for c in (0, 64)]
        smalls = jnp.concatenate(halves + [jnp.zeros((12, 64), F32)]).astype(BF)
        att_sum = att_sum.at[0, 0, 16:64, 576:640].add(smalls)
        two_own, two_other = total(two_keep, two_send)
        one_sum = total(one_keep, one_send)
        last_own, last_other = jnp.concatenate([one_sum, att_sum], axis=3)

    conv_held, book_grad, picked = blocks_call(
        finish_two_kernel,
        [whole((4, 64, 1408)), whole((4, 64, 1408))],
        [
            pl.BlockSpec((1, 9, C, 128), lambda i: (1, 0, 0, 0)),
            whole((64, CODES)),
            whole((64, CODES)),
        ],
        [sds((2, 9, C, 128), F32), sds((64, CODES), F32), sds((64, CODES), F32)],
        "finish_two",
        two_own,
        two_other,
    )

    def finish_last(*refs):
        finish_last_kernel(float(tokens_all), *refs)

    outs = [
        sds((2, 9, C, 128), F32),
        sds((3, 128), F32),
        sds((3, 128), F32),
        sds((2, 128), F32),
        sds((1, 64), F32),
        sds((3, C, 128), F32),
        sds((C, 128), F32),
        sds((64, C), F32),
        sds((64, CODES), F32),
        sds((1, 1), F32),
        sds((3, 128), F32),
        sds((1, 64), F32),
    ]
    (
        conv_grad,
        gain_grad,
        shift_grad,
        conv_bias_grad,
        commitment,
        qkv_grad,
        out_grad,
        proj_grad,
        new_codebook,
        perplexity,
        attn_bias_grad,
        proj_bias_grad,
    ) = blocks_call(
        finish_last,
        [whole((4, 64, 1792)), whole((4, 64, 1792)), whole((64, CODES)), whole((64, CODES))]
        + [pl.BlockSpec(memory_space=pl.ANY)],
        [pl.BlockSpec((1, 9, C, 128), lambda i: (0, 0, 0, 0))] + [whole(o.shape) for o in outs[1:]],
        outs,
        "finish_last",
        last_own,
        last_other,
        picked,
        codebook.T,
        conv_held,
        scratch=[pltpu.VMEM((8, 128), F32), pltpu.VMEM((C, 128), F32)],
        aliases={5: 0},
    )

    return (
        latents.reshape(images, LAT, LAT, -1),
        commitment.reshape(64),
        perplexity.reshape(()),
        new_codebook.T,
        grad_latents.reshape(images, LAT, LAT, 128),
        gain_grad,
        shift_grad,
        conv_grad.reshape(2, 3, 3, C, 128),
        conv_bias_grad,
        qkv_grad,
        attn_bias_grad,
        out_grad,
        proj_grad.T,
        proj_bias_grad.reshape(64),
        book_grad.T,
    )


def solution(mesh):
    return jax.shard_map(
        shards,
        mesh=mesh,
        in_specs=(
            P("dp", None, None, "chan"),
            P(None, "chan"),
            P(None, "chan"),
            P(None, None, None, None, "chan"),
            P(None, "chan"),
            P(None, None, "chan"),
            P(None, "chan"),
            P(None, "chan"),
            P(None, "chan"),
            P("chan"),
            P(None, "chan"),
            P("dp", None, None),
            P(),
            P("dp", None, None, "chan"),
        ),
        out_specs=(
            P("dp", None, None, "chan"),
            P("chan"),
            P(),
            P(None, "chan"),
            P("dp", None, None, "chan"),
            P(None, "chan"),
            P(None, "chan"),
            P(None, None, None, None, "chan"),
            P(None, "chan"),
            P(None, None, "chan"),
            P(None, "chan"),
            P(None, "chan"),
            P(None, "chan"),
            P("chan"),
            P(None, "chan"),
        ),
        check_vma=False,
    )
```

```python
import jax
import jax.numpy as jnp
from jax import lax
from jax.experimental import pallas as pl
from jax.experimental.pallas import tpu as pltpu
from jax.sharding import PartitionSpec as P

F32 = jnp.float32
BF = jnp.bfloat16
C = 512
CODES = 1024
LAT = 16
POS = LAT * LAT
EPSILON = 1e-06
BETA = 0.25
SCORE_SCALE = float(C) ** (-0.5)
GROUP_COUNT = float(POS * 16)
WIDE = 1152
VMEM = 20
HEAVY = 10**11
PARTS = 8


def call(body, outs, *args, scratch=(), flops=0, name=None, space=pltpu.VMEM):
    result = pl.pallas_call(
        body,
        out_shape=list(outs),
        in_specs=[pl.BlockSpec(memory_space=pltpu.SMEM)]
        + [pl.BlockSpec(memory_space=space)] * (len(args) - 1),
        out_specs=[pl.BlockSpec(memory_space=pltpu.VMEM)] * len(outs),
        scratch_shapes=list(scratch),
        compiler_params=pltpu.CompilerParams(vmem_limit_bytes=VMEM * 2**20),
        cost_estimate=pl.CostEstimate(flops=flops, bytes_accessed=1, transcendentals=0),
        name=name,
    )(*args)
    return result


def sds(shape, dtype):
    return jax.ShapeDtypeStruct(shape, dtype)


def dot(a, b):
    return jnp.dot(a, b, preferred_element_type=F32)


def dot_nt(a, b):
    return lax.dot_general(a, b, (((1,), (1,)), ((), ())), preferred_element_type=F32)


def dot_tn(a, b):
    return lax.dot_general(a, b, (((0,), (0,)), ((), ())), preferred_element_type=F32)


def lanes(parts):
    return jnp.concatenate(parts, axis=1)


def rows_of(parts):
    return jnp.concatenate(parts, axis=0)


def pack_rows(vectors, height=8):
    width = vectors[0].shape[1]
    spot = lax.broadcasted_iota(jnp.int32, (height, width), 0)
    result = jnp.zeros((height, width), F32)
    for index, vector in enumerate(vectors):
        result = jnp.where(spot == index, vector, result)
    return result


def split_low(values):
    high = values.astype(BF).astype(F32)
    return high, values - high


def group_sums(rows):
    first = lax.broadcasted_iota(jnp.int32, (128, 128), 0) >> 4
    second = lax.broadcasted_iota(jnp.int32, (128, 128), 1) >> 4
    ones = (first == second).astype(F32).astype(BF)
    high, rest = split_low(rows)
    middle, low = split_low(rest)
    stacked = rows_of([high, middle, low, jnp.zeros_like(high)]).astype(BF)
    summed = dot(stacked, ones)
    return summed[0:8] + summed[8:16] + summed[16:24]


def col_sum(values):
    return jnp.sum(values, axis=0, keepdims=True)


def moments(values):
    one, two = values[:POS], values[POS:]
    mean = group_sums(pack_rows([col_sum(one), col_sum(two)])) * (1.0 / GROUP_COUNT)
    one, two = one - mean[0:1], two - mean[1:2]
    variance = group_sums(pack_rows([col_sum(one * one), col_sum(two * two)])) * (
        1.0 / GROUP_COUNT
    )
    inverse = lax.rsqrt(variance + EPSILON)
    deviation = jnp.sqrt(variance + EPSILON)
    normed = rows_of([one * inverse[0:1], two * inverse[1:2]])
    stats = pack_rows(
        [mean[0:1], mean[1:2], inverse[0:1], inverse[1:2], deviation[0:1], deviation[1:2]]
    )
    return normed, stats


def renormed(values, stats):
    return rows_of(
        [
            (values[:POS] - stats[0:1]) * stats[2:3],
            (values[POS:] - stats[1:2]) * stats[3:4],
        ]
    )


def norm_back(upstream, normed, stats, gain):
    sides = [(upstream[:POS], normed[:POS]), (upstream[POS:], normed[POS:])]
    plain = [col_sum(u) for u, _ in sides]
    weighted = [col_sum(u * n) for u, n in sides]
    means = group_sums(
        pack_rows([plain[0] * gain, plain[1] * gain, weighted[0] * gain, weighted[1] * gain])
    ) * (1.0 / GROUP_COUNT)
    parts = [
        stats[2 + m : 3 + m] * (u * gain - means[m : m + 1] - n * means[2 + m : 3 + m])
        for m, (u, n) in enumerate(sides)
    ]
    return rows_of(parts), weighted[0] + weighted[1], plain[0] + plain[1]


GAIN, SHIFT, CONV_BIAS, ATTN_BIAS, PROJ_BIAS = 0, 3, 6, 8, 11


def param(ref, index):
    return ref[index : index + 1]


def column_masks(height):
    column = lax.broadcasted_iota(jnp.int32, (height, 128), 0) & (LAT - 1)
    return column >= 1, column <= LAT - 2


def later_rows(values):
    blank = jnp.zeros((LAT, values.shape[1]), values.dtype)
    return rows_of([values[LAT:POS], blank, values[POS + LAT :], blank])


def earlier_rows(values):
    blank = jnp.zeros((LAT, values.shape[1]), values.dtype)
    return rows_of([blank, values[: POS - LAT], blank, values[POS : 2 * POS - LAT]])


def conv_forward(pieces, w_ref, z):
    full = lanes(pieces)
    height = full.shape[0]
    inner, outer = column_masks(height)
    blocks = [pl.ds(pl.multiple_of((z ^ k) * 128, 128), 128) for k in range(4)]
    weights = lanes(
        [rows_of([w_ref[0, tap, block, :] for block in blocks]) for tap in range(9)]
    )
    every = dot(full, weights)
    sums = []
    for col_tap in range(3):
        total = None
        for row_tap in range(3):
            tap = 3 * row_tap + col_tap
            part = every[:, 128 * tap : 128 * tap + 128]
            if row_tap == 0:
                part = earlier_rows(part)
            elif row_tap == 2:
                part = later_rows(part)
            total = part if total is None else total + part
        sums.append(total)
    left = jnp.where(inner, pltpu.roll(sums[0], 1, 0), 0.0)
    right = jnp.where(outer, pltpu.roll(sums[2], height - 1, 0), 0.0)
    return sums[1] + left + right


def spread_taps(gradient):
    height = gradient.shape[0]
    inner, outer = column_masks(height)
    by_column = [
        jnp.where(outer, pltpu.roll(gradient, height - 1, 0), 0.0),
        gradient,
        jnp.where(inner, pltpu.roll(gradient, 1, 0), 0.0),
    ]
    copies = [None] * 9
    for col_tap in range(3):
        copies[col_tap] = later_rows(by_column[col_tap])
        copies[3 + col_tap] = by_column[col_tap]
        copies[6 + col_tap] = earlier_rows(by_column[col_tap])
    return lanes([c.astype(BF) for c in copies])


def part_row(scalars, part):
    place = scalars[1] ^ part
    block = (place >> 1) ^ scalars[0]
    return place, pl.multiple_of(block * 128 + (place & 1) * 64, 64)


def begin_kernel(
    by_hand,
    x_any,
    gain_any,
    shift_any,
    conv_b_any,
    attn_b_any,
    proj_b_any,
    qkv_any,
    out_w_any,
    proj_any,
    act_ref,
    stats_ref,
    pack_ref,
    param_ref,
    x_ref,
    gain_ref,
    shift_ref,
    conv_b_ref,
    attn_b_ref,
    proj_b_ref,
    weights,
    proj_ref,
    proj,
    sems,
):
    place = lax.axis_index("dp").astype(jnp.int32) if by_hand else jnp.int32(0)
    own = pl.ds(pl.multiple_of(place * 64, 64), 64)
    block = pl.ds(pl.multiple_of((place >> 1) * 128, 128), 128)
    pairs = [
        (x_any, x_ref),
        (gain_any, gain_ref),
        (shift_any, shift_ref),
        (proj_any.at[:, block], proj_ref),
        (out_w_any.at[own, :], weights.at[3]),
        (conv_b_any, conv_b_ref),
        (attn_b_any, attn_b_ref),
        (proj_b_any, proj_b_ref),
    ] + [(qkv_any.at[m, own, :], weights.at[m]) for m in range(3)]
    copies = [
        pltpu.make_async_copy(source, target, sems.at[i])
        for i, (source, target) in enumerate(pairs)
    ]
    for copy in copies:
        copy.start()
    for copy in copies[:3]:
        copy.wait()
    normed, stats = moments(x_ref[...].astype(F32))
    pre = normed * gain_ref[0:1] + shift_ref[0:1]
    act_ref[...] = (pre * jax.nn.sigmoid(pre)).astype(BF)
    stats_ref[...] = stats
    for copy in copies[3:]:
        copy.wait()
    for m in range(4):
        pack_ref[:, 128 * m : 128 * m + 128] = weights[m]
    proj[...] = jnp.transpose(proj_ref[...].astype(F32))
    mine = proj[pl.ds(pl.multiple_of((place & 1) * 64, 64), 64), :]
    pack_ref[:, 512:640] = lanes([mine, jnp.zeros((64, 64), F32)]).astype(BF)
    rows = [gain_ref[m : m + 1] for m in range(3)] + [shift_ref[m : m + 1] for m in range(3)]
    rows += [conv_b_ref[m : m + 1] for m in range(2)] + [attn_b_ref[m : m + 1] for m in range(3)]
    rows += [lanes([proj_b_ref[...], jnp.zeros_like(proj_b_ref[...])])]
    param_ref[...] = pack_rows(rows, 16)


def code_column(codes):
    grid = rows_of([codes[m] for m in range(codes.shape[0])])
    height = grid.shape[0] * LAT
    high = grid >> 5
    both = lanes([high.astype(F32), (grid - (high << 5)).astype(F32)]).astype(BF)
    lines = lax.broadcasted_iota(jnp.int32, (height, grid.shape[0]), 0) >> 4
    own = (lines == lax.broadcasted_iota(jnp.int32, lines.shape, 1)).astype(F32).astype(BF)
    spread = dot(own, both)
    column = lax.broadcasted_iota(jnp.int32, (height, LAT), 0) & (LAT - 1)
    here = column == lax.broadcasted_iota(jnp.int32, (height, LAT), 1)
    merged = 32.0 * spread[:, :LAT] + spread[:, LAT:]
    return jnp.sum(jnp.where(here, merged, 0.0), axis=1, keepdims=True).astype(jnp.int32)


def start_kernel(scalars, codes_ref, book_ref, cot_ref, _, hot_ref, quant_ref, usage_ref, fixed_ref, start):
    tokens = hot_ref.shape[0]
    hot32 = (
        code_column(codes_ref[...]) == lax.broadcasted_iota(jnp.int32, (tokens, CODES), 1)
    ).astype(F32)
    hot = hot32.astype(BF)
    hot_ref[...] = hot
    counts = col_sum(hot32)
    usage_ref[...] = pack_rows([counts[:, 128 * i : 128 * i + 128] for i in range(8)])
    high, rest = split_low(book_ref[...])
    middle, low = split_low(rest)
    picked = dot_nt(hot, rows_of([high, middle, low]).astype(BF))
    width = book_ref.shape[0]
    quantized = picked[:, :width] + picked[:, width : 2 * width] + picked[:, 2 * width :]
    quant_ref[...] = quantized
    start[...] = cot_ref[...].astype(F32) - 2.0 * BETA * quantized
    for k in range(4):
        row = (scalars[0] ^ k) * 128
        one = start[pl.ds(pl.multiple_of(row, 64), 64), :]
        two = start[pl.ds(pl.multiple_of(row + 64, 64), 64), :]
        fixed_ref[k] = lanes([one, two]).astype(BF)


def lay_weights(scalars, own_ref, other_ref, o_ref):
    for part in range(PARTS):
        source = (own_ref if part % 2 == 0 else other_ref).at[part // 2]
        _, row = part_row(scalars, part)
        spot = pl.ds(row, 64)
        for k in range(4):
            for m in range(4):
                o_ref[spot, 512 * m + 128 * k : 512 * m + 128 * k + 128] = source[
                    k, :, 128 * m : 128 * m + 128
                ]
        for pair in range(2):
            o_ref[spot, 2048 + 128 * pair : 2176 + 128 * pair] = lanes(
                [source[2 * pair + i, :, 512:576] for i in range(2)]
            )


def conv_one_kernel(
    scalars, a0, a1, a2, a3, w_ref, param_ref, _, hidden_ref, stats_ref, act_ref
):
    pieces = [a0[...], a1[...], a2[...], a3[...]]
    hidden = conv_forward(pieces, w_ref, scalars[0]) + param(param_ref, CONV_BIAS)
    hidden_ref[...] = hidden
    normed, stats = moments(hidden)
    stats_ref[...] = stats
    pre = normed * param(param_ref, GAIN + 1) + param(param_ref, SHIFT + 1)
    act_ref[...] = (pre * jax.nn.sigmoid(pre)).astype(BF)


def conv_two_kernel(
    scalars, a0, a1, a2, a3, w_ref, param_ref, x_ref, fixed_ref, normed_ref, stats_ref, *pay_refs
):
    residual = x_ref[...].astype(F32) + (
        conv_forward([a0[...], a1[...], a2[...], a3[...]], w_ref, scalars[0])
        + param(param_ref, CONV_BIAS + 1)
    )
    normed, stats = moments(residual)
    normed_ref[...] = normed
    stats_ref[...] = stats
    gain, shift = param(param_ref, GAIN + 2), param(param_ref, SHIFT + 2)
    for k, ref in enumerate(pay_refs):
        target = scalars[0] ^ k
        own, other = target * 128, (target ^ 1) * 128
        ref[0:128] = (
            normed_ref[pl.ds(pl.multiple_of(other, 128), 128), :] * gain + shift
        ).astype(BF)
        high, low = split_low(normed_ref[pl.ds(pl.multiple_of(own, 128), 128), :])
        ref[128:256] = high.astype(BF)
        ref[256:384] = low.astype(BF)
        is_two = jnp.broadcast_to(target >> 1, (1, 128)) == 1
        mean = jnp.where(is_two, stats[1:2], stats[0:1])
        deviation = jnp.where(is_two, stats[5:6], stats[4:5])
        rows = list(split_low(mean)) + list(split_low(deviation))
        for index in (GAIN + 2, SHIFT + 2, ATTN_BIAS, ATTN_BIAS + 1, ATTN_BIAS + 2, PROJ_BIAS):
            rows.extend(split_low(param(param_ref, index)))
        ref[384:400] = pack_rows(rows, 16).astype(BF)
        ref[400:464] = fixed_ref[k]


def attn_in_kernel(scalars, n0, n1, n2, n3, norm_ref, residual_ref, bias_ref):
    pieces = [n0, n1, n2, n3]
    tails = [n[384:400].astype(F32) for n in pieces]

    def vector(index, width=128):
        row = 2 * index
        return lanes([t[row : row + 1, :width] + t[row + 1 : row + 2, :width] for t in tails])

    mean, deviation, gain, shift = [vector(index) for index in range(4)]
    empty = jnp.zeros((1, 256), F32)
    bias_ref[...] = pack_rows([vector(4), vector(5), vector(6), lanes([vector(7, 64), empty])])
    own = lanes([n[128:256].astype(F32) + n[256:384].astype(F32) for n in pieces])
    residual_ref[...] = own * deviation + mean
    norm_ref[0:128] = (own * gain + shift).astype(BF)
    norm_ref[128:POS] = lanes([n[0:128] for n in pieces])


def attention_kernel(
    scalars,
    norm_ref,
    residual_ref,
    bias_ref,
    n0,
    n1,
    n2,
    n3,
    own_ref,
    other_ref,
    usage_ref,
    *refs,
):
    pay_refs, keep_refs, send_ref = refs[:4], refs[4:8], refs[8]
    w_ref, grads, lat_grad_ref, sums_ref = refs[9:]
    lay_weights(scalars, own_ref, other_ref, w_ref)
    query_bias, value_bias, out_bias = [bias_ref[m : m + 1] for m in range(3)]
    proj_bias = bias_ref[3:4, 0:256]
    pieces = [n0, n1, n2, n3]
    normed = norm_ref[...]
    query = (dot(norm_ref[0:128], w_ref[:, 0:512]) + query_bias).astype(BF)
    keys = dot(normed, w_ref[:, 512:1024]).astype(BF)
    values = (dot(normed, w_ref[:, 1024:1536]) + value_bias).astype(BF)
    scores = dot_nt(query, keys) * SCORE_SCALE
    weights = jnp.exp(scores - jnp.max(scores, axis=1, keepdims=True))
    probs = weights / jnp.sum(weights, axis=1, keepdims=True)
    probs_low = probs.astype(BF)
    mixed = dot(probs_low, values).astype(BF)
    attended = dot(mixed, w_ref[:, 1536:2048]) + out_bias
    output = (residual_ref[...] + attended).astype(BF)
    latents = dot(output, w_ref[:, 2048:2304]) + proj_bias
    fixed = []
    for n in pieces:
        both = n[400:464].astype(F32)
        fixed.append(rows_of([both[:, :64], both[:, 64:]]))
    lat_grad = (lanes(fixed) + 2.0 * BETA * latents).astype(BF)
    blank = jnp.zeros((128, 64), BF)
    for k in range(4):
        lat_grad_ref[:, 128 * k : 128 * k + 128] = lanes([lat_grad[:, 64 * k : 64 * k + 64], blank])
    out_grad = dot_nt(lat_grad, w_ref[:, 2048:2304])
    att_grad = out_grad.astype(BF)
    mixed_grad = dot_nt(att_grad, w_ref[:, 1536:2048]).astype(BF)
    probs_grad = dot_nt(mixed_grad, values)
    row_dot = jnp.sum(probs * probs_grad, axis=1, keepdims=True)
    score_grad = (probs * (probs_grad - row_dot)).astype(BF)
    query_grad = (dot(score_grad, keys) * SCORE_SCALE).astype(BF)
    key_grad = (dot_tn(score_grad, query) * SCORE_SCALE).astype(BF)
    value_grad = dot_tn(probs_low, mixed_grad).astype(BF)
    upstream = dot_nt(key_grad, w_ref[:, 512:1024]) + dot_nt(value_grad, w_ref[:, 1024:1536])
    upstream_own = upstream[:128] + dot_nt(query_grad, w_ref[:, 0:512])
    for k in range(4):
        ref = pay_refs[k]
        ref[0:128] = upstream_own[:, 128 * k : 128 * k + 128].astype(ref.dtype)
        ref[128:POS] = upstream[128:, 128 * k : 128 * k + 128].astype(ref.dtype)
        ref[POS : POS + 128] = out_grad[:, 128 * k : 128 * k + 128].astype(ref.dtype)
        piece = latents[:, 64 * k : 64 * k + 64]
        ref[POS + 128 : POS + 192] = lanes([piece[:64], piece[64:]]).astype(ref.dtype)
    sums_ref[...] = pack_rows(
        [
            col_sum(query_grad.astype(F32)),
            col_sum(value_grad.astype(F32)),
            col_sum(att_grad.astype(F32)),
            lanes(
                [
                    part
                    for k in range(4)
                    for part in (
                        col_sum(lat_grad[:, 64 * k : 64 * k + 64].astype(F32)),
                        jnp.zeros((1, 64), F32),
                    )
                ]
            ),
        ]
    )
    grads[:, 0:512] = dot_tn(norm_ref[0:128], query_grad).astype(BF)
    grads[:, 512:1024] = dot_tn(normed, key_grad).astype(BF)
    grads[:, 1024:1536] = dot_tn(normed, value_grad).astype(BF)
    grads[:, 1536:2048] = dot_tn(mixed, att_grad).astype(BF)
    grads[:, 2048:2560] = dot_tn(output, lat_grad_ref[...]).astype(BF)
    right = lax.broadcasted_iota(jnp.int32, (16, 128), 1) >= 64

    def halves(vectors, offset):
        blank = jnp.zeros((1, 128), F32)
        entries = [blank] * offset
        for vector in vectors:
            entries += [pltpu.roll(vector, 64, 1), vector]
        return jnp.where(right, pack_rows(entries, 16), 0.0)

    biases = []
    for k in range(4):
        vectors = [sums_ref[m : m + 1, 128 * k : 128 * k + 128] for m in range(4)]
        biases.append(halves(vectors, 4))
    tens = jnp.floor(usage_ref[...] * (1.0 / 16.0))
    ones = usage_ref[...] - 16.0 * tens
    for part in range(PARTS):
        place, row = part_row(scalars, part)
        is_first = (jnp.broadcast_to(place, (16, 128)) == 0).astype(F32)
        here = jnp.broadcast_to(place, (8, 128)) == lax.broadcasted_iota(jnp.int32, (8, 128), 0)
        counts = [col_sum(jnp.where(here, digit, 0.0)) for digit in (tens, ones)]
        for k in range(4):
            ref = keep_refs[part // 2].at[k] if part % 2 == 0 else send_ref.at[part // 2, k]
            for m in range(4):
                ref[:, 128 * m : 128 * m + 128] = grads[
                    pl.ds(row, 64), 512 * m + 128 * k : 512 * m + 128 * k + 128
                ]
            extra = biases[k] * is_first
            if k == 0:
                extra = extra + halves(counts, 0)
            block = slice(2048 + 128 * k, 2176 + 128 * k)
            ref[0:16, 512:640] = (grads[pl.ds(row, 16), block].astype(F32) + extra).astype(BF)
            ref[16:64, 512:640] = grads[pl.ds(row + 16, 48), block]


def third_back_kernel(
    scalars,
    p0,
    p1,
    p2,
    p3,
    normed_ref,
    stats_ref,
    param_ref,
    _,
    w_ref,
    residual_ref,
    taps_ref,
    lat_ref,
    small_ref,
    q0,
    q1,
    q2,
    q3,
    up_ref,
    out_ref,
):
    z = scalars[0]
    for near, far, base in ((p0, p1, z), (p2, p3, z ^ 2)):
        first, second = near[0:POS].astype(F32), far[0:POS].astype(F32)
        up_ref[pl.ds(pl.multiple_of(base * 128, 128), 128), :] = first[:128] + second[128:]
        up_ref[pl.ds(pl.multiple_of((base ^ 1) * 128, 128), 128), :] = first[128:] + second[:128]
    for k, ref in enumerate((p0, p1, p2, p3)):
        row = (z ^ k) * 128
        out_ref[pl.ds(pl.multiple_of(row, 128), 128), :] = ref[POS : POS + 128].astype(F32)
        piece = ref[POS + 128 : POS + 192].astype(F32)
        lat_ref[pl.ds(pl.multiple_of(row, 64), 64), :] = piece[:, :64]
        lat_ref[pl.ds(pl.multiple_of(row + 64, 64), 64), :] = piece[:, 64:]
    source, gain_grad, shift_grad = norm_back(
        up_ref[...], normed_ref[...], stats_ref[...], param(param_ref, GAIN + 2)
    )
    residual = out_ref[...] + source
    residual_ref[...] = residual
    low = residual.astype(BF).astype(F32)
    small_ref[...] = pack_rows([gain_grad, shift_grad, col_sum(low)])
    send_taps(low, w_ref, scalars[0], taps_ref, (q0, q1, q2, q3))


def send_taps(gradient, w_ref, z, taps_ref, piece_refs):
    taps = spread_taps(gradient)
    taps_ref[...] = taps
    rows = []
    for k in range(4):
        block = pl.ds(pl.multiple_of((z ^ k) * 128, 128), 128)
        rows.append(lanes([w_ref[0, tap, block, :] for tap in range(9)]))
    every = dot_nt(taps, rows_of(rows))
    for k, ref in enumerate(piece_refs):
        ref[...] = every[:, 128 * k : 128 * k + 128].astype(ref.dtype)


def swish_back(gradient, normed, gain, shift):
    pre = normed * gain + shift
    gate = jax.nn.sigmoid(pre)
    return gradient * (gate * (1.0 + pre * (1.0 - gate)))


def second_back_kernel(
    scalars,
    p0,
    p1,
    p2,
    p3,
    hidden_ref,
    stats_ref,
    param_ref,
    _,
    __,
    a0,
    a1,
    a2,
    a3,
    w_ref,
    small_ref,
    q0,
    q1,
    q2,
    q3,
    *refs,
):
    keep_refs, send_ref, grads, taps_ref = refs[:4], refs[4], refs[5], refs[6]
    gradient = p0[...] + p1[...].astype(F32) + p2[...].astype(F32) + p3[...].astype(F32)
    stats = stats_ref[...]
    normed = renormed(hidden_ref[...], stats)
    gain = param(param_ref, GAIN + 1)
    upstream = swish_back(gradient, normed, gain, param(param_ref, SHIFT + 1))
    source, gain_grad, shift_grad = norm_back(upstream, normed, stats, gain)
    low = source.astype(BF).astype(F32)
    small_ref[...] = pack_rows([gain_grad, shift_grad, col_sum(low)])
    send_taps(low, w_ref, scalars[0], taps_ref, (q0, q1, q2, q3))
    full = lanes([a0[...], a1[...], a2[...], a3[...]])
    grads[...] = dot_tn(full, taps_ref[...]).astype(BF)
    for part in range(PARTS):
        _, row = part_row(scalars, part)
        value = grads[pl.ds(row, 64), :]
        if part % 2 == 0:
            keep_refs[part // 2][...] = value
        else:
            send_ref[part // 2] = value


def first_back_kernel(
    scalars,
    p0,
    p1,
    p2,
    p3,
    x_ref,
    stats_ref,
    param_ref,
    residual_ref,
    _,
    __,
    ___,
    grad_ref,
    small_ref,
):
    gradient = p0[...] + p1[...].astype(F32) + p2[...].astype(F32) + p3[...].astype(F32)
    stats = stats_ref[...]
    normed = renormed(x_ref[...].astype(F32), stats)
    gain = param(param_ref, GAIN)
    upstream = swish_back(gradient, normed, gain, param(param_ref, SHIFT))
    source, gain_grad, shift_grad = norm_back(upstream, normed, stats, gain)
    grad_ref[...] = residual_ref[...] + source
    small_ref[...] = pack_rows([gain_grad, shift_grad])


def conv_two_grad_kernel(
    scalars, a0, a1, a2, a3, taps_ref, hot_ref, lat_ref, quant_ref, reset_ref, scale, *refs
):
    keep_refs, send_ref, commit_ref, grads, book = refs[:4], refs[4], refs[5], refs[6], refs[7]
    full = lanes([a0[...], a1[...], a2[...], a3[...]])
    grads[...] = dot_tn(full, taps_ref[...]).astype(BF)
    latents = lat_ref[...]
    difference = latents - quant_ref[...]
    commit_ref[...] = pack_rows([lanes([col_sum(difference * difference), jnp.zeros((1, 64), F32)])])
    high, low = split_low(difference * (-scale))
    sums = dot_tn(lanes([high, low]).astype(BF), hot_ref[...])
    tokens = latents.shape[0]
    where = reset_ref[...] - scalars[2] * tokens
    chosen = (where == lax.broadcasted_iota(jnp.int32, (tokens, CODES), 0)).astype(F32).astype(BF)
    picked = dot_tn(latents.astype(BF), chosen)
    book[0:64] = (sums[:64] + sums[64:]).astype(BF)
    book[64:128] = picked.astype(BF)
    for part in range(PARTS):
        place, row = part_row(scalars, part)
        ref = keep_refs[part // 2] if part % 2 == 0 else send_ref.at[part // 2]
        ref[:, 0:WIDE] = grads[pl.ds(row, 64), :]
        column = pl.ds(pl.multiple_of(place * 128, 128), 128)
        ref[:, WIDE : WIDE + 128] = book[0:64, column]
        ref[:, WIDE + 128 : WIDE + 256] = book[64:128, column]


def finish_two_kernel(scalars, own_ref, other_ref, conv_ref, book_grad_ref, picked_ref):
    for part in range(PARTS):
        source = (own_ref if part % 2 == 0 else other_ref).at[part // 2]
        place = scalars[1] ^ part
        rows = pl.ds(pl.multiple_of(place * 64, 64), 64)
        for tap in range(9):
            conv_ref[0, tap, rows, :] = source[:, 128 * tap : 128 * tap + 128].astype(F32)
        column = pl.ds(pl.multiple_of(place * 128, 128), 128)
        book_grad_ref[:, column] = source[:, WIDE : WIDE + 128].astype(F32)
        picked_ref[:, column] = source[:, WIDE + 128 : WIDE + 256].astype(F32)


def finish_last_kernel(
    tokens_all,
    scalars,
    own_ref,
    other_ref,
    picked,
    book_ref,
    held_ref,
    conv_ref,
    gain_ref,
    shift_ref,
    bias_ref,
    commit_ref,
    qkv_ref,
    out_w_ref,
    proj_ref,
    new_book_ref,
    perplexity_ref,
    attn_bias_ref,
    proj_bias_ref,
    usage,
    proj,
):
    extra_sum = jnp.zeros((16, 128), F32)
    total = jnp.zeros((9, 128), F32)
    for part in range(PARTS):
        source = (own_ref if part % 2 == 0 else other_ref).at[part // 2]
        place = scalars[1] ^ part
        rows = pl.ds(pl.multiple_of(place * 64, 64), 64)
        for tap in range(9):
            conv_ref[0, tap, rows, :] = source[:, 128 * tap : 128 * tap + 128].astype(F32)
        for m in range(3):
            qkv_ref[m, rows, :] = source[:, 1152 + 128 * m : 1280 + 128 * m].astype(F32)
        out_w_ref[rows, :] = source[:, 1536:1664].astype(F32)
        proj[rows, :] = source[:, 1664:1792].astype(F32)
        extra = source[0:16, 1664:1792].astype(F32)
        extra_sum = extra_sum + extra
        usage[pl.ds(place, 1), :] = lanes(
            [
                16.0 * extra[0:1, 64:] + extra[2:3, 64:],
                16.0 * extra[1:2, 64:] + extra[3:4, 64:],
            ]
        )
        both = source[16:64, 1728:1792].astype(F32)
        both = both[0:18] + both[18:36]
        total = total + lanes([both[0:9], both[9:18]])
    for index, row in enumerate((0, 2, 5)):
        gain_ref[index : index + 1] = total[row : row + 1]
        shift_ref[index : index + 1] = total[row + 1 : row + 2]
    bias_ref[0:1] = total[4:5]
    bias_ref[1:2] = total[7:8]
    commit_ref[...] = total[8:9, :64] * (1.0 / tokens_all)
    proj_ref[...] = jnp.transpose(proj[...])[0:64]
    counts = usage[...]
    share = counts * (1.0 / tokens_all)
    terms = share * jnp.log(jnp.maximum(share, 1.0 / tokens_all))
    entropy = jnp.sum(jnp.sum(terms, axis=1, keepdims=True), axis=0, keepdims=True)
    perplexity_ref[...] = jnp.exp(-entropy)
    for block in range(8):
        spot = slice(128 * block, 128 * block + 128)
        new_book_ref[:, spot] = jnp.where(
            counts[block : block + 1] > 0.5, book_ref[:, spot], picked[:, spot]
        )
    for m in range(3):
        attn_bias_ref[m : m + 1] = lanes(
            [extra_sum[4 + 2 * m : 5 + 2 * m, 64:], extra_sum[5 + 2 * m : 6 + 2 * m, 64:]]
        )
    proj_bias_ref[...] = extra_sum[10:11, 64:]


def pair_add_kernel(scalars, k0, k1, k2, k3, get_ref, _, keep_ref, send_ref):
    for i, ref in enumerate((k0, k1, k2, k3)):
        target = (send_ref if i % 2 else keep_ref).at[i // 2]
        target[...] = plus(ref[...], get_ref[i])


def plus(first, second):
    return (first.astype(F32) + second.astype(F32)).astype(BF)


def half_add_kernel(scalars, keep_ref, get_ref, _, own_ref, send_ref):
    own_ref[...] = plus(keep_ref[0], get_ref[0])
    send_ref[...] = plus(keep_ref[1], get_ref[1])


def attn_sum_kernel(scalars, a0, a1, _, keep_ref, send_ref):
    for k in range(4):
        (send_ref if k % 2 else keep_ref)[k // 2] = plus(a0[k], a1[k])


def half_pass_kernel(scalars, keep_ref, get_ref, _, a0, a1, a2, own_ref, send_ref, b0, b1, b2):
    half_add_kernel(scalars, keep_ref, get_ref, _, own_ref, send_ref)
    for source, target in ((a0, b0), (a1, b1), (a2, b2)):
        target[...] = source[...]


def add_kernel(scalars, k0, k1, k2, k3, get_ref, _, *sum_refs):
    for i, ref in enumerate((k0, k1, k2, k3)):
        sum_refs[i][...] = plus(ref[...], get_ref[i])


def two_sum_kernel(scalars, a0, a1, _, sum_ref):
    sum_ref[...] = plus(a0[...], a1[...])


def last_kernel(
    scalars, o0, o1, o2, o3, att_own, att_get, small_one, small_two, small_three, commit, last_ref
):
    total = o0[...].astype(F32)
    for ref in (o1, o2, o3):
        total = total + ref[...].astype(F32)
    last_ref[:, 0:WIDE] = total.astype(BF)
    last_ref[:, 1152:1664] = plus(att_own[:, 0:512], att_get[:, 0:512])
    rows = [small_one[0:1], small_one[1:2]]
    rows += [small_two[m : m + 1] for m in range(3)]
    rows += [small_three[m : m + 1] for m in range(3)]
    rows += [commit[0:1]]
    high, low = split_low(pack_rows(rows, 16))
    blank = jnp.zeros((48, 64), F32)
    small = rows_of([high[:9, :64], high[:9, 64:], low[:9, :64], low[:9, 64:], jnp.zeros((12, 64), F32)])
    small = lanes([blank, small])
    block = att_own[:, 512:640].astype(F32) + att_get[:, 512:640].astype(F32)
    last_ref[0:16, 1664:1792] = block[0:16].astype(BF)
    last_ref[16:64, 1664:1792] = (block[16:64] + small).astype(BF)


def stack_kernel(scalars, *refs):
    out_ref = refs[-1]
    for k in range(out_ref.shape[0]):
        out_ref[k] = refs[k][...]


def over(axis, array, flip):
    size = lax.axis_size(axis)
    return lax.ppermute(array, axis, [(i, i ^ flip) for i in range(size)])


def flips(array):
    return [over("chan", array, k) for k in (1, 2, 3)]


def plane(array):
    return [array] + [over("dp", array, k) for k in (2, 4, 6)]


def add(*arrays):
    total = arrays[0].astype(F32)
    for array in arrays[1:]:
        total = total + array.astype(F32)
    return total.astype(BF)


def shards(
    latents_in,
    norm_gains,
    norm_shifts,
    conv_weights,
    conv_biases,
    qkv_weights,
    attn_biases,
    out_weight,
    proj_weight,
    proj_bias,
    codebook,
    codes,
    reset_src,
    cotangent,
):
    images = latents_in.shape[0]
    tokens = images * POS
    quarter = tokens // 4
    devices = lax.axis_size("dp")
    tokens_all = tokens * devices
    by_hand = devices == PARTS
    z = lax.axis_index("chan").astype(jnp.int32)
    dp = lax.axis_index("dp").astype(jnp.int32)
    scalars = jnp.stack([z, dp if by_hand else jnp.zeros_like(dp), dp, jnp.zeros_like(dp)])
    x = latents_in.reshape(tokens, 128)
    conv_w = conv_weights.reshape(2, 9, C, 128)

    def whole(shape):
        return pl.BlockSpec(shape, lambda i, n=len(shape): (0,) * n)

    def blocks_call(body, in_specs, out_specs, outs, name, *args, scratch=(), aliases={}):
        return pl.pallas_call(
            body,
            grid=(1,),
            out_shape=outs,
            in_specs=[pl.BlockSpec(memory_space=pltpu.SMEM)] + in_specs,
            out_specs=out_specs,
            scratch_shapes=scratch,
            input_output_aliases=aliases,
            compiler_params=pltpu.CompilerParams(vmem_limit_bytes=VMEM * 2**20),
            cost_estimate=pl.CostEstimate(flops=HEAVY, bytes_accessed=1, transcendentals=0),
            name=name,
        )(scalars, *args)

    anywhere = pl.BlockSpec(memory_space=pl.ANY)

    def begin(*refs):
        begin_kernel(by_hand, *refs)

    act_one, stats_one, pack, params = pl.pallas_call(
        begin,
        out_shape=[
            sds((tokens, 128), BF),
            sds((8, 128), F32),
            sds((64, 640), BF),
            sds((16, 128), F32),
        ],
        in_specs=[anywhere] * 9,
        out_specs=[pl.BlockSpec(memory_space=pltpu.VMEM)] * 4,
        scratch_shapes=[
            pltpu.VMEM((tokens, 128), BF),
            pltpu.VMEM((3, 128), F32),
            pltpu.VMEM((3, 128), F32),
            pltpu.VMEM((2, 128), F32),
            pltpu.VMEM((3, 128), F32),
            pltpu.VMEM((1, 64), F32),
            pltpu.VMEM((4, 64, 128), BF),
            pltpu.VMEM((64, 128), BF),
            pltpu.VMEM((128, 64), F32),
            pltpu.SemaphoreType.DMA((11,)),
        ],
        compiler_params=pltpu.CompilerParams(vmem_limit_bytes=60 * 2**20),
        cost_estimate=pl.CostEstimate(flops=HEAVY, bytes_accessed=1, transcendentals=0),
        name="begin",
    )(
        x,
        norm_gains,
        norm_shifts,
        conv_biases,
        attn_biases,
        proj_bias.reshape(1, 64),
        qkv_weights,
        out_weight,
        proj_weight.T,
    )
    pieces_one = [act_one] + flips(act_one)
    packs = [pack] + flips(pack)
    hot, quantized, usage, fixed = call(
        start_kernel,
        [
            sds((tokens, CODES), BF),
            sds((tokens, 64), F32),
            sds((8, 128), F32),
            sds((4, 64, 128), BF),
        ],
        scalars,
        codes,
        codebook.T,
        cotangent.reshape(tokens, 64),
        stats_one,
        scratch=[pltpu.VMEM((tokens, 64), F32)],
        name="start",
    )
    def conv_call(body, index, outs, name, *args):
        specs = []
        for a in args:
            if a is conv_w:
                specs.append(pl.BlockSpec((1, 9, C, 128), lambda i: (index, 0, 0, 0)))
            else:
                specs.append(whole(a.shape))
        scratch = ()
        if body is third_back_kernel:
            scratch = [pltpu.VMEM((tokens, 128), F32), pltpu.VMEM((tokens, 128), F32)]
        if body is second_back_kernel:
            scratch = [pltpu.VMEM((C, WIDE), BF), pltpu.VMEM((tokens, WIDE), BF)]
        return blocks_call(
            body, specs, [whole(o.shape) for o in outs], outs, name, *args, scratch=scratch
        )

    hidden, stats_two, act_two = conv_call(
        conv_one_kernel,
        0,
        [sds((tokens, 128), F32), sds((8, 128), F32), sds((tokens, 128), BF)],
        "conv_one",
        *pieces_one,
        conv_w,
        params,
        usage,
    )
    pieces_two = [act_two] + flips(act_two)
    if by_hand:
        block = call(
            stack_kernel,
            [sds((4, 64, 640), BF)],
            scalars,
            *packs,
            flops=HEAVY,
            name="pack_join",
        )[0]
        blocks = [block] + [over("dp", block, k) for k in (2, 4, 6)]
    else:
        packed = jnp.concatenate(
            [qkv_weights[0], qkv_weights[1], qkv_weights[2], out_weight, proj_weight]
            + [jnp.zeros((C, 64), BF)],
            axis=1,
        )
        block = jnp.stack([packed] + flips(packed)).reshape(4, PARTS, 64, 640)
        block = jnp.swapaxes(block, 0, 1)
        block_own, block_other = block[0::2], block[1::2]
    normed_three, stats_three, *pays = conv_call(
        conv_two_kernel,
        1,
        [sds((tokens, 128), F32), sds((8, 128), F32)] + [sds((464, 128), BF)] * 4,
        "conv_two",
        *pieces_two,
        conv_w,
        params,
        x,
        fixed,
    )
    normed_pieces = [pays[0]] + [over("chan", pays[k], k) for k in (1, 2, 3)]
    if by_hand:
        block_own = call(
            stack_kernel,
            [sds((4, 4, 64, 640), BF)],
            scalars,
            *blocks,
            name="pack_plane",
        )[0]
        block_other = over("dp", block_own, 1)
    normed, residual_part, bias_rows = call(
        attn_in_kernel,
        [sds((POS, C), BF), sds((quarter, C), F32), sds((8, C), F32)],
        scalars,
        *normed_pieces,
        flops=HEAVY,
        name="attn_in",
    )
    *pays, k0, k1, k2, k3, att_send = call(
        attention_kernel,
        [sds((POS + 192, 128), F32)]
        + [sds((POS + 192, 128), BF)] * 3
        + [sds((4, 64, 640), BF)] * 4
        + [sds((4, 4, 64, 640), BF)],
        scalars,
        normed,
        residual_part,
        bias_rows,
        *normed_pieces,
        block_own,
        block_other,
        usage,
        scratch=[
            pltpu.VMEM((C, 2304), BF),
            pltpu.VMEM((C, 2560), BF),
            pltpu.VMEM((quarter, C), BF),
            pltpu.VMEM((8, C), F32),
        ],
        flops=HEAVY,
        name="attention",
    )
    att_keep = [k0, k1, k2, k3]

    back_three = [pays[0]] + [over("chan", pays[k], k) for k in (1, 2, 3)]
    def pair_sum(keep, send, after, name):
        outs = [sds((2,) + keep[0].shape, BF)] * 2
        got = over("dp", send, 1)
        kept, sent = call(pair_add_kernel, outs, scalars, *keep, got, after, name=name)
        return kept, over("dp", sent, 2)

    if by_hand:
        att_kept, att_got = pair_sum(att_keep, att_send, back_three[1], "attn_pair")
    residual_grad, taps_two, latents, small_three, *pays = conv_call(
        third_back_kernel,
        1,
        [
            sds((tokens, 128), F32),
            sds((tokens, WIDE), BF),
            sds((tokens, 64), F32),
            sds((8, 128), F32),
            sds((tokens, 128), F32),
        ]
        + [sds((tokens, 128), BF)] * 3,
        "third_back",
        *back_three,
        normed_three,
        stats_three,
        params,
        att_kept if by_hand else bias_rows,
        conv_w,
    )
    back_two = [pays[0]] + [over("chan", pays[k], k) for k in (1, 2, 3)]
    book_scale = 2.0 * CODES / tokens_all

    def two_grad(*refs):
        conv_two_grad_kernel(*refs[:10], book_scale, *refs[10:])

    *two_keep, two_send, commit = call(
        two_grad,
        [sds((64, 1408), BF)] * 4 + [sds((4, 64, 1408), BF), sds((8, 128), F32)],
        scalars,
        *pieces_two,
        taps_two,
        hot,
        latents,
        quantized,
        reset_src.reshape(1, CODES),
        scratch=[pltpu.VMEM((C, WIDE), BF), pltpu.VMEM((128, CODES), BF)],
        name="conv_two_grad",
    )
    if by_hand:
        att_own, att_sent = call(
            half_add_kernel,
            [sds((4, 64, 640), BF)] * 2,
            scalars,
            att_kept,
            att_got,
            small_three,
            flops=HEAVY,
            name="attn_half",
        )
        att_got = over("dp", att_sent, 4)
        two_kept, two_got = pair_sum(two_keep, two_send, att_own, "conv_two_pair")
    small_two, *pays = conv_call(
        second_back_kernel,
        0,
        [sds((8, 128), F32), sds((tokens, 128), F32)]
        + [sds((tokens, 128), BF)] * 3
        + [sds((64, WIDE), BF)] * 4
        + [sds((4, 64, WIDE), BF)],
        "second_back",
        *back_two,
        hidden,
        stats_two,
        params,
        att_own if by_hand else bias_rows,
        two_kept if by_hand else bias_rows,
        *pieces_one,
        conv_w,
    )
    *one_keep, one_send = pays[4:]
    pays = pays[:4]
    one_got = over("dp", one_send, 1) if by_hand else one_send
    if by_hand:
        att_kept, att_sent = call(
            attn_sum_kernel,
            [sds((2, 64, 640), BF)] * 2,
            scalars,
            att_own,
            att_got,
            small_two,
            name="attn_sum",
        )
        att_got = over("chan", att_sent, 1)
        two_own, two_sent, *pays[1:] = call(
            half_pass_kernel,
            [sds((64, 1408), BF)] * 2 + [sds((tokens, 128), BF)] * 3,
            scalars,
            two_kept,
            two_got,
            att_kept,
            *pays[1:],
            flops=HEAVY,
            name="conv_two_half",
        )
        two_got = over("dp", two_sent, 4)
        one_parts = call(
            add_kernel,
            [sds((64, WIDE), BF)] * 4,
            scalars,
            *one_keep,
            one_got,
            att_kept,
            name="conv_one_add",
        )
        one_parts = [one_parts[0]] + [over("dp", one_parts[i], 2 * i) for i in (1, 2, 3)]
        att_own, att_sent = call(
            half_add_kernel,
            [sds((64, 640), BF)] * 2,
            scalars,
            att_kept,
            att_got,
            two_own,
            name="attn_last",
        )
        att_got = over("chan", att_sent, 2)
        two = call(
            two_sum_kernel,
            [sds((64, 1408), BF)],
            scalars,
            two_own,
            two_got,
            one_parts[0],
            name="conv_two_sum",
        )[0]
    back_one = [pays[0]] + [over("chan", pays[k], k) for k in (1, 2, 3)]
    grad_latents, small_one = call(
        first_back_kernel,
        [sds((tokens, 128), F32), sds((8, 128), F32)],
        scalars,
        *back_one,
        x,
        stats_one,
        params,
        residual_grad,
        one_parts[0] if by_hand else bias_rows,
        two if by_hand else bias_rows,
        att_own if by_hand else bias_rows,
        flops=HEAVY,
        name="first_back",
    )

    if by_hand:
        last = call(
            last_kernel,
            [sds((64, 1792), BF)],
            scalars,
            *one_parts,
            att_own,
            att_got,
            small_one,
            small_two,
            small_three,
            commit,
            flops=HEAVY,
            name="last",
        )[0]

        def chip(array, name, *after, flops=0):
            parts = plane(array)
            outs = [sds((4,) + array.shape, BF)]
            return call(stack_kernel, outs, scalars, *parts, *after, flops=flops, name=name)[0]

        two_own = chip(two, "stack_two", last, flops=HEAVY)
        two_other = over("dp", two_own, 1)
        last_own = chip(last, "stack_last", flops=HEAVY)
        last_other = over("dp", last_own, 1)
    else:

        def total(keep, send):
            parts = jnp.stack([jnp.stack(keep), send]).astype(F32)
            return lax.psum(parts, "dp").astype(BF)

        att_sum = total(att_keep, att_send)
        att_sum = add(att_sum[:, :, 0], *[over("chan", att_sum[:, :, k], k) for k in (1, 2, 3)])
        small = jnp.concatenate([small_one[0:2], small_two[0:3], small_three[0:3], commit[0:1]])
        small = jnp.concatenate([lax.psum(small, "dp"), jnp.zeros((7, 128), F32)])
        high = lax.reduce_precision(small, 8, 7)
        halves = [v[:9, c : c + 64] for v in (high, small - high) for c in (0, 64)]
        smalls = jnp.concatenate(halves + [jnp.zeros((12, 64), F32)]).astype(BF)
        att_sum = att_sum.at[0, 0, 16:64, 576:640].add(smalls)
        two_own, two_other = total(two_keep, two_send)
        one_sum = total(one_keep, one_send)
        last_own, last_other = jnp.concatenate([one_sum, att_sum], axis=3)

    conv_held, book_grad, picked = blocks_call(
        finish_two_kernel,
        [whole((4, 64, 1408)), whole((4, 64, 1408))],
        [
            pl.BlockSpec((1, 9, C, 128), lambda i: (1, 0, 0, 0)),
            whole((64, CODES)),
            whole((64, CODES)),
        ],
        [sds((2, 9, C, 128), F32), sds((64, CODES), F32), sds((64, CODES), F32)],
        "finish_two",
        two_own,
        two_other,
    )

    def finish_last(*refs):
        finish_last_kernel(float(tokens_all), *refs)

    outs = [
        sds((2, 9, C, 128), F32),
        sds((3, 128), F32),
        sds((3, 128), F32),
        sds((2, 128), F32),
        sds((1, 64), F32),
        sds((3, C, 128), F32),
        sds((C, 128), F32),
        sds((64, C), F32),
        sds((64, CODES), F32),
        sds((1, 1), F32),
        sds((3, 128), F32),
        sds((1, 64), F32),
    ]
    (
        conv_grad,
        gain_grad,
        shift_grad,
        conv_bias_grad,
        commitment,
        qkv_grad,
        out_grad,
        proj_grad,
        new_codebook,
        perplexity,
        attn_bias_grad,
        proj_bias_grad,
    ) = blocks_call(
        finish_last,
        [whole((4, 64, 1792)), whole((4, 64, 1792)), whole((64, CODES)), whole((64, CODES))]
        + [pl.BlockSpec(memory_space=pl.ANY)],
        [pl.BlockSpec((1, 9, C, 128), lambda i: (0, 0, 0, 0))] + [whole(o.shape) for o in outs[1:]],
        outs,
        "finish_last",
        last_own,
        last_other,
        picked,
        codebook.T,
        conv_held,
        scratch=[pltpu.VMEM((8, 128), F32), pltpu.VMEM((C, 128), F32)],
        aliases={5: 0},
    )

    return (
        latents.reshape(images, LAT, LAT, -1),
        commitment.reshape(64),
        perplexity.reshape(()),
        new_codebook.T,
        grad_latents.reshape(images, LAT, LAT, 128),
        gain_grad,
        shift_grad,
        conv_grad.reshape(2, 3, 3, C, 128),
        conv_bias_grad,
        qkv_grad,
        attn_bias_grad,
        out_grad,
        proj_grad.T,
        proj_bias_grad.reshape(64),
        book_grad.T,
    )


def solution(mesh):
    return jax.shard_map(
        shards,
        mesh=mesh,
        in_specs=(
            P("dp", None, None, "chan"),
            P(None, "chan"),
            P(None, "chan"),
            P(None, None, None, None, "chan"),
            P(None, "chan"),
            P(None, None, "chan"),
            P(None, "chan"),
            P(None, "chan"),
            P(None, "chan"),
            P("chan"),
            P(None, "chan"),
            P("dp", None, None),
            P(),
            P("dp", None, None, "chan"),
        ),
        out_specs=(
            P("dp", None, None, "chan"),
            P("chan"),
            P(),
            P(None, "chan"),
            P("dp", None, None, "chan"),
            P(None, "chan"),
            P(None, "chan"),
            P(None, None, None, None, "chan"),
            P(None, "chan"),
            P(None, None, "chan"),
            P(None, "chan"),
            P(None, "chan"),
            P(None, "chan"),
            P("chan"),
            P(None, "chan"),
        ),
        check_vma=False,
    )
```

```python
import jax
import jax.numpy as jnp
from jax import lax
from jax.experimental import pallas as pl
from jax.experimental.pallas import tpu as pltpu
from jax.sharding import PartitionSpec as P

F32 = jnp.float32
BF = jnp.bfloat16
C = 512
CODES = 1024
LAT = 16
POS = LAT * LAT
EPSILON = 1e-06
BETA = 0.25
SCORE_SCALE = float(C) ** (-0.5)
GROUP_COUNT = float(POS * 16)
WIDE = 1152
VMEM = 20
HEAVY = 10**11
PARTS = 8


def call(body, outs, *args, scratch=(), flops=0, name=None, space=pltpu.VMEM):
    result = pl.pallas_call(
        body,
        out_shape=list(outs),
        in_specs=[pl.BlockSpec(memory_space=pltpu.SMEM)]
        + [pl.BlockSpec(memory_space=space)] * (len(args) - 1),
        out_specs=[pl.BlockSpec(memory_space=pltpu.VMEM)] * len(outs),
        scratch_shapes=list(scratch),
        compiler_params=pltpu.CompilerParams(vmem_limit_bytes=VMEM * 2**20),
        cost_estimate=pl.CostEstimate(flops=flops, bytes_accessed=1, transcendentals=0),
        name=name,
    )(*args)
    return result


def sds(shape, dtype):
    return jax.ShapeDtypeStruct(shape, dtype)


def dot(a, b):
    return jnp.dot(a, b, preferred_element_type=F32)


def dot_nt(a, b):
    return lax.dot_general(a, b, (((1,), (1,)), ((), ())), preferred_element_type=F32)


def dot_tn(a, b):
    return lax.dot_general(a, b, (((0,), (0,)), ((), ())), preferred_element_type=F32)


def lanes(parts):
    return jnp.concatenate(parts, axis=1)


def rows_of(parts):
    return jnp.concatenate(parts, axis=0)


def pack_rows(vectors, height=8):
    width = vectors[0].shape[1]
    spot = lax.broadcasted_iota(jnp.int32, (height, width), 0)
    result = jnp.zeros((height, width), F32)
    for index, vector in enumerate(vectors):
        result = jnp.where(spot == index, vector, result)
    return result


def split_low(values):
    high = values.astype(BF).astype(F32)
    return high, values - high


def group_sums(rows):
    first = lax.broadcasted_iota(jnp.int32, (128, 128), 0) >> 4
    second = lax.broadcasted_iota(jnp.int32, (128, 128), 1) >> 4
    ones = (first == second).astype(F32).astype(BF)
    high, rest = split_low(rows)
    middle, low = split_low(rest)
    stacked = rows_of([high, middle, low, jnp.zeros_like(high)]).astype(BF)
    summed = dot(stacked, ones)
    return summed[0:8] + summed[8:16] + summed[16:24]


def col_sum(values):
    return jnp.sum(values, axis=0, keepdims=True)


def moments(values):
    one, two = values[:POS], values[POS:]
    mean = group_sums(pack_rows([col_sum(one), col_sum(two)])) * (1.0 / GROUP_COUNT)
    one, two = one - mean[0:1], two - mean[1:2]
    variance = group_sums(pack_rows([col_sum(one * one), col_sum(two * two)])) * (
        1.0 / GROUP_COUNT
    )
    inverse = lax.rsqrt(variance + EPSILON)
    deviation = jnp.sqrt(variance + EPSILON)
    normed = rows_of([one * inverse[0:1], two * inverse[1:2]])
    stats = pack_rows(
        [mean[0:1], mean[1:2], inverse[0:1], inverse[1:2], deviation[0:1], deviation[1:2]]
    )
    return normed, stats


def renormed(values, stats):
    return rows_of(
        [
            (values[:POS] - stats[0:1]) * stats[2:3],
            (values[POS:] - stats[1:2]) * stats[3:4],
        ]
    )


def norm_back(upstream, normed, stats, gain):
    sides = [(upstream[:POS], normed[:POS]), (upstream[POS:], normed[POS:])]
    plain = [col_sum(u) for u, _ in sides]
    weighted = [col_sum(u * n) for u, n in sides]
    means = group_sums(
        pack_rows([plain[0] * gain, plain[1] * gain, weighted[0] * gain, weighted[1] * gain])
    ) * (1.0 / GROUP_COUNT)
    parts = [
        stats[2 + m : 3 + m] * (u * gain - means[m : m + 1] - n * means[2 + m : 3 + m])
        for m, (u, n) in enumerate(sides)
    ]
    return rows_of(parts), weighted[0] + weighted[1], plain[0] + plain[1]


GAIN, SHIFT, CONV_BIAS, ATTN_BIAS, PROJ_BIAS = 0, 3, 6, 8, 11


def param(ref, index):
    return ref[index : index + 1]


def column_masks(height):
    column = lax.broadcasted_iota(jnp.int32, (height, 128), 0) & (LAT - 1)
    return column >= 1, column <= LAT - 2


def later_rows(values):
    blank = jnp.zeros((LAT, values.shape[1]), values.dtype)
    return rows_of([values[LAT:POS], blank, values[POS + LAT :], blank])


def earlier_rows(values):
    blank = jnp.zeros((LAT, values.shape[1]), values.dtype)
    return rows_of([blank, values[: POS - LAT], blank, values[POS : 2 * POS - LAT]])


def conv_forward(pieces, w_ref, z):
    full = lanes(pieces)
    height = full.shape[0]
    inner, outer = column_masks(height)
    blocks = [pl.ds(pl.multiple_of((z ^ k) * 128, 128), 128) for k in range(4)]
    weights = lanes(
        [rows_of([w_ref[0, tap, block, :] for block in blocks]) for tap in range(9)]
    )
    every = dot(full, weights)
    sums = []
    for col_tap in range(3):
        total = None
        for row_tap in range(3):
            tap = 3 * row_tap + col_tap
            part = every[:, 128 * tap : 128 * tap + 128]
            if row_tap == 0:
                part = earlier_rows(part)
            elif row_tap == 2:
                part = later_rows(part)
            total = part if total is None else total + part
        sums.append(total)
    left = jnp.where(inner, pltpu.roll(sums[0], 1, 0), 0.0)
    right = jnp.where(outer, pltpu.roll(sums[2], height - 1, 0), 0.0)
    return sums[1] + left + right


def spread_taps(gradient):
    height = gradient.shape[0]
    inner, outer = column_masks(height)
    by_column = [
        jnp.where(outer, pltpu.roll(gradient, height - 1, 0), 0.0),
        gradient,
        jnp.where(inner, pltpu.roll(gradient, 1, 0), 0.0),
    ]
    copies = [None] * 9
    for col_tap in range(3):
        copies[col_tap] = later_rows(by_column[col_tap])
        copies[3 + col_tap] = by_column[col_tap]
        copies[6 + col_tap] = earlier_rows(by_column[col_tap])
    return lanes([c.astype(BF) for c in copies])


def part_row(scalars, part):
    place = scalars[1] ^ part
    block = (place >> 1) ^ scalars[0]
    return place, pl.multiple_of(block * 128 + (place & 1) * 64, 64)


def begin_kernel(
    by_hand,
    x_any,
    gain_any,
    shift_any,
    conv_b_any,
    attn_b_any,
    proj_b_any,
    qkv_any,
    out_w_any,
    proj_any,
    act_ref,
    stats_ref,
    pack_ref,
    param_ref,
    x_ref,
    gain_ref,
    shift_ref,
    conv_b_ref,
    attn_b_ref,
    proj_b_ref,
    weights,
    proj_ref,
    proj,
    sems,
):
    place = lax.axis_index("dp").astype(jnp.int32) if by_hand else jnp.int32(0)
    own = pl.ds(pl.multiple_of(place * 64, 64), 64)
    block = pl.ds(pl.multiple_of((place >> 1) * 128, 128), 128)
    pairs = [
        (x_any, x_ref),
        (gain_any, gain_ref),
        (shift_any, shift_ref),
        (proj_any.at[:, block], proj_ref),
        (out_w_any.at[own, :], weights.at[3]),
        (conv_b_any, conv_b_ref),
        (attn_b_any, attn_b_ref),
        (proj_b_any, proj_b_ref),
    ] + [(qkv_any.at[m, own, :], weights.at[m]) for m in range(3)]
    copies = [
        pltpu.make_async_copy(source, target, sems.at[i])
        for i, (source, target) in enumerate(pairs)
    ]
    for copy in copies:
        copy.start()
    for copy in copies[:3]:
        copy.wait()
    normed, stats = moments(x_ref[...].astype(F32))
    pre = normed * gain_ref[0:1] + shift_ref[0:1]
    act_ref[...] = (pre * jax.nn.sigmoid(pre)).astype(BF)
    stats_ref[...] = stats
    for copy in copies[3:]:
        copy.wait()
    for m in range(4):
        pack_ref[:, 128 * m : 128 * m + 128] = weights[m]
    proj[...] = jnp.transpose(proj_ref[...].astype(F32))
    mine = proj[pl.ds(pl.multiple_of((place & 1) * 64, 64), 64), :]
    pack_ref[:, 512:640] = lanes([mine, jnp.zeros((64, 64), F32)]).astype(BF)
    rows = [gain_ref[m : m + 1] for m in range(3)] + [shift_ref[m : m + 1] for m in range(3)]
    rows += [conv_b_ref[m : m + 1] for m in range(2)] + [attn_b_ref[m : m + 1] for m in range(3)]
    rows += [lanes([proj_b_ref[...], jnp.zeros_like(proj_b_ref[...])])]
    param_ref[...] = pack_rows(rows, 16)


def code_column(codes):
    grid = rows_of([codes[m] for m in range(codes.shape[0])])
    height = grid.shape[0] * LAT
    high = grid >> 5
    both = lanes([high.astype(F32), (grid - (high << 5)).astype(F32)]).astype(BF)
    lines = lax.broadcasted_iota(jnp.int32, (height, grid.shape[0]), 0) >> 4
    own = (lines == lax.broadcasted_iota(jnp.int32, lines.shape, 1)).astype(F32).astype(BF)
    spread = dot(own, both)
    column = lax.broadcasted_iota(jnp.int32, (height, LAT), 0) & (LAT - 1)
    here = column == lax.broadcasted_iota(jnp.int32, (height, LAT), 1)
    merged = 32.0 * spread[:, :LAT] + spread[:, LAT:]
    return jnp.sum(jnp.where(here, merged, 0.0), axis=1, keepdims=True).astype(jnp.int32)


def start_kernel(scalars, codes_ref, book_ref, cot_ref, _, hot_ref, quant_ref, usage_ref, fixed_ref, start):
    tokens = hot_ref.shape[0]
    hot32 = (
        code_column(codes_ref[...]) == lax.broadcasted_iota(jnp.int32, (tokens, CODES), 1)
    ).astype(F32)
    hot = hot32.astype(BF)
    hot_ref[...] = hot
    counts = col_sum(hot32)
    usage_ref[...] = pack_rows([counts[:, 128 * i : 128 * i + 128] for i in range(8)])
    high, rest = split_low(book_ref[...])
    middle, low = split_low(rest)
    picked = dot_nt(hot, rows_of([high, middle, low]).astype(BF))
    width = book_ref.shape[0]
    quantized = picked[:, :width] + picked[:, width : 2 * width] + picked[:, 2 * width :]
    quant_ref[...] = quantized
    start[...] = cot_ref[...].astype(F32) - 2.0 * BETA * quantized
    for k in range(4):
        row = (scalars[0] ^ k) * 128
        one = start[pl.ds(pl.multiple_of(row, 64), 64), :]
        two = start[pl.ds(pl.multiple_of(row + 64, 64), 64), :]
        fixed_ref[k] = lanes([one, two]).astype(BF)


def lay_weights(scalars, own_ref, other_ref, o_ref):
    for part in range(PARTS):
        source = (own_ref if part % 2 == 0 else other_ref).at[part // 2]
        _, row = part_row(scalars, part)
        spot = pl.ds(row, 64)
        for k in range(4):
            for m in range(4):
                o_ref[spot, 512 * m + 128 * k : 512 * m + 128 * k + 128] = source[
                    k, :, 128 * m : 128 * m + 128
                ]
        for pair in range(2):
            o_ref[spot, 2048 + 128 * pair : 2176 + 128 * pair] = lanes(
                [source[2 * pair + i, :, 512:576] for i in range(2)]
            )


def conv_one_kernel(
    scalars, a0, a1, a2, a3, w_ref, param_ref, _, hidden_ref, stats_ref, act_ref
):
    pieces = [a0[...], a1[...], a2[...], a3[...]]
    hidden = conv_forward(pieces, w_ref, scalars[0]) + param(param_ref, CONV_BIAS)
    hidden_ref[...] = hidden
    normed, stats = moments(hidden)
    stats_ref[...] = stats
    pre = normed * param(param_ref, GAIN + 1) + param(param_ref, SHIFT + 1)
    act_ref[...] = (pre * jax.nn.sigmoid(pre)).astype(BF)


def conv_two_kernel(
    scalars, a0, a1, a2, a3, w_ref, param_ref, x_ref, fixed_ref, normed_ref, stats_ref, *pay_refs
):
    residual = x_ref[...].astype(F32) + (
        conv_forward([a0[...], a1[...], a2[...], a3[...]], w_ref, scalars[0])
        + param(param_ref, CONV_BIAS + 1)
    )
    normed, stats = moments(residual)
    normed_ref[...] = normed
    stats_ref[...] = stats
    gain, shift = param(param_ref, GAIN + 2), param(param_ref, SHIFT + 2)
    for k, ref in enumerate(pay_refs):
        target = scalars[0] ^ k
        own, other = target * 128, (target ^ 1) * 128
        ref[0:128] = (
            normed_ref[pl.ds(pl.multiple_of(other, 128), 128), :] * gain + shift
        ).astype(BF)
        high, low = split_low(normed_ref[pl.ds(pl.multiple_of(own, 128), 128), :])
        ref[128:256] = high.astype(BF)
        ref[256:384] = low.astype(BF)
        is_two = jnp.broadcast_to(target >> 1, (1, 128)) == 1
        mean = jnp.where(is_two, stats[1:2], stats[0:1])
        deviation = jnp.where(is_two, stats[5:6], stats[4:5])
        rows = list(split_low(mean)) + list(split_low(deviation))
        for index in (GAIN + 2, SHIFT + 2, ATTN_BIAS, ATTN_BIAS + 1, ATTN_BIAS + 2, PROJ_BIAS):
            rows.extend(split_low(param(param_ref, index)))
        ref[384:400] = pack_rows(rows, 16).astype(BF)
        ref[400:464] = fixed_ref[k]


def attn_in_kernel(scalars, n0, n1, n2, n3, norm_ref, residual_ref, bias_ref):
    pieces = [n0, n1, n2, n3]
    tails = [n[384:400].astype(F32) for n in pieces]

    def vector(index, width=128):
        row = 2 * index
        return lanes([t[row : row + 1, :width] + t[row + 1 : row + 2, :width] for t in tails])

    mean, deviation, gain, shift = [vector(index) for index in range(4)]
    empty = jnp.zeros((1, 256), F32)
    bias_ref[...] = pack_rows([vector(4), vector(5), vector(6), lanes([vector(7, 64), empty])])
    own = lanes([n[128:256].astype(F32) + n[256:384].astype(F32) for n in pieces])
    residual_ref[...] = own * deviation + mean
    norm_ref[0:128] = (own * gain + shift).astype(BF)
    norm_ref[128:POS] = lanes([n[0:128] for n in pieces])


def attention_kernel(
    scalars,
    norm_ref,
    residual_ref,
    bias_ref,
    n0,
    n1,
    n2,
    n3,
    own_ref,
    other_ref,
    usage_ref,
    *refs,
):
    pay_refs, keep_refs, send_ref = refs[:4], refs[4:8], refs[8]
    w_ref, grads, lat_grad_ref, sums_ref = refs[9:]
    lay_weights(scalars, own_ref, other_ref, w_ref)
    query_bias, value_bias, out_bias = [bias_ref[m : m + 1] for m in range(3)]
    proj_bias = bias_ref[3:4, 0:256]
    pieces = [n0, n1, n2, n3]
    normed = norm_ref[...]
    query = (dot(norm_ref[0:128], w_ref[:, 0:512]) + query_bias).astype(BF)
    keys = dot(normed, w_ref[:, 512:1024]).astype(BF)
    values = (dot(normed, w_ref[:, 1024:1536]) + value_bias).astype(BF)
    scores = dot_nt(query, keys) * SCORE_SCALE
    weights = jnp.exp(scores - jnp.max(scores, axis=1, keepdims=True))
    probs = weights / jnp.sum(weights, axis=1, keepdims=True)
    probs_low = probs.astype(BF)
    mixed = dot(probs_low, values).astype(BF)
    attended = dot(mixed, w_ref[:, 1536:2048]) + out_bias
    output = (residual_ref[...] + attended).astype(BF)
    latents = dot(output, w_ref[:, 2048:2304]) + proj_bias
    fixed = []
    for n in pieces:
        both = n[400:464].astype(F32)
        fixed.append(rows_of([both[:, :64], both[:, 64:]]))
    lat_grad = (lanes(fixed) + 2.0 * BETA * latents).astype(BF)
    blank = jnp.zeros((128, 64), BF)
    for k in range(4):
        lat_grad_ref[:, 128 * k : 128 * k + 128] = lanes([lat_grad[:, 64 * k : 64 * k + 64], blank])
    out_grad = dot_nt(lat_grad, w_ref[:, 2048:2304])
    att_grad = out_grad.astype(BF)
    mixed_grad = dot_nt(att_grad, w_ref[:, 1536:2048]).astype(BF)
    probs_grad = dot_nt(mixed_grad, values)
    row_dot = jnp.sum(probs * probs_grad, axis=1, keepdims=True)
    score_grad = (probs * (probs_grad - row_dot)).astype(BF)
    query_grad = (dot(score_grad, keys) * SCORE_SCALE).astype(BF)
    key_grad = (dot_tn(score_grad, query) * SCORE_SCALE).astype(BF)
    value_grad = dot_tn(probs_low, mixed_grad).astype(BF)
    upstream = dot_nt(key_grad, w_ref[:, 512:1024]) + dot_nt(value_grad, w_ref[:, 1024:1536])
    upstream_own = upstream[:128] + dot_nt(query_grad, w_ref[:, 0:512])
    for k in range(4):
        ref = pay_refs[k]
        ref[0:128] = upstream_own[:, 128 * k : 128 * k + 128].astype(ref.dtype)
        ref[128:POS] = upstream[128:, 128 * k : 128 * k + 128].astype(ref.dtype)
        ref[POS : POS + 128] = out_grad[:, 128 * k : 128 * k + 128].astype(ref.dtype)
        piece = latents[:, 64 * k : 64 * k + 64]
        ref[POS + 128 : POS + 192] = lanes([piece[:64], piece[64:]]).astype(ref.dtype)
    sums_ref[...] = pack_rows(
        [
            col_sum(query_grad.astype(F32)),
            col_sum(value_grad.astype(F32)),
            col_sum(att_grad.astype(F32)),
            lanes(
                [
                    part
                    for k in range(4)
                    for part in (
                        col_sum(lat_grad[:, 64 * k : 64 * k + 64].astype(F32)),
                        jnp.zeros((1, 64), F32),
                    )
                ]
            ),
        ]
    )
    grads[:, 0:512] = dot_tn(norm_ref[0:128], query_grad).astype(BF)
    grads[:, 512:1024] = dot_tn(normed, key_grad).astype(BF)
    grads[:, 1024:1536] = dot_tn(normed, value_grad).astype(BF)
    grads[:, 1536:2048] = dot_tn(mixed, att_grad).astype(BF)
    grads[:, 2048:2560] = dot_tn(output, lat_grad_ref[...]).astype(BF)
    right = lax.broadcasted_iota(jnp.int32, (16, 128), 1) >= 64

    def halves(vectors, offset):
        blank = jnp.zeros((1, 128), F32)
        entries = [blank] * offset
        for vector in vectors:
            entries += [pltpu.roll(vector, 64, 1), vector]
        return jnp.where(right, pack_rows(entries, 16), 0.0)

    biases = []
    for k in range(4):
        vectors = [sums_ref[m : m + 1, 128 * k : 128 * k + 128] for m in range(4)]
        biases.append(halves(vectors, 4))
    tens = jnp.floor(usage_ref[...] * (1.0 / 16.0))
    ones = usage_ref[...] - 16.0 * tens
    for part in range(PARTS):
        place, row = part_row(scalars, part)
        is_first = (jnp.broadcast_to(place, (16, 128)) == 0).astype(F32)
        here = jnp.broadcast_to(place, (8, 128)) == lax.broadcasted_iota(jnp.int32, (8, 128), 0)
        counts = [col_sum(jnp.where(here, digit, 0.0)) for digit in (tens, ones)]
        for k in range(4):
            ref = keep_refs[part // 2].at[k] if part % 2 == 0 else send_ref.at[part // 2, k]
            for m in range(4):
                ref[:, 128 * m : 128 * m + 128] = grads[
                    pl.ds(row, 64), 512 * m + 128 * k : 512 * m + 128 * k + 128
                ]
            extra = biases[k] * is_first
            if k == 0:
                extra = extra + halves(counts, 0)
            block = slice(2048 + 128 * k, 2176 + 128 * k)
            ref[0:16, 512:640] = (grads[pl.ds(row, 16), block].astype(F32) + extra).astype(BF)
            ref[16:64, 512:640] = grads[pl.ds(row + 16, 48), block]


def third_back_kernel(
    scalars,
    p0,
    p1,
    p2,
    p3,
    normed_ref,
    stats_ref,
    param_ref,
    _,
    w_ref,
    residual_ref,
    taps_ref,
    lat_ref,
    small_ref,
    q0,
    q1,
    q2,
    q3,
    up_ref,
    out_ref,
):
    z = scalars[0]
    for near, far, base in ((p0, p1, z), (p2, p3, z ^ 2)):
        first, second = near[0:POS].astype(F32), far[0:POS].astype(F32)
        up_ref[pl.ds(pl.multiple_of(base * 128, 128), 128), :] = first[:128] + second[128:]
        up_ref[pl.ds(pl.multiple_of((base ^ 1) * 128, 128), 128), :] = first[128:] + second[:128]
    for k, ref in enumerate((p0, p1, p2, p3)):
        row = (z ^ k) * 128
        out_ref[pl.ds(pl.multiple_of(row, 128), 128), :] = ref[POS : POS + 128].astype(F32)
        piece = ref[POS + 128 : POS + 192].astype(F32)
        lat_ref[pl.ds(pl.multiple_of(row, 64), 64), :] = piece[:, :64]
        lat_ref[pl.ds(pl.multiple_of(row + 64, 64), 64), :] = piece[:, 64:]
    source, gain_grad, shift_grad = norm_back(
        up_ref[...], normed_ref[...], stats_ref[...], param(param_ref, GAIN + 2)
    )
    residual = out_ref[...] + source
    residual_ref[...] = residual
    low = residual.astype(BF).astype(F32)
    small_ref[...] = pack_rows([gain_grad, shift_grad, col_sum(low)])
    send_taps(low, w_ref, scalars[0], taps_ref, (q0, q1, q2, q3))


def send_taps(gradient, w_ref, z, taps_ref, piece_refs):
    taps = spread_taps(gradient)
    taps_ref[...] = taps
    rows = []
    for k in range(4):
        block = pl.ds(pl.multiple_of((z ^ k) * 128, 128), 128)
        rows.append(lanes([w_ref[0, tap, block, :] for tap in range(9)]))
    every = dot_nt(taps, rows_of(rows))
    for k, ref in enumerate(piece_refs):
        ref[...] = every[:, 128 * k : 128 * k + 128].astype(ref.dtype)


def swish_back(gradient, normed, gain, shift):
    pre = normed * gain + shift
    gate = jax.nn.sigmoid(pre)
    return gradient * (gate * (1.0 + pre * (1.0 - gate)))


def second_back_kernel(
    scalars,
    p0,
    p1,
    p2,
    p3,
    hidden_ref,
    stats_ref,
    param_ref,
    _,
    __,
    a0,
    a1,
    a2,
    a3,
    w_ref,
    small_ref,
    q0,
    q1,
    q2,
    q3,
    *refs,
):
    keep_refs, send_ref, grads, taps_ref = refs[:4], refs[4], refs[5], refs[6]
    gradient = p0[...] + p1[...].astype(F32) + p2[...].astype(F32) + p3[...].astype(F32)
    stats = stats_ref[...]
    normed = renormed(hidden_ref[...], stats)
    gain = param(param_ref, GAIN + 1)
    upstream = swish_back(gradient, normed, gain, param(param_ref, SHIFT + 1))
    source, gain_grad, shift_grad = norm_back(upstream, normed, stats, gain)
    low = source.astype(BF).astype(F32)
    small_ref[...] = pack_rows([gain_grad, shift_grad, col_sum(low)])
    send_taps(low, w_ref, scalars[0], taps_ref, (q0, q1, q2, q3))
    full = lanes([a0[...], a1[...], a2[...], a3[...]])
    grads[...] = dot_tn(full, taps_ref[...]).astype(BF)
    for part in range(PARTS):
        _, row = part_row(scalars, part)
        value = grads[pl.ds(row, 64), :]
        if part % 2 == 0:
            keep_refs[part // 2][...] = value
        else:
            send_ref[part // 2] = value


def first_back_kernel(
    scalars,
    p0,
    p1,
    p2,
    p3,
    x_ref,
    stats_ref,
    param_ref,
    residual_ref,
    _,
    __,
    ___,
    grad_ref,
    small_ref,
):
    gradient = p0[...] + p1[...].astype(F32) + p2[...].astype(F32) + p3[...].astype(F32)
    stats = stats_ref[...]
    normed = renormed(x_ref[...].astype(F32), stats)
    gain = param(param_ref, GAIN)
    upstream = swish_back(gradient, normed, gain, param(param_ref, SHIFT))
    source, gain_grad, shift_grad = norm_back(upstream, normed, stats, gain)
    grad_ref[...] = residual_ref[...] + source
    small_ref[...] = pack_rows([gain_grad, shift_grad])


def conv_two_grad_kernel(
    scalars, a0, a1, a2, a3, taps_ref, hot_ref, lat_ref, quant_ref, reset_ref, scale, *refs
):
    keep_refs, send_ref, commit_ref, grads, book = refs[:4], refs[4], refs[5], refs[6], refs[7]
    full = lanes([a0[...], a1[...], a2[...], a3[...]])
    grads[...] = dot_tn(full, taps_ref[...]).astype(BF)
    latents = lat_ref[...]
    difference = latents - quant_ref[...]
    commit_ref[...] = pack_rows([lanes([col_sum(difference * difference), jnp.zeros((1, 64), F32)])])
    high, low = split_low(difference * (-scale))
    sums = dot_tn(lanes([high, low]).astype(BF), hot_ref[...])
    tokens = latents.shape[0]
    where = reset_ref[...] - scalars[2] * tokens
    chosen = (where == lax.broadcasted_iota(jnp.int32, (tokens, CODES), 0)).astype(F32).astype(BF)
    picked = dot_tn(latents.astype(BF), chosen)
    book[0:64] = (sums[:64] + sums[64:]).astype(BF)
    book[64:128] = picked.astype(BF)
    for part in range(PARTS):
        place, row = part_row(scalars, part)
        ref = keep_refs[part // 2] if part % 2 == 0 else send_ref.at[part // 2]
        ref[:, 0:WIDE] = grads[pl.ds(row, 64), :]
        column = pl.ds(pl.multiple_of(place * 128, 128), 128)
        ref[:, WIDE : WIDE + 128] = book[0:64, column]
        ref[:, WIDE + 128 : WIDE + 256] = book[64:128, column]


def finish_two_kernel(scalars, own_ref, other_ref, conv_ref, book_grad_ref, picked_ref):
    for part in range(PARTS):
        source = (own_ref if part % 2 == 0 else other_ref).at[part // 2]
        place = scalars[1] ^ part
        rows = pl.ds(pl.multiple_of(place * 64, 64), 64)
        for tap in range(9):
            conv_ref[0, tap, rows, :] = source[:, 128 * tap : 128 * tap + 128].astype(F32)
        column = pl.ds(pl.multiple_of(place * 128, 128), 128)
        book_grad_ref[:, column] = source[:, WIDE : WIDE + 128].astype(F32)
        picked_ref[:, column] = source[:, WIDE + 128 : WIDE + 256].astype(F32)


def finish_last_kernel(
    tokens_all,
    scalars,
    own_ref,
    other_ref,
    picked,
    book_ref,
    held_ref,
    conv_ref,
    gain_ref,
    shift_ref,
    bias_ref,
    commit_ref,
    qkv_ref,
    out_w_ref,
    proj_ref,
    new_book_ref,
    perplexity_ref,
    attn_bias_ref,
    proj_bias_ref,
    usage,
    proj,
):
    extra_sum = jnp.zeros((16, 128), F32)
    total = jnp.zeros((9, 128), F32)
    for part in range(PARTS):
        source = (own_ref if part % 2 == 0 else other_ref).at[part // 2]
        place = scalars[1] ^ part
        rows = pl.ds(pl.multiple_of(place * 64, 64), 64)
        for tap in range(9):
            conv_ref[0, tap, rows, :] = source[:, 128 * tap : 128 * tap + 128].astype(F32)
        for m in range(3):
            qkv_ref[m, rows, :] = source[:, 1152 + 128 * m : 1280 + 128 * m].astype(F32)
        out_w_ref[rows, :] = source[:, 1536:1664].astype(F32)
        proj[rows, :] = source[:, 1664:1792].astype(F32)
        extra = source[0:16, 1664:1792].astype(F32)
        extra_sum = extra_sum + extra
        usage[pl.ds(place, 1), :] = lanes(
            [
                16.0 * extra[0:1, 64:] + extra[2:3, 64:],
                16.0 * extra[1:2, 64:] + extra[3:4, 64:],
            ]
        )
        both = source[16:64, 1728:1792].astype(F32)
        both = both[0:18] + both[18:36]
        total = total + lanes([both[0:9], both[9:18]])
    for index, row in enumerate((0, 2, 5)):
        gain_ref[index : index + 1] = total[row : row + 1]
        shift_ref[index : index + 1] = total[row + 1 : row + 2]
    bias_ref[0:1] = total[4:5]
    bias_ref[1:2] = total[7:8]
    commit_ref[...] = total[8:9, :64] * (1.0 / tokens_all)
    proj_ref[...] = jnp.transpose(proj[...])[0:64]
    counts = usage[...]
    share = counts * (1.0 / tokens_all)
    terms = share * jnp.log(jnp.maximum(share, 1.0 / tokens_all))
    entropy = jnp.sum(jnp.sum(terms, axis=1, keepdims=True), axis=0, keepdims=True)
    perplexity_ref[...] = jnp.exp(-entropy)
    for block in range(8):
        spot = slice(128 * block, 128 * block + 128)
        new_book_ref[:, spot] = jnp.where(
            counts[block : block + 1] > 0.5, book_ref[:, spot], picked[:, spot]
        )
    for m in range(3):
        attn_bias_ref[m : m + 1] = lanes(
            [extra_sum[4 + 2 * m : 5 + 2 * m, 64:], extra_sum[5 + 2 * m : 6 + 2 * m, 64:]]
        )
    proj_bias_ref[...] = extra_sum[10:11, 64:]


def pair_add_kernel(scalars, k0, k1, k2, k3, get_ref, _, keep_ref, send_ref):
    for i, ref in enumerate((k0, k1, k2, k3)):
        target = (send_ref if i % 2 else keep_ref).at[i // 2]
        target[...] = plus(ref[...], get_ref[i])


def plus(first, second):
    return (first.astype(F32) + second.astype(F32)).astype(BF)


def half_add_kernel(scalars, keep_ref, get_ref, _, own_ref, send_ref):
    own_ref[...] = plus(keep_ref[0], get_ref[0])
    send_ref[...] = plus(keep_ref[1], get_ref[1])


def attn_sum_kernel(scalars, a0, a1, _, keep_ref, send_ref):
    for k in range(4):
        (send_ref if k % 2 else keep_ref)[k // 2] = plus(a0[k], a1[k])


def half_pass_kernel(scalars, keep_ref, get_ref, _, a0, a1, a2, own_ref, send_ref, b0, b1, b2):
    half_add_kernel(scalars, keep_ref, get_ref, _, own_ref, send_ref)
    for source, target in ((a0, b0), (a1, b1), (a2, b2)):
        target[...] = source[...]


def add_kernel(scalars, k0, k1, k2, k3, get_ref, _, *sum_refs):
    for i, ref in enumerate((k0, k1, k2, k3)):
        sum_refs[i][...] = plus(ref[...], get_ref[i])


def two_sum_kernel(scalars, a0, a1, _, sum_ref):
    sum_ref[...] = plus(a0[...], a1[...])


def last_kernel(
    scalars, o0, o1, o2, o3, att_own, att_get, small_one, small_two, small_three, commit, last_ref
):
    total = o0[...].astype(F32)
    for ref in (o1, o2, o3):
        total = total + ref[...].astype(F32)
    last_ref[:, 0:WIDE] = total.astype(BF)
    last_ref[:, 1152:1664] = plus(att_own[:, 0:512], att_get[:, 0:512])
    rows = [small_one[0:1], small_one[1:2]]
    rows += [small_two[m : m + 1] for m in range(3)]
    rows += [small_three[m : m + 1] for m in range(3)]
    rows += [commit[0:1]]
    high, low = split_low(pack_rows(rows, 16))
    blank = jnp.zeros((48, 64), F32)
    small = rows_of([high[:9, :64], high[:9, 64:], low[:9, :64], low[:9, 64:], jnp.zeros((12, 64), F32)])
    small = lanes([blank, small])
    block = att_own[:, 512:640].astype(F32) + att_get[:, 512:640].astype(F32)
    last_ref[0:16, 1664:1792] = block[0:16].astype(BF)
    last_ref[16:64, 1664:1792] = (block[16:64] + small).astype(BF)


def stack_kernel(scalars, *refs):
    out_ref = refs[-1]
    for k in range(out_ref.shape[0]):
        out_ref[k] = refs[k][...]


def over(axis, array, flip):
    size = lax.axis_size(axis)
    return lax.ppermute(array, axis, [(i, i ^ flip) for i in range(size)])


def flips(array):
    return [over("chan", array, k) for k in (1, 2, 3)]


def plane(array):
    return [array] + [over("dp", array, k) for k in (2, 4, 6)]


def add(*arrays):
    total = arrays[0].astype(F32)
    for array in arrays[1:]:
        total = total + array.astype(F32)
    return total.astype(BF)


def shards(
    latents_in,
    norm_gains,
    norm_shifts,
    conv_weights,
    conv_biases,
    qkv_weights,
    attn_biases,
    out_weight,
    proj_weight,
    proj_bias,
    codebook,
    codes,
    reset_src,
    cotangent,
):
    images = latents_in.shape[0]
    tokens = images * POS
    quarter = tokens // 4
    devices = lax.axis_size("dp")
    tokens_all = tokens * devices
    by_hand = devices == PARTS
    z = lax.axis_index("chan").astype(jnp.int32)
    dp = lax.axis_index("dp").astype(jnp.int32)
    scalars = jnp.stack([z, dp if by_hand else jnp.zeros_like(dp), dp, jnp.zeros_like(dp)])
    x = latents_in.reshape(tokens, 128)
    conv_w = conv_weights.reshape(2, 9, C, 128)

    def whole(shape):
        return pl.BlockSpec(shape, lambda i, n=len(shape): (0,) * n)

    def blocks_call(body, in_specs, out_specs, outs, name, *args, scratch=(), aliases={}):
        return pl.pallas_call(
            body,
            grid=(1,),
            out_shape=outs,
            in_specs=[pl.BlockSpec(memory_space=pltpu.SMEM)] + in_specs,
            out_specs=out_specs,
            scratch_shapes=scratch,
            input_output_aliases=aliases,
            compiler_params=pltpu.CompilerParams(vmem_limit_bytes=VMEM * 2**20),
            cost_estimate=pl.CostEstimate(flops=HEAVY, bytes_accessed=1, transcendentals=0),
            name=name,
        )(scalars, *args)

    anywhere = pl.BlockSpec(memory_space=pl.ANY)

    def begin(*refs):
        begin_kernel(by_hand, *refs)

    act_one, stats_one, pack, params = pl.pallas_call(
        begin,
        out_shape=[
            sds((tokens, 128), BF),
            sds((8, 128), F32),
            sds((64, 640), BF),
            sds((16, 128), F32),
        ],
        in_specs=[anywhere] * 9,
        out_specs=[pl.BlockSpec(memory_space=pltpu.VMEM)] * 4,
        scratch_shapes=[
            pltpu.VMEM((tokens, 128), BF),
            pltpu.VMEM((3, 128), F32),
            pltpu.VMEM((3, 128), F32),
            pltpu.VMEM((2, 128), F32),
            pltpu.VMEM((3, 128), F32),
            pltpu.VMEM((1, 64), F32),
            pltpu.VMEM((4, 64, 128), BF),
            pltpu.VMEM((64, 128), BF),
            pltpu.VMEM((128, 64), F32),
            pltpu.SemaphoreType.DMA((11,)),
        ],
        compiler_params=pltpu.CompilerParams(vmem_limit_bytes=60 * 2**20),
        cost_estimate=pl.CostEstimate(flops=HEAVY, bytes_accessed=1, transcendentals=0),
        name="begin",
    )(
        x,
        norm_gains,
        norm_shifts,
        conv_biases,
        attn_biases,
        proj_bias.reshape(1, 64),
        qkv_weights,
        out_weight,
        proj_weight.T,
    )
    pieces_one = [act_one] + flips(act_one)
    packs = [pack] + flips(pack)
    hot, quantized, usage, fixed = call(
        start_kernel,
        [
            sds((tokens, CODES), BF),
            sds((tokens, 64), F32),
            sds((8, 128), F32),
            sds((4, 64, 128), BF),
        ],
        scalars,
        codes,
        codebook.T,
        cotangent.reshape(tokens, 64),
        stats_one,
        scratch=[pltpu.VMEM((tokens, 64), F32)],
        name="start",
    )
    def conv_call(body, index, outs, name, *args):
        specs = []
        for a in args:
            if a is conv_w:
                specs.append(pl.BlockSpec((1, 9, C, 128), lambda i: (index, 0, 0, 0)))
            else:
                specs.append(whole(a.shape))
        scratch = ()
        if body is third_back_kernel:
            scratch = [pltpu.VMEM((tokens, 128), F32), pltpu.VMEM((tokens, 128), F32)]
        if body is second_back_kernel:
            scratch = [pltpu.VMEM((C, WIDE), BF), pltpu.VMEM((tokens, WIDE), BF)]
        return blocks_call(
            body, specs, [whole(o.shape) for o in outs], outs, name, *args, scratch=scratch
        )

    hidden, stats_two, act_two = conv_call(
        conv_one_kernel,
        0,
        [sds((tokens, 128), F32), sds((8, 128), F32), sds((tokens, 128), BF)],
        "conv_one",
        *pieces_one,
        conv_w,
        params,
        usage,
    )
    pieces_two = [act_two] + flips(act_two)
    if by_hand:
        block = call(
            stack_kernel,
            [sds((4, 64, 640), BF)],
            scalars,
            *packs,
            flops=HEAVY,
            name="pack_join",
        )[0]
        blocks = [block] + [over("dp", block, k) for k in (2, 4, 6)]
    else:
        packed = jnp.concatenate(
            [qkv_weights[0], qkv_weights[1], qkv_weights[2], out_weight, proj_weight]
            + [jnp.zeros((C, 64), BF)],
            axis=1,
        )
        block = jnp.stack([packed] + flips(packed)).reshape(4, PARTS, 64, 640)
        block = jnp.swapaxes(block, 0, 1)
        block_own, block_other = block[0::2], block[1::2]
    normed_three, stats_three, *pays = conv_call(
        conv_two_kernel,
        1,
        [sds((tokens, 128), F32), sds((8, 128), F32)] + [sds((464, 128), BF)] * 4,
        "conv_two",
        *pieces_two,
        conv_w,
        params,
        x,
        fixed,
    )
    normed_pieces = [pays[0]] + [over("chan", pays[k], k) for k in (1, 2, 3)]
    if by_hand:
        block_own = call(
            stack_kernel,
            [sds((4, 4, 64, 640), BF)],
            scalars,
            *blocks,
            name="pack_plane",
        )[0]
        block_other = over("dp", block_own, 1)
    normed, residual_part, bias_rows = call(
        attn_in_kernel,
        [sds((POS, C), BF), sds((quarter, C), F32), sds((8, C), F32)],
        scalars,
        *normed_pieces,
        flops=HEAVY,
        name="attn_in",
    )
    *pays, k0, k1, k2, k3, att_send = call(
        attention_kernel,
        [sds((POS + 192, 128), F32)]
        + [sds((POS + 192, 128), BF)] * 3
        + [sds((4, 64, 640), BF)] * 4
        + [sds((4, 4, 64, 640), BF)],
        scalars,
        normed,
        residual_part,
        bias_rows,
        *normed_pieces,
        block_own,
        block_other,
        usage,
        scratch=[
            pltpu.VMEM((C, 2304), BF),
            pltpu.VMEM((C, 2560), BF),
            pltpu.VMEM((quarter, C), BF),
            pltpu.VMEM((8, C), F32),
        ],
        flops=HEAVY,
        name="attention",
    )
    att_keep = [k0, k1, k2, k3]

    back_three = [pays[0]] + [over("chan", pays[k], k) for k in (1, 2, 3)]
    def pair_sum(keep, send, after, name):
        outs = [sds((2,) + keep[0].shape, BF)] * 2
        got = over("dp", send, 1)
        kept, sent = call(pair_add_kernel, outs, scalars, *keep, got, after, name=name)
        return kept, over("dp", sent, 2)

    if by_hand:
        att_kept, att_got = pair_sum(att_keep, att_send, back_three[1], "attn_pair")
    residual_grad, taps_two, latents, small_three, *pays = conv_call(
        third_back_kernel,
        1,
        [
            sds((tokens, 128), F32),
            sds((tokens, WIDE), BF),
            sds((tokens, 64), F32),
            sds((8, 128), F32),
            sds((tokens, 128), F32),
        ]
        + [sds((tokens, 128), BF)] * 3,
        "third_back",
        *back_three,
        normed_three,
        stats_three,
        params,
        att_kept if by_hand else bias_rows,
        conv_w,
    )
    back_two = [pays[0]] + [over("chan", pays[k], k) for k in (1, 2, 3)]
    book_scale = 2.0 * CODES / tokens_all

    def two_grad(*refs):
        conv_two_grad_kernel(*refs[:10], book_scale, *refs[10:])

    *two_keep, two_send, commit = call(
        two_grad,
        [sds((64, 1408), BF)] * 4 + [sds((4, 64, 1408), BF), sds((8, 128), F32)],
        scalars,
        *pieces_two,
        taps_two,
        hot,
        latents,
        quantized,
        reset_src.reshape(1, CODES),
        scratch=[pltpu.VMEM((C, WIDE), BF), pltpu.VMEM((128, CODES), BF)],
        name="conv_two_grad",
    )
    if by_hand:
        att_own, att_sent = call(
            half_add_kernel,
            [sds((4, 64, 640), BF)] * 2,
            scalars,
            att_kept,
            att_got,
            small_three,
            flops=HEAVY,
            name="attn_half",
        )
        att_got = over("dp", att_sent, 4)
        two_kept, two_got = pair_sum(two_keep, two_send, att_own, "conv_two_pair")
    small_two, *pays = conv_call(
        second_back_kernel,
        0,
        [sds((8, 128), F32), sds((tokens, 128), F32)]
        + [sds((tokens, 128), BF)] * 3
        + [sds((64, WIDE), BF)] * 4
        + [sds((4, 64, WIDE), BF)],
        "second_back",
        *back_two,
        hidden,
        stats_two,
        params,
        att_own if by_hand else bias_rows,
        two_kept if by_hand else bias_rows,
        *pieces_one,
        conv_w,
    )
    *one_keep, one_send = pays[4:]
    pays = pays[:4]
    one_got = over("dp", one_send, 1) if by_hand else one_send
    if by_hand:
        att_kept, att_sent = call(
            attn_sum_kernel,
            [sds((2, 64, 640), BF)] * 2,
            scalars,
            att_own,
            att_got,
            small_two,
            name="attn_sum",
        )
        att_got = over("chan", att_sent, 1)
        two_own, two_sent, *pays[1:] = call(
            half_pass_kernel,
            [sds((64, 1408), BF)] * 2 + [sds((tokens, 128), BF)] * 3,
            scalars,
            two_kept,
            two_got,
            small_two,
            *pays[1:],
            flops=HEAVY,
            name="conv_two_half",
        )
        two_got = over("dp", two_sent, 4)
        one_parts = call(
            add_kernel,
            [sds((64, WIDE), BF)] * 4,
            scalars,
            *one_keep,
            one_got,
            att_kept,
            name="conv_one_add",
        )
        one_parts = [one_parts[0]] + [over("dp", one_parts[i], 2 * i) for i in (1, 2, 3)]
        att_own, att_sent = call(
            half_add_kernel,
            [sds((64, 640), BF)] * 2,
            scalars,
            att_kept,
            att_got,
            two_own,
            name="attn_last",
        )
        att_got = over("chan", att_sent, 2)
        two = call(
            two_sum_kernel,
            [sds((64, 1408), BF)],
            scalars,
            two_own,
            two_got,
            one_parts[0],
            name="conv_two_sum",
        )[0]
    back_one = [pays[0]] + [over("chan", pays[k], k) for k in (1, 2, 3)]
    grad_latents, small_one = call(
        first_back_kernel,
        [sds((tokens, 128), F32), sds((8, 128), F32)],
        scalars,
        *back_one,
        x,
        stats_one,
        params,
        residual_grad,
        one_parts[0] if by_hand else bias_rows,
        two if by_hand else bias_rows,
        att_own if by_hand else bias_rows,
        flops=HEAVY,
        name="first_back",
    )

    if by_hand:
        last = call(
            last_kernel,
            [sds((64, 1792), BF)],
            scalars,
            *one_parts,
            att_own,
            att_got,
            small_one,
            small_two,
            small_three,
            commit,
            flops=HEAVY,
            name="last",
        )[0]

        def chip(array, name, *after, flops=0):
            parts = plane(array)
            outs = [sds((4,) + array.shape, BF)]
            return call(stack_kernel, outs, scalars, *parts, *after, flops=flops, name=name)[0]

        two_own = chip(two, "stack_two", last, flops=HEAVY)
        two_other = over("dp", two_own, 1)
        last_own = chip(last, "stack_last", flops=HEAVY)
        last_other = over("dp", last_own, 1)
    else:

        def total(keep, send):
            parts = jnp.stack([jnp.stack(keep), send]).astype(F32)
            return lax.psum(parts, "dp").astype(BF)

        att_sum = total(att_keep, att_send)
        att_sum = add(att_sum[:, :, 0], *[over("chan", att_sum[:, :, k], k) for k in (1, 2, 3)])
        small = jnp.concatenate([small_one[0:2], small_two[0:3], small_three[0:3], commit[0:1]])
        small = jnp.concatenate([lax.psum(small, "dp"), jnp.zeros((7, 128), F32)])
        high = lax.reduce_precision(small, 8, 7)
        halves = [v[:9, c : c + 64] for v in (high, small - high) for c in (0, 64)]
        smalls = jnp.concatenate(halves + [jnp.zeros((12, 64), F32)]).astype(BF)
        att_sum = att_sum.at[0, 0, 16:64, 576:640].add(smalls)
        two_own, two_other = total(two_keep, two_send)
        one_sum = total(one_keep, one_send)
        last_own, last_other = jnp.concatenate([one_sum, att_sum], axis=3)

    conv_held, book_grad, picked = blocks_call(
        finish_two_kernel,
        [whole((4, 64, 1408)), whole((4, 64, 1408))],
        [
            pl.BlockSpec((1, 9, C, 128), lambda i: (1, 0, 0, 0)),
            whole((64, CODES)),
            whole((64, CODES)),
        ],
        [sds((2, 9, C, 128), F32), sds((64, CODES), F32), sds((64, CODES), F32)],
        "finish_two",
        two_own,
        two_other,
    )

    def finish_last(*refs):
        finish_last_kernel(float(tokens_all), *refs)

    outs = [
        sds((2, 9, C, 128), F32),
        sds((3, 128), F32),
        sds((3, 128), F32),
        sds((2, 128), F32),
        sds((1, 64), F32),
        sds((3, C, 128), F32),
        sds((C, 128), F32),
        sds((64, C), F32),
        sds((64, CODES), F32),
        sds((1, 1), F32),
        sds((3, 128), F32),
        sds((1, 64), F32),
    ]
    (
        conv_grad,
        gain_grad,
        shift_grad,
        conv_bias_grad,
        commitment,
        qkv_grad,
        out_grad,
        proj_grad,
        new_codebook,
        perplexity,
        attn_bias_grad,
        proj_bias_grad,
    ) = blocks_call(
        finish_last,
        [whole((4, 64, 1792)), whole((4, 64, 1792)), whole((64, CODES)), whole((64, CODES))]
        + [pl.BlockSpec(memory_space=pl.ANY)],
        [pl.BlockSpec((1, 9, C, 128), lambda i: (0, 0, 0, 0))] + [whole(o.shape) for o in outs[1:]],
        outs,
        "finish_last",
        last_own,
        last_other,
        picked,
        codebook.T,
        conv_held,
        scratch=[pltpu.VMEM((8, 128), F32), pltpu.VMEM((C, 128), F32)],
        aliases={5: 0},
    )

    return (
        latents.reshape(images, LAT, LAT, -1),
        commitment.reshape(64),
        perplexity.reshape(()),
        new_codebook.T,
        grad_latents.reshape(images, LAT, LAT, 128),
        gain_grad,
        shift_grad,
        conv_grad.reshape(2, 3, 3, C, 128),
        conv_bias_grad,
        qkv_grad,
        attn_bias_grad,
        out_grad,
        proj_grad.T,
        proj_bias_grad.reshape(64),
        book_grad.T,
    )


def solution(mesh):
    return jax.shard_map(
        shards,
        mesh=mesh,
        in_specs=(
            P("dp", None, None, "chan"),
            P(None, "chan"),
            P(None, "chan"),
            P(None, None, None, None, "chan"),
            P(None, "chan"),
            P(None, None, "chan"),
            P(None, "chan"),
            P(None, "chan"),
            P(None, "chan"),
            P("chan"),
            P(None, "chan"),
            P("dp", None, None),
            P(),
            P("dp", None, None, "chan"),
        ),
        out_specs=(
            P("dp", None, None, "chan"),
            P("chan"),
            P(),
            P(None, "chan"),
            P("dp", None, None, "chan"),
            P(None, "chan"),
            P(None, "chan"),
            P(None, None, None, None, "chan"),
            P(None, "chan"),
            P(None, None, "chan"),
            P(None, "chan"),
            P(None, "chan"),
            P(None, "chan"),
            P("chan"),
            P(None, "chan"),
        ),
        check_vma=False,
    )
```
